32 devices in a mesh: pipe: 4 (over y, x), seq: 8 (over z, core).
Axes of the slice: x: 2, y: 2, z: 4, core: 2. Of those that a mesh axis runs over, the one named last changes fastest.
Arguments:
- latents: bfloat16 [2, 64, 1536], P(None, 'seq', 'pipe'), may hold values from -6 to 6
- timesteps: int32 [2, 2], replicated, may hold values from 0 to 15
- step_sizes: float32 [16], replicated, may hold values from 0.2 to 0.8
- mod_table: float32 [4, 16, 4608], P('pipe'), may hold values from -4 to 4
- qk_gain: float32 [4, 2, 128], P('pipe'), may hold values from 0.5 to 2
- w_query: bfloat16 [4, 1536, 1536], P('pipe'), may hold values from -0.15625 to 0.15625
- w_kv: bfloat16 [4, 1536, 3072], P('pipe', 'seq'), may hold values from -0.15625 to 0.15625
- w_out: bfloat16 [4, 1536, 1536], P('pipe'), may hold values from -0.15625 to 0.15625
Outputs:
- final_latents: bfloat16 [2, 64, 1536], P(None, 'seq', 'pipe')
The draws below stay inside these ranges and needn't reach their ends.
All inputs are finite; a program needn't handle non-finite values.
Results may differ from the reference program's by a relative error of at most 0.025.
Values may be sent and summed in bfloat16 or wider, within the bound.
A program may use at most 64 MiB of HBM per device.

```python
import math
import jax
import jax.numpy as jnp
from jax import lax

D = 1536
HEADS = 12
HEAD_DIM = 128
MICRO = 2
STEPS = 2
NT = 16
INNER = 1536
SEQ_LEN = 64
SECTIONS = 4
N_PIPE = 4


def set_ends(values, own_key, least, top_value):
    index_at = [jax.random.randint(jax.random.fold_in(own_key, axis), (), 0, length) for axis, length in enumerate(values.shape)]
    longest = values.shape.index(max(values.shape))
    beside = index_at[:longest] + [(index_at[longest] + 1) % values.shape[longest]] + index_at[longest + 1:]
    return values.at[tuple(index_at)].set(least).at[tuple(beside)].set(top_value)


def steps_of(key, shape, split, least, high):
    factor_of = 1.0
    for axis_at, blocks in split:
        draws = jax.random.uniform(jax.random.fold_in(jax.random.fold_in(key, 6), axis_at), (blocks,), jnp.float32, least / len(split), high / len(split))
        factor_of = factor_of * jnp.repeat(jnp.exp(draws), shape[axis_at] // blocks).reshape((-1,) + (1,) * (len(shape) - 1 - axis_at))
    return factor_of


def centred(rng, dims, scale, bound, shards=(), kind=jnp.bfloat16):
    drawn = jax.random.normal(rng, dims, jnp.float32) * scale
    if len(shards) > 0:
        drawn = steps_of(rng, dims, shards, -0.22, 0.18) * drawn
    return jnp.clip(drawn, min=-bound, max=bound).astype(kind)


def setup_inputs(seed: int = 0) -> dict:
    arg_keys = jax.random.split(jax.random.key(seed), 9)
    return {
        "latents": centred(arg_keys[0], (MICRO, SEQ_LEN, D), 1.0, 6.0, ((1, 8), (2, 4))),
        "timesteps": set_ends(jax.random.randint(arg_keys[1], (STEPS, MICRO), 0, NT), jax.random.fold_in(arg_keys[1], 1), 0, NT - 1).astype(jnp.int32),
        "step_sizes": jnp.clip(jnp.exp(jax.random.uniform(arg_keys[2], (NT,), jnp.float32, math.log(0.2), math.log(0.8))), 0.2, 0.8),
        "mod_table": centred(arg_keys[3], (SECTIONS, NT, 3 * D), 0.5, 4.0, ((0, 4),), jnp.float32),
        "qk_gain": jnp.clip(0.5 + 1.5 * jax.random.uniform(arg_keys[4], (SECTIONS, 2, HEAD_DIM), jnp.float32) ** steps_of(arg_keys[4], (SECTIONS, 2, HEAD_DIM), ((0, 4),), -0.2, 0.2), 0.5, 2.0),
        "w_query": centred(arg_keys[5], (SECTIONS, D, INNER), D ** -0.5, 0.15625, ((0, 4),)),
        "w_kv": centred(arg_keys[6], (SECTIONS, D, 2 * INNER), D ** -0.5, 0.15625, ((0, 4), (1, 8))),
        "w_out": centred(arg_keys[7], (SECTIONS, INNER, D), INNER ** -0.5, 0.15625, ((0, 4),)),
    }


norm_eps = 1e-06

def rms_heads(values, gain_row):
    mean_square = lax.optimization_barrier(jnp.mean(values * values, axis=-1, keepdims=True))
    return values * lax.rsqrt(mean_square + norm_eps) * gain_row

def apply_layer(hidden, mod_row, gain_pair, query_weight, kv_weight, out_weight):
    as_float = hidden.astype(jnp.float32)
    shift_row = mod_row[:D]
    scale_row = mod_row[D:2 * D]
    gate_row = mod_row[2 * D:]
    center = lax.optimization_barrier(jnp.mean(as_float, axis=-1, keepdims=True))
    spread = lax.optimization_barrier(jnp.mean(jnp.square(as_float - center), axis=-1, keepdims=True))
    modded = ((as_float - center) * lax.rsqrt(spread + norm_eps) * (1.0 + scale_row) + shift_row).astype(jnp.bfloat16)
    query_proj = jnp.dot(modded, query_weight, preferred_element_type=jnp.float32).reshape(-1, HEADS, HEAD_DIM)
    kv_proj = jnp.dot(modded, kv_weight, preferred_element_type=jnp.float32).reshape(-1, 2, HEADS, HEAD_DIM)
    queries = rms_heads(query_proj, gain_pair[0]).astype(jnp.bfloat16)
    key_rows = rms_heads(kv_proj[:, 0], gain_pair[1]).astype(jnp.bfloat16)
    value_rows = kv_proj[:, 1].astype(jnp.bfloat16)
    logits = jnp.einsum('qhd,khd->hqk', queries.astype(jnp.float32), key_rows.astype(jnp.float32)) * (1.0 / math.sqrt(HEAD_DIM))
    weights_soft = jnp.exp(logits)
    running_sum = lax.optimization_barrier(jnp.sum(weights_soft, axis=-1))
    rounded = lax.optimization_barrier(weights_soft.astype(jnp.bfloat16))
    attended = jnp.einsum('hqk,khd->hqd', rounded.astype(jnp.float32), value_rows.astype(jnp.float32)) / running_sum[..., None]
    attended = jnp.transpose(attended.astype(jnp.bfloat16), (1, 0, 2)).reshape(-1, HEADS * HEAD_DIM)
    projected_out = jnp.dot(attended, out_weight, preferred_element_type=jnp.float32)
    return (as_float + gate_row * projected_out).astype(jnp.bfloat16)

def reference(latents, timesteps, step_sizes, mod_table, qk_gain, w_query, w_kv, w_out):
    slots = [latents[slot_now] for slot_now in range(MICRO)]
    for step_now in range(STEPS):
        renewed = []
        for slot_now in range(MICRO):
            time_index = timesteps[step_now, slot_now]
            hidden = slots[slot_now]
            for segment_now in range(N_PIPE):
                hidden = apply_layer(hidden, mod_table[segment_now, time_index], qk_gain[segment_now], w_query[segment_now], w_kv[segment_now], w_out[segment_now])
            update = slots[slot_now].astype(jnp.float32) - step_sizes[time_index] * hidden.astype(jnp.float32)
            renewed.append(update.astype(jnp.bfloat16))
        slots = renewed
    return jnp.stack(slots)
```

```python
import functools
import math

import jax
import jax.numpy as jnp
from jax import lax
from jax.experimental import pallas as pl
from jax.experimental.pallas import tpu as pltpu
from jax.sharding import PartitionSpec as P

norm_eps = 1e-06
MESH = pl.DeviceIdType.MESH


def rms_rows(values, gain_row):
    mean_square = jnp.mean(values * values, axis=-1, keepdims=True)
    return (values * lax.rsqrt(mean_square + norm_eps) * gain_row).astype(jnp.bfloat16)


def kernel(
    n_pipe, n_seq, groups, micro, steps, head_dim,
    lat_ref, ts_ref, ss_ref, mod_ref, gain_ref, wq_hbm, wkv_hbm, wo_hbm,
    out_ref,
    wq, wk, wv, wo, latbuf, hid, att, outb, prev, modded, fin_src, fin,
    local_sem, kv_recv, kv_send, kv_fwd, lat_send, lat_recv,
    hid_recv, hid_send, hid_fwd, att_recv, att_send, fin_send, fin_recv,
):
    sharers = n_seq // groups
    rows, share = lat_ref.shape[1], lat_ref.shape[2]
    tokens = rows * n_seq
    width = share * n_pipe
    block = wq.shape[1]
    inner = block * groups
    depth = wkv_hbm.shape[1]
    part = tokens // sharers
    per_block = n_pipe // groups
    per_part = n_seq // sharers
    heads = block // head_dim
    score_scale = 1.0 / math.sqrt(head_dim)
    last = n_pipe - 1

    pipe, seq = lax.axis_index("pipe"), lax.axis_index("seq")
    mine, sharer = seq // sharers, seq % sharers

    def remote(src, dst, send, recv, to_pipe, to_seq):
        return pltpu.make_async_remote_copy(
            src_ref=src, dst_ref=dst, send_sem=send, recv_sem=recv,
            device_id=(to_pipe, to_seq), device_id_type=MESH,
        )

    def lat_copy(to_pipe, to_seq, index):
        return remote(lat_ref, latbuf.at[pipe, seq], lat_send.at[index],
                      lat_recv.at[pipe, seq], to_pipe, to_seq)

    def lat_local():
        return pltpu.make_async_copy(lat_ref, latbuf.at[pipe, seq], lat_recv.at[pipe, seq])

    def lat_arrived(from_pipe, from_seq):
        pltpu.make_async_copy(lat_ref, latbuf.at[from_pipe, from_seq],
                              lat_recv.at[from_pipe, from_seq]).wait()

    keeper = (pipe // per_block) * sharers + seq // per_part
    for ahead in range(n_seq):
        target = lax.rem(seq + ahead, n_seq)
        if ahead == 0:
            @pl.when(pipe == 0)
            def _():
                lat_local().start()

            @pl.when(pipe != 0)
            def _():
                lat_copy(0, target, ahead).start()
        else:
            lat_copy(0, target, ahead).start()
    keeps_own = (pipe == last) & (keeper == seq)

    @pl.when(keeps_own)
    def _():
        lat_local().start()

    @pl.when(jnp.logical_not(keeps_own))
    def _():
        lat_copy(last, keeper, n_seq).start()

    wkv = (wk, wv)

    def columns(kv, group):
        start = pl.multiple_of(kv * inner + group * block, 128)
        return wkv_hbm.at[0, :, pl.ds(start, block)]

    def slab(kv, owner):
        return wkv[kv].at[pl.ds(pl.multiple_of(owner * depth, 16), depth), :]

    def kv_copy(kv, ahead):
        group = lax.rem(mine + ahead, groups)
        return remote(columns(kv, group), slab(kv, seq), kv_send.at[kv, ahead],
                      kv_recv.at[kv, seq], pipe, group * sharers + sharer)

    def kv_pass(kv, ahead, step):
        group = lax.rem(mine + ahead, groups)
        owner = group * sharers + sharer
        source = columns(kv, mine) if ahead == 0 else slab(kv, owner)
        return remote(source, slab(kv, owner), kv_fwd.at[kv, ahead, step],
                      kv_recv.at[kv, owner], pipe, mine * sharers + lax.rem(sharer + step, sharers))

    def kv_arrived(kv, owner):
        pltpu.make_async_copy(columns(kv, mine), slab(kv, owner), kv_recv.at[kv, owner]).wait()

    own_columns = pl.ds(pl.multiple_of(mine * block, 128), block)
    copy_q = pltpu.make_async_copy(wq_hbm.at[0, :, own_columns], wq, local_sem.at[0])
    copy_o = pltpu.make_async_copy(wo_hbm.at[0, :, own_columns], wo, local_sem.at[1])
    for kv in range(2):
        for ahead in range(groups - 1, 0, -1):
            kv_copy(kv, ahead).start()
    for kv in range(2):
        pltpu.make_async_copy(columns(kv, mine), slab(kv, seq), kv_recv.at[kv, seq]).start()
        for step in range(1, sharers):
            kv_pass(kv, 0, step).start()
    copy_q.start()
    copy_o.start()
    for kv in range(2):
        for ahead in range(1, groups):
            kv_arrived(kv, lax.rem(mine + ahead, groups) * sharers + sharer)
            for step in range(1, sharers):
                kv_pass(kv, ahead, step).start()
    for kv in range(2):
        kv_arrived(kv, seq)
        for step in range(1, sharers):
            for group in range(groups):
                kv_arrived(kv, group * sharers + lax.rem(sharer + step, sharers))
    copy_q.wait()
    copy_o.wait()

    @pl.when(pipe == 0)
    def _():
        for from_pipe in range(n_pipe):
            for from_seq in range(n_seq):
                lat_arrived(from_pipe, from_seq)

    @pl.when(pipe == last)
    def _():
        for slot in range(micro):
            pieces = []
            for wide in range(per_block):
                pieces.append(jnp.concatenate([
                    latbuf_wait_load(latbuf, lat_arrived, slot == 0, mine * per_block + wide,
                                     sharer * per_part + index, slot)
                    for index in range(per_part)
                ], axis=0))
            prev[slot] = jnp.concatenate(pieces, axis=1) if per_block > 1 else pieces[0]

    def hid_send_copy(step, slot, group):
        at_last = pipe == last
        to_step = step + jnp.where(at_last, 1, 0)
        return remote(outb.at[step, slot], hid.at[to_step, slot, mine, sharer],
                      hid_send.at[step, slot, group], hid_recv.at[to_step, slot, mine, sharer],
                      lax.rem(pipe + 1, n_pipe), group * sharers + sharer)

    def hid_pass(step, slot, group, ahead):
        return remote(hid.at[step, slot, group, sharer], hid.at[step, slot, group, sharer],
                      hid_fwd.at[step, slot, group, ahead], hid_recv.at[step, slot, group, sharer],
                      pipe, mine * sharers + lax.rem(sharer + ahead, sharers))

    def hid_arrived(step, slot, group, from_sharer):
        pltpu.make_async_copy(outb.at[step, slot], hid.at[step, slot, group, from_sharer],
                              hid_recv.at[step, slot, group, from_sharer]).wait()

    def att_copy(step, slot, ahead):
        group = lax.rem(mine + ahead, groups)
        return remote(att.at[step, slot, mine], att.at[step, slot, mine],
                      att_send.at[step, slot, ahead], att_recv.at[step, slot, mine],
                      pipe, group * sharers + sharer)

    def att_arrived(step, slot, ahead):
        group = lax.rem(mine + ahead, groups)
        pltpu.make_async_copy(att.at[step, slot, mine], att.at[step, slot, group],
                              att_recv.at[step, slot, group]).wait()

    def fin_targets(slot):
        for wide in range(per_block):
            for index in range(per_part):
                to_pipe, to_seq = mine * per_block + wide, sharer * per_part + index
                source = fin_src.at[slot, wide, pl.ds(index * rows, rows), :]
                yield to_pipe, to_seq, source, fin_send.at[slot, wide, index]

    def visit(item, carry):
        step, slot = item // micro, item % micro
        tau = ts_ref[step, slot]
        from_latents = (pipe == 0) & (step == 0)

        @pl.when(from_latents)
        def _():
            for group in range(groups):
                pieces = []
                for wide in range(per_block):
                    pieces.append(jnp.concatenate([
                        latbuf[group * per_block + wide, index, slot].astype(jnp.float32)
                        for index in range(n_seq)
                    ], axis=0))
                whole = jnp.concatenate(pieces, axis=1) if per_block > 1 else pieces[0]
                for at in range(sharers):
                    hid[0, slot, group, at] = whole[at * part:(at + 1) * part].astype(jnp.bfloat16)

        @pl.when(jnp.logical_not(from_latents))
        def _():
            for group in range(groups):
                hid_arrived(step, slot, group, sharer)
                for ahead in range(1, sharers):
                    hid_pass(step, slot, group, ahead).start()
            for group in range(groups):
                for ahead in range(1, sharers):
                    hid_arrived(step, slot, group, lax.rem(sharer + ahead, sharers))

        as_float = jnp.concatenate([
            jnp.concatenate([hid[step, slot, group, at].astype(jnp.float32) for at in range(sharers)], axis=0)
            for group in range(groups)
        ], axis=1)
        center = jnp.mean(as_float, axis=-1, keepdims=True)
        away = as_float - center
        spread = jnp.mean(away * away, axis=-1, keepdims=True)
        shift_row = mod_ref[0, pl.ds(tau, 1), 0:width]
        scale_row = mod_ref[0, pl.ds(tau, 1), width:2 * width]
        modded[...] = (
            away * lax.rsqrt(spread + norm_eps) * (1.0 + scale_row) + shift_row
        ).astype(jnp.bfloat16)
        queries = jnp.dot(modded[pl.ds(pl.multiple_of(sharer * part, 16), part), :], wq[...],
                          preferred_element_type=jnp.float32)
        keys = jnp.dot(modded[...], wk[...], preferred_element_type=jnp.float32)
        values = jnp.dot(modded[...], wv[...], preferred_element_type=jnp.float32).astype(jnp.bfloat16)
        gain_query, gain_key = gain_ref[0, 0:1, :], gain_ref[0, 1:2, :]
        for head in range(heads):
            here = slice(head * head_dim, (head + 1) * head_dim)
            logits = lax.dot_general(
                rms_rows(queries[:, here], gain_query), rms_rows(keys[:, here], gain_key),
                (((1,), (1,)), ((), ())), preferred_element_type=jnp.float32,
            ) * score_scale
            weights = jnp.exp(logits)
            total = jnp.sum(weights, axis=-1, keepdims=True)
            weighted = jnp.dot(weights.astype(jnp.bfloat16), values[:, here],
                               preferred_element_type=jnp.float32)
            att[step, slot, mine, :, here] = (weighted / total).astype(jnp.bfloat16)
        for ahead in range(1, groups):
            att_copy(step, slot, ahead).start()
        gate_row = mod_ref[0, pl.ds(tau, 1), pl.ds(pl.multiple_of(2 * width + mine * block, 128), block)]
        residual = hid[step, slot, mine, sharer].astype(jnp.float32)
        for ahead in range(1, groups):
            att_arrived(step, slot, ahead)
        attended = jnp.concatenate([att[step, slot, group] for group in range(groups)], axis=1)
        projected = jnp.dot(attended, wo[...], preferred_element_type=jnp.float32)
        layer_out = (residual + gate_row * projected).astype(jnp.bfloat16)
        ends = (pipe == last) & (step == steps - 1)

        @pl.when(pipe != last)
        def _():
            outb[step, slot] = layer_out

        @pl.when(pipe == last)
        def _():
            update = (prev[slot] - ss_ref[tau] * layer_out.astype(jnp.float32)).astype(jnp.bfloat16)
            outb[step, slot] = update
            prev[slot] = update.astype(jnp.float32)

        @pl.when(jnp.logical_not(ends))
        def _():
            for ahead in range(groups):
                hid_send_copy(step, slot, lax.rem(mine + ahead, groups)).start()

        @pl.when(ends)
        def _():
            update = prev[slot]
            for wide in range(per_block):
                fin_src[slot, wide] = update[:, wide * share:(wide + 1) * share]
            for to_pipe, to_seq, source, send in fin_targets(slot):
                own = (to_pipe == pipe) & (to_seq == seq)

                @pl.when(own)
                def _():
                    pltpu.make_async_copy(source, fin.at[slot], fin_recv.at[slot]).start()

                @pl.when(jnp.logical_not(own))
                def _():
                    remote(source, fin.at[slot], send, fin_recv.at[slot], to_pipe, to_seq).start()
        return carry

    lax.fori_loop(0, micro * steps, visit, 0)

    for slot in range(micro):
        pltpu.make_async_copy(fin_src.at[slot, 0, pl.ds(0, rows), :], fin.at[slot],
                              fin_recv.at[slot]).wait()
        out_ref[slot] = fin[slot].astype(jnp.bfloat16)

    for ahead in range(n_seq):
        target = lax.rem(seq + ahead, n_seq)
        if ahead == 0:
            @pl.when(pipe != 0)
            def _():
                lat_copy(0, target, ahead).wait_send()
        else:
            lat_copy(0, target, ahead).wait_send()

    @pl.when(jnp.logical_not(keeps_own))
    def _():
        lat_copy(last, keeper, n_seq).wait_send()

    for kv in range(2):
        for ahead in range(1, groups):
            kv_copy(kv, ahead).wait_send()
        for ahead in range(groups):
            for step in range(1, sharers):
                kv_pass(kv, ahead, step).wait_send()

    def drain(item, carry):
        step, slot = item // micro, item % micro
        ends = (pipe == last) & (step == steps - 1)
        for ahead in range(1, groups):
            att_copy(step, slot, ahead).wait_send()

        @pl.when(jnp.logical_not((pipe == 0) & (step == 0)))
        def _():
            for group in range(groups):
                for ahead in range(1, sharers):
                    hid_pass(step, slot, group, ahead).wait_send()

        @pl.when(jnp.logical_not(ends))
        def _():
            for group in range(groups):
                hid_send_copy(step, slot, group).wait_send()

        @pl.when(ends)
        def _():
            for to_pipe, to_seq, source, send in fin_targets(slot):
                @pl.when(jnp.logical_not((to_pipe == pipe) & (to_seq == seq)))
                def _():
                    remote(source, fin.at[slot], send, fin_recv.at[slot], to_pipe, to_seq).wait_send()
        return carry

    lax.fori_loop(0, micro * steps, drain, 0)


def latbuf_wait_load(latbuf, lat_arrived, first, from_pipe, from_seq, slot):
    if first:
        lat_arrived(from_pipe, from_seq)
    return latbuf[from_pipe, from_seq, slot].astype(jnp.float32)


def shards(latents, timesteps, step_sizes, mod_table, qk_gain, w_query, w_kv, w_out):
    n_pipe, n_seq = lax.axis_size("pipe"), lax.axis_size("seq")
    micro, rows, share = latents.shape
    steps = timesteps.shape[0]
    head_dim = qk_gain.shape[2]
    width, inner = w_query.shape[1], w_query.shape[2]
    heads = inner // head_dim
    groups = math.gcd(math.gcd(heads, n_seq), n_pipe)
    while n_seq // groups < 2:
        groups //= 2
    sharers = n_seq // groups
    block = inner // groups
    part = rows * n_seq // sharers
    per_block, per_part = n_pipe // groups, n_seq // sharers
    bf16, f32 = jnp.bfloat16, jnp.float32
    vmem = pl.BlockSpec(memory_space=pltpu.VMEM)
    smem = pl.BlockSpec(memory_space=pltpu.SMEM)
    hbm = pl.BlockSpec(memory_space=pl.ANY)
    dma = pltpu.SemaphoreType.DMA
    return pl.pallas_call(
        functools.partial(kernel, n_pipe, n_seq, groups, micro, steps, head_dim),
        out_shape=jax.ShapeDtypeStruct(latents.shape, bf16),
        in_specs=[vmem, smem, smem, vmem, vmem, hbm, hbm, hbm],
        out_specs=vmem,
        scratch_shapes=[
            pltpu.VMEM((width, block), bf16),
            pltpu.VMEM((width, block), bf16),
            pltpu.VMEM((width, block), bf16),
            pltpu.VMEM((inner, block), bf16),
            pltpu.VMEM((n_pipe, n_seq, micro, rows, share), bf16),
            pltpu.VMEM((steps, micro, groups, sharers, part, block), bf16),
            pltpu.VMEM((steps, micro, groups, part, block), bf16),
            pltpu.VMEM((steps, micro, part, block), bf16),
            pltpu.VMEM((micro, part, block), f32),
            pltpu.VMEM((rows * n_seq, width), bf16),
            pltpu.VMEM((micro, per_block, part, share), f32),
            pltpu.VMEM((micro, rows, share), f32),
            dma((2,)),
            dma((2, n_seq)),
            dma((2, groups)),
            dma((2, groups, sharers)),
            dma((n_seq + 1,)),
            dma((n_pipe, n_seq)),
            dma((steps, micro, groups, sharers)),
            dma((steps, micro, groups)),
            dma((steps, micro, groups, sharers)),
            dma((steps, micro, groups)),
            dma((steps, micro, groups)),
            dma((micro, per_block, per_part)),
            dma((micro,)),
        ],
        compiler_params=pltpu.CompilerParams(
            has_side_effects=True, vmem_limit_bytes=48 * 1024 * 1024
        ),
        cost_estimate=pl.CostEstimate(
            flops=2 * 4 * rows * n_seq * width * block * micro * steps,
            bytes_accessed=2 * 4 * width * block, transcendentals=0,
        ),
        name="denoise",
    )(latents, timesteps, step_sizes, mod_table, qk_gain, w_query, w_kv, w_out)


def solution(mesh):
    in_specs = (
        P(None, "seq", "pipe"),
        P(),
        P(),
        P("pipe", None, None),
        P("pipe", None, None),
        P("pipe", None, None),
        P("pipe", "seq", None),
        P("pipe", None, None),
    )
    out_specs = P(None, "seq", "pipe")
    return jax.shard_map(shards, mesh=mesh, in_specs=in_specs, out_specs=out_specs, check_vma=False)
```

```python
import functools
import math

import jax
import jax.numpy as jnp
from jax import lax
from jax.experimental import pallas as pl
from jax.experimental.pallas import tpu as pltpu
from jax.sharding import PartitionSpec as P

norm_eps = 1e-06
MESH = pl.DeviceIdType.MESH


def rms_rows(values, gain_row):
    mean_square = jnp.mean(values * values, axis=-1, keepdims=True)
    return (values * lax.rsqrt(mean_square + norm_eps) * gain_row).astype(jnp.bfloat16)


def kernel(
    n_pipe, n_seq, groups, micro, steps, head_dim,
    lat_ref, ts_hbm, ss_hbm, mod_hbm, gain_hbm, wq_hbm, wkv_hbm, wo_hbm,
    out_ref,
    ts_ref, ss_ref, mod_ref, gain_ref, wq, wk, wv, wo, latbuf, hid, att, outb, prev, modded, fin_src, fin,
    local_sem, kv_recv, kv_send, kv_fwd, lat_send, lat_recv,
    hid_recv, hid_send, hid_fwd, att_recv, att_send, fin_send, fin_recv,
):
    sharers = n_seq // groups
    rows, share = lat_ref.shape[1], lat_ref.shape[2]
    tokens = rows * n_seq
    width = share * n_pipe
    block = wq.shape[1]
    inner = block * groups
    depth = wkv_hbm.shape[1]
    part = tokens // sharers
    per_block = n_pipe // groups
    per_part = n_seq // sharers
    heads = block // head_dim
    score_scale = 1.0 / math.sqrt(head_dim)
    last = n_pipe - 1

    pipe, seq = lax.axis_index("pipe"), lax.axis_index("seq")
    mine, sharer = seq // sharers, seq % sharers

    def remote(src, dst, send, recv, to_pipe, to_seq):
        return pltpu.make_async_remote_copy(
            src_ref=src, dst_ref=dst, send_sem=send, recv_sem=recv,
            device_id=(to_pipe, to_seq), device_id_type=MESH,
        )

    def lat_copy(to_pipe, to_seq, index):
        return remote(lat_ref, latbuf.at[pipe, seq], lat_send.at[index],
                      lat_recv.at[pipe, seq], to_pipe, to_seq)

    def lat_local():
        return pltpu.make_async_copy(lat_ref, latbuf.at[pipe, seq], lat_recv.at[pipe, seq])

    def lat_arrived(from_pipe, from_seq):
        pltpu.make_async_copy(lat_ref, latbuf.at[from_pipe, from_seq],
                              lat_recv.at[from_pipe, from_seq]).wait()

    keeper = (pipe // per_block) * sharers + seq // per_part
    for ahead in range(n_seq):
        target = lax.rem(seq + ahead, n_seq)
        if ahead == 0:
            @pl.when(pipe == 0)
            def _():
                lat_local().start()

            @pl.when(pipe != 0)
            def _():
                lat_copy(0, target, ahead).start()
        else:
            lat_copy(0, target, ahead).start()
    keeps_own = (pipe == last) & (keeper == seq)

    @pl.when(keeps_own)
    def _():
        lat_local().start()

    @pl.when(jnp.logical_not(keeps_own))
    def _():
        lat_copy(last, keeper, n_seq).start()

    wkv = (wk, wv)

    def columns(kv, group):
        start = pl.multiple_of(kv * inner + group * block, 128)
        return wkv_hbm.at[0, :, pl.ds(start, block)]

    def slab(kv, owner):
        return wkv[kv].at[pl.ds(pl.multiple_of(owner * depth, 16), depth), :]

    def kv_copy(kv, ahead):
        group = lax.rem(mine + ahead, groups)
        return remote(columns(kv, group), slab(kv, seq), kv_send.at[kv, ahead],
                      kv_recv.at[kv, seq], pipe, group * sharers + sharer)

    def kv_pass(kv, ahead, step):
        group = lax.rem(mine + ahead, groups)
        owner = group * sharers + sharer
        source = columns(kv, mine) if ahead == 0 else slab(kv, owner)
        return remote(source, slab(kv, owner), kv_fwd.at[kv, ahead, step],
                      kv_recv.at[kv, owner], pipe, mine * sharers + lax.rem(sharer + step, sharers))

    def kv_arrived(kv, owner):
        pltpu.make_async_copy(columns(kv, mine), slab(kv, owner), kv_recv.at[kv, owner]).wait()

    own_columns = pl.ds(pl.multiple_of(mine * block, 128), block)
    copy_q = pltpu.make_async_copy(wq_hbm.at[0, :, own_columns], wq, local_sem.at[0])
    copy_o = pltpu.make_async_copy(wo_hbm.at[0, :, own_columns], wo, local_sem.at[1])
    for kv in range(2):
        for ahead in range(groups - 1, 0, -1):
            kv_copy(kv, ahead).start()
    for kv in range(2):
        pltpu.make_async_copy(columns(kv, mine), slab(kv, seq), kv_recv.at[kv, seq]).start()
        for step in range(1, sharers):
            kv_pass(kv, 0, step).start()
    locals_in = [
        copy_q, copy_o,
        pltpu.make_async_copy(ts_hbm, ts_ref, local_sem.at[2]),
        pltpu.make_async_copy(ss_hbm, ss_ref, local_sem.at[3]),
        pltpu.make_async_copy(mod_hbm, mod_ref, local_sem.at[4]),
        pltpu.make_async_copy(gain_hbm, gain_ref, local_sem.at[5]),
    ]
    for copy in locals_in:
        copy.start()
    for kv in range(2):
        for ahead in range(1, groups):
            kv_arrived(kv, lax.rem(mine + ahead, groups) * sharers + sharer)
            for step in range(1, sharers):
                kv_pass(kv, ahead, step).start()
    for kv in range(2):
        kv_arrived(kv, seq)
        for step in range(1, sharers):
            for group in range(groups):
                kv_arrived(kv, group * sharers + lax.rem(sharer + step, sharers))
    for copy in locals_in:
        copy.wait()

    @pl.when(pipe == 0)
    def _():
        for from_pipe in range(n_pipe):
            for from_seq in range(n_seq):
                lat_arrived(from_pipe, from_seq)

    @pl.when(pipe == last)
    def _():
        for slot in range(micro):
            pieces = []
            for wide in range(per_block):
                pieces.append(jnp.concatenate([
                    latbuf_wait_load(latbuf, lat_arrived, slot == 0, mine * per_block + wide,
                                     sharer * per_part + index, slot)
                    for index in range(per_part)
                ], axis=0))
            prev[slot] = jnp.concatenate(pieces, axis=1) if per_block > 1 else pieces[0]

    def hid_send_copy(step, slot, group):
        at_last = pipe == last
        to_step = step + jnp.where(at_last, 1, 0)
        return remote(outb.at[step, slot], hid.at[to_step, slot, mine, sharer],
                      hid_send.at[step, slot, group], hid_recv.at[to_step, slot, mine, sharer],
                      lax.rem(pipe + 1, n_pipe), group * sharers + sharer)

    def hid_pass(step, slot, group, ahead):
        return remote(hid.at[step, slot, group, sharer], hid.at[step, slot, group, sharer],
                      hid_fwd.at[step, slot, group, ahead], hid_recv.at[step, slot, group, sharer],
                      pipe, mine * sharers + lax.rem(sharer + ahead, sharers))

    def hid_arrived(step, slot, group, from_sharer):
        pltpu.make_async_copy(outb.at[step, slot], hid.at[step, slot, group, from_sharer],
                              hid_recv.at[step, slot, group, from_sharer]).wait()

    def att_copy(step, slot, head, ahead):
        group = lax.rem(mine + ahead, groups)
        return remote(att.at[step, slot, mine, head], att.at[step, slot, mine, head],
                      att_send.at[step, slot, head, ahead], att_recv.at[step, slot, mine, head],
                      pipe, group * sharers + sharer)

    def att_arrived(step, slot, head, ahead):
        group = lax.rem(mine + ahead, groups)
        pltpu.make_async_copy(att.at[step, slot, mine, head], att.at[step, slot, group, head],
                              att_recv.at[step, slot, group, head]).wait()

    def fin_targets(slot):
        for wide in range(per_block):
            for index in range(per_part):
                to_pipe, to_seq = mine * per_block + wide, sharer * per_part + index
                source = fin_src.at[slot, wide, pl.ds(index * rows, rows), :]
                yield to_pipe, to_seq, source, fin_send.at[slot, wide, index]

    def first_half(step, slot):
        tau = ts_ref[step, slot]
        from_latents = (pipe == 0) & (step == 0)

        @pl.when(from_latents)
        def _():
            for group in range(groups):
                pieces = []
                for wide in range(per_block):
                    pieces.append(jnp.concatenate([
                        latbuf[group * per_block + wide, index, slot].astype(jnp.float32)
                        for index in range(n_seq)
                    ], axis=0))
                whole = jnp.concatenate(pieces, axis=1) if per_block > 1 else pieces[0]
                for at in range(sharers):
                    hid[0, slot, group, at] = whole[at * part:(at + 1) * part].astype(jnp.bfloat16)

        @pl.when(jnp.logical_not(from_latents))
        def _():
            for group in range(groups):
                hid_arrived(step, slot, group, sharer)
                for ahead in range(1, sharers):
                    hid_pass(step, slot, group, ahead).start()
            for group in range(groups):
                for ahead in range(1, sharers):
                    hid_arrived(step, slot, group, lax.rem(sharer + ahead, sharers))

        as_float = jnp.concatenate([
            jnp.concatenate([hid[step, slot, group, at].astype(jnp.float32) for at in range(sharers)], axis=0)
            for group in range(groups)
        ], axis=1)
        center = jnp.mean(as_float, axis=-1, keepdims=True)
        away = as_float - center
        spread = jnp.mean(away * away, axis=-1, keepdims=True)
        shift_row = mod_ref[0, pl.ds(tau, 1), 0:width]
        scale_row = mod_ref[0, pl.ds(tau, 1), width:2 * width]
        modded[...] = (
            away * lax.rsqrt(spread + norm_eps) * (1.0 + scale_row) + shift_row
        ).astype(jnp.bfloat16)
        queries = jnp.dot(modded[pl.ds(pl.multiple_of(sharer * part, 16), part), :], wq[...],
                          preferred_element_type=jnp.float32)
        keys = jnp.dot(modded[...], wk[...], preferred_element_type=jnp.float32)
        values = jnp.dot(modded[...], wv[...], preferred_element_type=jnp.float32).astype(jnp.bfloat16)
        gain_query, gain_key = gain_ref[0, 0:1, :], gain_ref[0, 1:2, :]
        for head in range(heads):
            here = slice(head * head_dim, (head + 1) * head_dim)
            logits = lax.dot_general(
                rms_rows(queries[:, here], gain_query), rms_rows(keys[:, here], gain_key),
                (((1,), (1,)), ((), ())), preferred_element_type=jnp.float32,
            ) * score_scale
            weights = jnp.exp(logits)
            total = jnp.sum(weights, axis=-1, keepdims=True)
            weighted = jnp.dot(weights.astype(jnp.bfloat16), values[:, here],
                               preferred_element_type=jnp.float32)
            att[step, slot, mine, head] = (weighted / total).astype(jnp.bfloat16)
            for ahead in range(1, groups):
                att_copy(step, slot, head, ahead).start()

    def second_half(step, slot):
        tau = ts_ref[step, slot]
        gate_row = mod_ref[0, pl.ds(tau, 1), pl.ds(pl.multiple_of(2 * width + mine * block, 128), block)]
        residual = hid[step, slot, mine, sharer].astype(jnp.float32)
        projected = 0.0
        for ahead in range(groups):
            group = lax.rem(mine + ahead, groups)
            if ahead > 0:
                for head in range(heads):
                    att_arrived(step, slot, head, ahead)
            attended = jnp.concatenate([att[step, slot, group, head] for head in range(heads)], axis=1)
            rows_here = pl.ds(pl.multiple_of(group * block, 128), block)
            projected += jnp.dot(attended, wo[rows_here, :], preferred_element_type=jnp.float32)
        layer_out = (residual + gate_row * projected).astype(jnp.bfloat16)
        ends = (pipe == last) & (step == steps - 1)

        @pl.when(pipe != last)
        def _():
            outb[step, slot] = layer_out

        @pl.when(pipe == last)
        def _():
            update = (prev[slot] - ss_ref[tau] * layer_out.astype(jnp.float32)).astype(jnp.bfloat16)
            outb[step, slot] = update
            prev[slot] = update.astype(jnp.float32)

        @pl.when(jnp.logical_not(ends))
        def _():
            for ahead in range(groups):
                hid_send_copy(step, slot, lax.rem(mine + ahead, groups)).start()

        @pl.when(ends)
        def _():
            update = prev[slot]
            for wide in range(per_block):
                fin_src[slot, wide] = update[:, wide * share:(wide + 1) * share]
            for to_pipe, to_seq, source, send in fin_targets(slot):
                own = (to_pipe == pipe) & (to_seq == seq)

                @pl.when(own)
                def _():
                    pltpu.make_async_copy(source, fin.at[slot], fin_recv.at[slot]).start()

                @pl.when(jnp.logical_not(own))
                def _():
                    remote(source, fin.at[slot], send, fin_recv.at[slot], to_pipe, to_seq).start()

    def visit(step, carry):
        for slot in range(micro):
            first_half(step, slot)
        for slot in range(micro):
            second_half(step, slot)
        return carry

    lax.fori_loop(0, steps, visit, 0)

    for slot in range(micro):
        pltpu.make_async_copy(fin_src.at[slot, 0, pl.ds(0, rows), :], fin.at[slot],
                              fin_recv.at[slot]).wait()
        out_ref[slot] = fin[slot].astype(jnp.bfloat16)

    for ahead in range(n_seq):
        target = lax.rem(seq + ahead, n_seq)
        if ahead == 0:
            @pl.when(pipe != 0)
            def _():
                lat_copy(0, target, ahead).wait_send()
        else:
            lat_copy(0, target, ahead).wait_send()

    @pl.when(jnp.logical_not(keeps_own))
    def _():
        lat_copy(last, keeper, n_seq).wait_send()

    for kv in range(2):
        for ahead in range(1, groups):
            kv_copy(kv, ahead).wait_send()
        for ahead in range(groups):
            for step in range(1, sharers):
                kv_pass(kv, ahead, step).wait_send()

    def drain(item, carry):
        step, slot = item // micro, item % micro
        ends = (pipe == last) & (step == steps - 1)
        for head in range(heads):
            for ahead in range(1, groups):
                att_copy(step, slot, head, ahead).wait_send()

        @pl.when(jnp.logical_not((pipe == 0) & (step == 0)))
        def _():
            for group in range(groups):
                for ahead in range(1, sharers):
                    hid_pass(step, slot, group, ahead).wait_send()

        @pl.when(jnp.logical_not(ends))
        def _():
            for group in range(groups):
                hid_send_copy(step, slot, group).wait_send()

        @pl.when(ends)
        def _():
            for to_pipe, to_seq, source, send in fin_targets(slot):
                @pl.when(jnp.logical_not((to_pipe == pipe) & (to_seq == seq)))
                def _():
                    remote(source, fin.at[slot], send, fin_recv.at[slot], to_pipe, to_seq).wait_send()
        return carry

    lax.fori_loop(0, micro * steps, drain, 0)


def latbuf_wait_load(latbuf, lat_arrived, first, from_pipe, from_seq, slot):
    if first:
        lat_arrived(from_pipe, from_seq)
    return latbuf[from_pipe, from_seq, slot].astype(jnp.float32)


def shards(latents, timesteps, step_sizes, mod_table, qk_gain, w_query, w_kv, w_out):
    n_pipe, n_seq = lax.axis_size("pipe"), lax.axis_size("seq")
    micro, rows, share = latents.shape
    steps = timesteps.shape[0]
    head_dim = qk_gain.shape[2]
    width, inner = w_query.shape[1], w_query.shape[2]
    heads = inner // head_dim
    groups = math.gcd(math.gcd(heads, n_seq), n_pipe)
    while n_seq // groups < 2:
        groups //= 2
    sharers = n_seq // groups
    block = inner // groups
    part = rows * n_seq // sharers
    per_block, per_part = n_pipe // groups, n_seq // sharers
    bf16, f32 = jnp.bfloat16, jnp.float32
    vmem = pl.BlockSpec(memory_space=pltpu.VMEM)
    hbm = pl.BlockSpec(memory_space=pl.ANY)
    dma = pltpu.SemaphoreType.DMA
    return pl.pallas_call(
        functools.partial(kernel, n_pipe, n_seq, groups, micro, steps, head_dim),
        out_shape=jax.ShapeDtypeStruct(latents.shape, bf16),
        in_specs=[hbm] * 8,
        out_specs=vmem,
        scratch_shapes=[
            pltpu.SMEM(timesteps.shape, timesteps.dtype),
            pltpu.SMEM(step_sizes.shape, f32),
            pltpu.VMEM(mod_table.shape, f32),
            pltpu.VMEM(qk_gain.shape, f32),
            pltpu.VMEM((width, block), bf16),
            pltpu.VMEM((width, block), bf16),
            pltpu.VMEM((width, block), bf16),
            pltpu.VMEM((inner, block), bf16),
            pltpu.VMEM((n_pipe, n_seq, micro, rows, share), bf16),
            pltpu.VMEM((steps, micro, groups, sharers, part, block), bf16),
            pltpu.VMEM((steps, micro, groups, block // head_dim, part, head_dim), bf16),
            pltpu.VMEM((steps, micro, part, block), bf16),
            pltpu.VMEM((micro, part, block), f32),
            pltpu.VMEM((rows * n_seq, width), bf16),
            pltpu.VMEM((micro, per_block, part, share), f32),
            pltpu.VMEM((micro, rows, share), f32),
            dma((6,)),
            dma((2, n_seq)),
            dma((2, groups)),
            dma((2, groups, sharers)),
            dma((n_seq + 1,)),
            dma((n_pipe, n_seq)),
            dma((steps, micro, groups, sharers)),
            dma((steps, micro, groups)),
            dma((steps, micro, groups, sharers)),
            dma((steps, micro, groups, block // head_dim)),
            dma((steps, micro, block // head_dim, groups)),
            dma((micro, per_block, per_part)),
            dma((micro,)),
        ],
        compiler_params=pltpu.CompilerParams(
            has_side_effects=True, vmem_limit_bytes=64 * 1024 * 1024
        ),
        cost_estimate=pl.CostEstimate(
            flops=2 * 4 * rows * n_seq * width * block * micro * steps,
            bytes_accessed=2 * 4 * width * block, transcendentals=0,
        ),
        name="denoise",
    )(latents, timesteps, step_sizes, mod_table, qk_gain, w_query, w_kv, w_out)


def solution(mesh):
    in_specs = (
        P(None, "seq", "pipe"),
        P(),
        P(),
        P("pipe", None, None),
        P("pipe", None, None),
        P("pipe", None, None),
        P("pipe", "seq", None),
        P("pipe", None, None),
    )
    out_specs = P(None, "seq", "pipe")
    return jax.shard_map(shards, mesh=mesh, in_specs=in_specs, out_specs=out_specs, check_vma=False)
```

```python
import functools
import math

import jax
import jax.numpy as jnp
from jax import lax
from jax.experimental import pallas as pl
from jax.experimental.pallas import tpu as pltpu
from jax.sharding import PartitionSpec as P

norm_eps = 1e-06
MESH = pl.DeviceIdType.MESH


def rms_rows(values, gain_row):
    mean_square = jnp.mean(values * values, axis=-1, keepdims=True)
    return (values * lax.rsqrt(mean_square + norm_eps) * gain_row).astype(jnp.bfloat16)


def kernel(
    n_pipe, n_seq, groups, micro, steps, head_dim,
    lat_ref, ts_hbm, ss_hbm, mod_hbm, gain_hbm, wq_hbm, wkv_hbm, wo_hbm,
    out_ref,
    ts_ref, ss_ref, mod_ref, gain_ref, wq, wk, wv, wo, wrows, latbuf, hid, att, outb, prev, modded,
    first_x, first_mod, slabs, pbuf, pin, csum, cin, pre, kvx, fin_src, fin,
    local_sem, kv_recv, kv_send, kv_fwd, lat_send, lat_recv, pin_send, pin_recv, cin_send, cin_recv,
    hid_recv, hid_send, kvx_send, kvx_recv, att_recv, att_send, fin_send, fin_recv,
):
    sharers = n_seq // groups
    rows, share = lat_ref.shape[1], lat_ref.shape[2]
    tokens = rows * n_seq
    width = share * n_pipe
    block = wq.shape[1]
    inner = block * groups
    depth = wkv_hbm.shape[1]
    part = tokens // sharers
    per_block = n_pipe // groups
    per_part = n_seq // sharers
    heads = block // head_dim
    score_scale = 1.0 / math.sqrt(head_dim)
    last = n_pipe - 1

    pipe, seq = lax.axis_index("pipe"), lax.axis_index("seq")
    mine, sharer = seq // sharers, seq % sharers

    def remote(src, dst, send, recv, to_pipe, to_seq):
        return pltpu.make_async_remote_copy(
            src_ref=src, dst_ref=dst, send_sem=send, recv_sem=recv,
            device_id=(to_pipe, to_seq), device_id_type=MESH,
        )

    def lat_copy(to_pipe, to_seq, index):
        return remote(lat_ref, latbuf.at[pipe, seq], lat_send.at[index],
                      lat_recv.at[pipe, seq], to_pipe, to_seq)

    def lat_local():
        return pltpu.make_async_copy(lat_ref, latbuf.at[pipe, seq], lat_recv.at[pipe, seq])

    def lat_arrived(from_pipe, from_seq):
        pltpu.make_async_copy(lat_ref, latbuf.at[from_pipe, from_seq],
                              lat_recv.at[from_pipe, from_seq]).wait()

    keeper = (pipe // per_block) * sharers + seq // per_part
    for ahead in range(n_seq):
        target = lax.rem(seq + ahead, n_seq)
        if ahead == 0:
            @pl.when(pipe == 0)
            def _():
                lat_local().start()

            @pl.when(pipe != 0)
            def _():
                lat_copy(0, target, ahead).start()
        else:
            lat_copy(0, target, ahead).start()
    keeps_own = (pipe == last) & (keeper == seq)

    @pl.when(keeps_own)
    def _():
        lat_local().start()

    @pl.when(jnp.logical_not(keeps_own))
    def _():
        lat_copy(last, keeper, n_seq).start()

    wkv = (wk, wv)

    def columns(kv, group):
        start = pl.multiple_of(kv * inner + group * block, 128)
        return wkv_hbm.at[0, :, pl.ds(start, block)]

    def slab(kv, owner):
        return wkv[kv].at[pl.ds(pl.multiple_of(owner * depth, 16), depth), :]

    def kv_copy(kv, ahead):
        group = lax.rem(mine + ahead, groups)
        return remote(columns(kv, group), slab(kv, seq), kv_send.at[kv, ahead],
                      kv_recv.at[kv, seq], pipe, group * sharers + sharer)

    def kv_pass(kv, ahead, step):
        group = lax.rem(mine + ahead, groups)
        owner = group * sharers + sharer
        source = columns(kv, mine) if ahead == 0 else slab(kv, owner)
        return remote(source, slab(kv, owner), kv_fwd.at[kv, ahead, step],
                      kv_recv.at[kv, owner], pipe, mine * sharers + lax.rem(sharer + step, sharers))

    def kv_arrived(kv, owner):
        pltpu.make_async_copy(columns(kv, mine), slab(kv, owner), kv_recv.at[kv, owner]).wait()

    own_columns = pl.ds(pl.multiple_of(mine * block, 128), block)
    copy_q = pltpu.make_async_copy(wq_hbm.at[0, :, own_columns], wq, local_sem.at[0])
    copy_o = pltpu.make_async_copy(wo_hbm.at[0, :, own_columns], wo, local_sem.at[1])
    def weights_start():
        for kv in range(2):
            for ahead in range(groups - 1, 0, -1):
                kv_copy(kv, ahead).start()
        for kv in range(2):
            pltpu.make_async_copy(columns(kv, mine), slab(kv, seq), kv_recv.at[kv, seq]).start()
            for step in range(1, sharers):
                kv_pass(kv, 0, step).start()

    def weights_finish():
        for kv in range(2):
            for ahead in range(1, groups):
                kv_arrived(kv, lax.rem(mine + ahead, groups) * sharers + sharer)
                for step in range(1, sharers):
                    kv_pass(kv, ahead, step).start()
        for kv in range(2):
            kv_arrived(kv, seq)
            for step in range(1, sharers):
                for group in range(groups):
                    kv_arrived(kv, group * sharers + lax.rem(sharer + step, sharers))

    pl.when(pipe != 0)(weights_start)
    locals_in = [
        copy_q, copy_o,
        pltpu.make_async_copy(ts_hbm, ts_ref, local_sem.at[2]),
        pltpu.make_async_copy(ss_hbm, ss_ref, local_sem.at[3]),
        pltpu.make_async_copy(mod_hbm, mod_ref, local_sem.at[4]),
        pltpu.make_async_copy(gain_hbm, gain_ref, local_sem.at[5]),
        pltpu.make_async_copy(wkv_hbm.at[0], wrows, local_sem.at[6]),
    ]
    for copy in locals_in:
        copy.start()
    for copy in locals_in:
        copy.wait()

    def modulate(as_float, tau):
        center = jnp.mean(as_float, axis=-1, keepdims=True)
        away = as_float - center
        spread = jnp.mean(away * away, axis=-1, keepdims=True)
        shift_row = mod_ref[0, pl.ds(tau, 1), 0:width]
        scale_row = mod_ref[0, pl.ds(tau, 1), width:2 * width]
        return (
            away * lax.rsqrt(spread + norm_eps) * (1.0 + scale_row) + shift_row
        ).astype(jnp.bfloat16)

    def pin_copy(slot, ahead):
        other = lax.rem(sharer + ahead, sharers)
        return remote(pbuf.at[slot, other], pin.at[slot, sharer], pin_send.at[slot, ahead],
                      pin_recv.at[slot, sharer], pipe, mine * sharers + other)

    def cin_copy(slot, ahead):
        group = lax.rem(mine + ahead, groups)
        return remote(csum.at[slot, group], cin.at[slot, mine], cin_send.at[slot, ahead],
                      cin_recv.at[slot, mine], pipe, group * sharers + sharer)

    @pl.when(pipe == 0)
    def _():
        for from_pipe in range(n_pipe):
            for from_seq in range(n_seq):
                lat_arrived(from_pipe, from_seq)
        for slot in range(micro):
            pieces = []
            for from_pipe in range(n_pipe):
                pieces.append(jnp.concatenate([
                    latbuf[from_pipe, index, slot].astype(jnp.float32) for index in range(n_seq)
                ], axis=0))
            whole = jnp.concatenate(pieces, axis=1)
            first_x[...] = whole.astype(jnp.bfloat16)
            mine_rows = pl.ds(pl.multiple_of(sharer * part, 16), part)
            for group in range(groups):
                hid[0, slot, group] = first_x[mine_rows, group * block:(group + 1) * block]
            whole_mod = modulate(whole, ts_ref[0, slot])
            first_mod[slot] = whole_mod
            for index in range(n_seq):
                slabs[index] = whole_mod[:, index * depth:(index + 1) * depth]
            feature_rows = slabs[seq]
            for kv in range(2):
                for group in range(groups):
                    start = kv * inner + group * block
                    partial = jnp.dot(feature_rows, wrows[:, start:start + block],
                                      preferred_element_type=jnp.float32).astype(jnp.bfloat16)
                    for at in range(sharers):
                        pbuf[slot, at, group, kv] = partial[at * part:(at + 1) * part]
            for ahead in range(1, sharers):
                pin_copy(slot, ahead).start()
        for slot in range(micro):
            for ahead in range(1, sharers):
                other = lax.rem(sharer + ahead, sharers)
                pltpu.make_async_copy(pbuf.at[slot, other], pin.at[slot, other],
                                      pin_recv.at[slot, other]).wait()
            total = pbuf[slot, sharer].astype(jnp.float32)
            for ahead in range(1, sharers):
                total += pin[slot, lax.rem(sharer + ahead, sharers)].astype(jnp.float32)
            csum[slot] = total.astype(jnp.bfloat16)
            for ahead in range(1, groups):
                cin_copy(slot, ahead).start()

    pl.when(pipe != 0)(weights_finish)

    @pl.when(pipe == last)
    def _():
        for slot in range(micro):
            pieces = []
            for wide in range(per_block):
                pieces.append(jnp.concatenate([
                    latbuf_wait_load(latbuf, lat_arrived, slot == 0, mine * per_block + wide,
                                     sharer * per_part + index, slot)
                    for index in range(per_part)
                ], axis=0))
            prev[slot] = jnp.concatenate(pieces, axis=1) if per_block > 1 else pieces[0]

    def hid_send_copy(step, slot, group):
        at_last = pipe == last
        to_step = step + jnp.where(at_last, 1, 0)
        return remote(outb.at[step, slot], hid.at[to_step, slot, mine],
                      hid_send.at[step, slot, group], hid_recv.at[to_step, slot, mine],
                      lax.rem(pipe + 1, n_pipe), group * sharers + sharer)

    def hid_arrived(step, slot, group):
        pltpu.make_async_copy(outb.at[step, slot], hid.at[step, slot, group],
                              hid_recv.at[step, slot, group]).wait()

    def kvx_copy(step, slot, ahead):
        other = lax.rem(sharer + ahead, sharers)
        return remote(kvx.at[step, slot, sharer], kvx.at[step, slot, sharer], kvx_send.at[step, slot, ahead],
                      kvx_recv.at[step, slot, sharer], pipe, mine * sharers + other)

    def att_copy(step, slot, ahead):
        group = lax.rem(mine + ahead, groups)
        return remote(att.at[step, slot, mine], att.at[step, slot, mine],
                      att_send.at[step, slot, ahead], att_recv.at[step, slot, mine],
                      pipe, group * sharers + sharer)

    def att_arrived(step, slot, ahead):
        group = lax.rem(mine + ahead, groups)
        pltpu.make_async_copy(att.at[step, slot, mine], att.at[step, slot, group],
                              att_recv.at[step, slot, group]).wait()

    def fin_targets(slot):
        for wide in range(per_block):
            for index in range(per_part):
                to_pipe, to_seq = mine * per_block + wide, sharer * per_part + index
                source = fin_src.at[slot, wide, pl.ds(index * rows, rows), :]
                yield to_pipe, to_seq, source, fin_send.at[slot, wide, index]

    def first_half(step, slot):
        tau = ts_ref[step, slot]
        from_latents = (pipe == 0) & (step == 0)

        @pl.when(from_latents)
        def _():
            modded[...] = first_mod[slot, pl.ds(pl.multiple_of(sharer * part, 16), part), :]
            total = csum[slot, mine].astype(jnp.float32)
            for ahead in range(1, groups):
                group = lax.rem(mine + ahead, groups)
                pltpu.make_async_copy(csum.at[slot, group], cin.at[slot, group],
                                      cin_recv.at[slot, group]).wait()
                total += cin[slot, group].astype(jnp.float32)
            pre[...] = total

        @pl.when(jnp.logical_not(from_latents))
        def _():
            for group in range(groups):
                hid_arrived(step, slot, group)
            modded[...] = modulate(
                jnp.concatenate([hid[step, slot, group].astype(jnp.float32) for group in range(groups)], axis=1),
                tau,
            )
            for kv in range(2):
                pre[kv] = jnp.dot(modded[...], wkv[kv][...], preferred_element_type=jnp.float32)

        gain_query, gain_key = gain_ref[0, 0:1, :], gain_ref[0, 1:2, :]
        slices = [slice(head * head_dim, (head + 1) * head_dim) for head in range(heads)]
        for here in slices:
            kvx[step, slot, sharer, 0, :, here] = rms_rows(pre[0, :, here], gain_key)
        kvx[step, slot, sharer, 1] = pre[1].astype(jnp.bfloat16)
        for ahead in range(1, sharers):
            kvx_copy(step, slot, ahead).start()
        projected = jnp.dot(modded[...], wq[...], preferred_element_type=jnp.float32)
        queries = [rms_rows(projected[:, here], gain_query) for here in slices]
        totals, weighted = [0.0] * heads, [0.0] * heads
        for ahead in range(sharers):
            owner = lax.rem(sharer + ahead, sharers)
            if ahead > 0:
                pltpu.make_async_copy(kvx.at[step, slot, sharer], kvx.at[step, slot, owner],
                                      kvx_recv.at[step, slot, owner]).wait()
            for head, here in enumerate(slices):
                logits = lax.dot_general(
                    queries[head], kvx[step, slot, owner, 0, :, here],
                    (((1,), (1,)), ((), ())), preferred_element_type=jnp.float32,
                ) * score_scale
                weights = jnp.exp(logits)
                totals[head] += jnp.sum(weights, axis=-1, keepdims=True)
                weighted[head] += jnp.dot(weights.astype(jnp.bfloat16), kvx[step, slot, owner, 1, :, here],
                                          preferred_element_type=jnp.float32)
        for head, here in enumerate(slices):
            att[step, slot, mine, :, here] = (weighted[head] / totals[head]).astype(jnp.bfloat16)
        for ahead in range(1, groups):
            att_copy(step, slot, ahead).start()

    def second_half(step, slot):
        tau = ts_ref[step, slot]
        gate_row = mod_ref[0, pl.ds(tau, 1), pl.ds(pl.multiple_of(2 * width + mine * block, 128), block)]
        residual = hid[step, slot, mine].astype(jnp.float32)
        projected = 0.0
        for ahead in range(groups):
            group = lax.rem(mine + ahead, groups)
            if ahead > 0:
                att_arrived(step, slot, ahead)
            attended = att[step, slot, group]
            rows_here = pl.ds(pl.multiple_of(group * block, 128), block)
            projected += jnp.dot(attended, wo[rows_here, :], preferred_element_type=jnp.float32)
        layer_out = (residual + gate_row * projected).astype(jnp.bfloat16)
        ends = (pipe == last) & (step == steps - 1)

        @pl.when(pipe != last)
        def _():
            outb[step, slot] = layer_out

        @pl.when(pipe == last)
        def _():
            update = (prev[slot] - ss_ref[tau] * layer_out.astype(jnp.float32)).astype(jnp.bfloat16)
            outb[step, slot] = update
            prev[slot] = update.astype(jnp.float32)

        @pl.when(jnp.logical_not(ends))
        def _():
            for ahead in range(groups):
                hid_send_copy(step, slot, lax.rem(mine + ahead, groups)).start()

        @pl.when(ends)
        def _():
            update = prev[slot]
            for wide in range(per_block):
                fin_src[slot, wide] = update[:, wide * share:(wide + 1) * share]
            for to_pipe, to_seq, source, send in fin_targets(slot):
                own = (to_pipe == pipe) & (to_seq == seq)

                @pl.when(own)
                def _():
                    pltpu.make_async_copy(source, fin.at[slot], fin_recv.at[slot]).start()

                @pl.when(jnp.logical_not(own))
                def _():
                    remote(source, fin.at[slot], send, fin_recv.at[slot], to_pipe, to_seq).start()

    def visit(step, carry):
        @pl.when((pipe == 0) & (step == 1))
        def _():
            weights_start()
            weights_finish()

        for slot in range(micro):
            first_half(step, slot)
        for slot in range(micro):
            second_half(step, slot)
        return carry

    lax.fori_loop(0, steps, visit, 0)

    for slot in range(micro):
        pltpu.make_async_copy(fin_src.at[slot, 0, pl.ds(0, rows), :], fin.at[slot],
                              fin_recv.at[slot]).wait()
        out_ref[slot] = fin[slot].astype(jnp.bfloat16)

    for ahead in range(n_seq):
        target = lax.rem(seq + ahead, n_seq)
        if ahead == 0:
            @pl.when(pipe != 0)
            def _():
                lat_copy(0, target, ahead).wait_send()
        else:
            lat_copy(0, target, ahead).wait_send()

    @pl.when(jnp.logical_not(keeps_own))
    def _():
        lat_copy(last, keeper, n_seq).wait_send()

    @pl.when(pipe == 0)
    def _():
        for slot in range(micro):
            for ahead in range(1, sharers):
                pin_copy(slot, ahead).wait_send()
            for ahead in range(1, groups):
                cin_copy(slot, ahead).wait_send()

    for kv in range(2):
        for ahead in range(1, groups):
            kv_copy(kv, ahead).wait_send()
        for ahead in range(groups):
            for step in range(1, sharers):
                kv_pass(kv, ahead, step).wait_send()

    def drain(item, carry):
        step, slot = item // micro, item % micro
        ends = (pipe == last) & (step == steps - 1)
        for ahead in range(1, groups):
            att_copy(step, slot, ahead).wait_send()
        for ahead in range(1, sharers):
            kvx_copy(step, slot, ahead).wait_send()

        @pl.when(jnp.logical_not(ends))
        def _():
            for group in range(groups):
                hid_send_copy(step, slot, group).wait_send()

        @pl.when(ends)
        def _():
            for to_pipe, to_seq, source, send in fin_targets(slot):
                @pl.when(jnp.logical_not((to_pipe == pipe) & (to_seq == seq)))
                def _():
                    remote(source, fin.at[slot], send, fin_recv.at[slot], to_pipe, to_seq).wait_send()
        return carry

    lax.fori_loop(0, micro * steps, drain, 0)


def latbuf_wait_load(latbuf, lat_arrived, first, from_pipe, from_seq, slot):
    if first:
        lat_arrived(from_pipe, from_seq)
    return latbuf[from_pipe, from_seq, slot].astype(jnp.float32)


def shards(latents, timesteps, step_sizes, mod_table, qk_gain, w_query, w_kv, w_out):
    n_pipe, n_seq = lax.axis_size("pipe"), lax.axis_size("seq")
    micro, rows, share = latents.shape
    steps = timesteps.shape[0]
    head_dim = qk_gain.shape[2]
    width, inner = w_query.shape[1], w_query.shape[2]
    heads = inner // head_dim
    groups = math.gcd(math.gcd(heads, n_seq), n_pipe)
    while n_seq // groups < 2:
        groups //= 2
    sharers = n_seq // groups
    block = inner // groups
    part = rows * n_seq // sharers
    per_block, per_part = n_pipe // groups, n_seq // sharers
    bf16, f32 = jnp.bfloat16, jnp.float32
    vmem = pl.BlockSpec(memory_space=pltpu.VMEM)
    hbm = pl.BlockSpec(memory_space=pl.ANY)
    dma = pltpu.SemaphoreType.DMA
    return pl.pallas_call(
        functools.partial(kernel, n_pipe, n_seq, groups, micro, steps, head_dim),
        out_shape=jax.ShapeDtypeStruct(latents.shape, bf16),
        in_specs=[hbm] * 8,
        out_specs=vmem,
        scratch_shapes=[
            pltpu.SMEM(timesteps.shape, timesteps.dtype),
            pltpu.SMEM(step_sizes.shape, f32),
            pltpu.VMEM(mod_table.shape, f32),
            pltpu.VMEM(qk_gain.shape, f32),
            pltpu.VMEM((width, block), bf16),
            pltpu.VMEM((width, block), bf16),
            pltpu.VMEM((width, block), bf16),
            pltpu.VMEM((inner, block), bf16),
            pltpu.VMEM(w_kv.shape[1:], bf16),
            pltpu.VMEM((n_pipe, n_seq, micro, rows, share), bf16),
            pltpu.VMEM((steps, micro, groups, part, block), bf16),
            pltpu.VMEM((steps, micro, groups, part, block), bf16),
            pltpu.VMEM((steps, micro, part, block), bf16),
            pltpu.VMEM((micro, part, block), f32),
            pltpu.VMEM((part, width), bf16),
            pltpu.VMEM((rows * n_seq, width), bf16),
            pltpu.VMEM((micro, rows * n_seq, width), bf16),
            pltpu.VMEM((n_seq, rows * n_seq, w_kv.shape[1]), bf16),
            pltpu.VMEM((micro, sharers, groups, 2, part, block), bf16),
            pltpu.VMEM((micro, sharers, groups, 2, part, block), bf16),
            pltpu.VMEM((micro, groups, 2, part, block), bf16),
            pltpu.VMEM((micro, groups, 2, part, block), bf16),
            pltpu.VMEM((2, part, block), f32),
            pltpu.VMEM((steps, micro, sharers, 2, part, block), bf16),
            pltpu.VMEM((micro, per_block, part, share), f32),
            pltpu.VMEM((micro, rows, share), f32),
            dma((7,)),
            dma((2, n_seq)),
            dma((2, groups)),
            dma((2, groups, sharers)),
            dma((n_seq + 1,)),
            dma((n_pipe, n_seq)),
            dma((micro, sharers)),
            dma((micro, sharers)),
            dma((micro, groups)),
            dma((micro, groups)),
            dma((steps, micro, groups)),
            dma((steps, micro, groups)),
            dma((steps, micro, sharers)),
            dma((steps, micro, sharers)),
            dma((steps, micro, groups)),
            dma((steps, micro, groups)),
            dma((micro, per_block, per_part)),
            dma((micro,)),
        ],
        compiler_params=pltpu.CompilerParams(
            has_side_effects=True, vmem_limit_bytes=64 * 1024 * 1024
        ),
        cost_estimate=pl.CostEstimate(
            flops=2 * 4 * rows * n_seq * width * block * micro * steps,
            bytes_accessed=2 * 4 * width * block, transcendentals=0,
        ),
        name="denoise",
    )(latents, timesteps, step_sizes, mod_table, qk_gain, w_query, w_kv, w_out)


def solution(mesh):
    in_specs = (
        P(None, "seq", "pipe"),
        P(),
        P(),
        P("pipe", None, None),
        P("pipe", None, None),
        P("pipe", None, None),
        P("pipe", "seq", None),
        P("pipe", None, None),
    )
    out_specs = P(None, "seq", "pipe")
    return jax.shard_map(shards, mesh=mesh, in_specs=in_specs, out_specs=out_specs, check_vma=False)
```

```python
import functools
import math

import jax
import jax.numpy as jnp
from jax import lax
from jax.experimental import pallas as pl
from jax.experimental.pallas import tpu as pltpu
from jax.sharding import PartitionSpec as P

norm_eps = 1e-06
MESH = pl.DeviceIdType.MESH


def rms_rows(values, gain_row):
    mean_square = jnp.mean(values * values, axis=-1, keepdims=True)
    return (values * lax.rsqrt(mean_square + norm_eps) * gain_row).astype(jnp.bfloat16)


def kernel(
    n_pipe, n_seq, groups, micro, steps, head_dim,
    lat_ref, ts_hbm, ss_hbm, mod_hbm, gain_hbm, wq_hbm, wkv_hbm, wo_hbm,
    out_ref,
    ts_ref, ss_ref, mod_ref, gain_ref, wq, wk, wv, wo, wrows, latbuf, hid, att, outb, prev, modded,
    first_x, first_mod, slabs, pbuf, pin, csum, cin, pre, kvx, fin_src, fin,
    local_sem, kv_recv, kv_send, kv_fwd, lat_send, lat_recv, pin_send, pin_recv, cin_send, cin_recv,
    hid_recv, hid_send, kvx_send, kvx_recv, att_recv, att_send, fin_send, fin_recv,
):
    sharers = n_seq // groups
    rows, share = lat_ref.shape[1], lat_ref.shape[2]
    tokens = rows * n_seq
    width = share * n_pipe
    block = wq.shape[1]
    inner = block * groups
    depth = wkv_hbm.shape[1]
    part = tokens // sharers
    per_block = n_pipe // groups
    per_part = n_seq // sharers
    heads = block // head_dim
    score_scale = 1.0 / math.sqrt(head_dim)
    last = n_pipe - 1

    pipe, seq = lax.axis_index("pipe"), lax.axis_index("seq")
    mine, sharer = seq // sharers, seq % sharers

    def remote(src, dst, send, recv, to_pipe, to_seq):
        return pltpu.make_async_remote_copy(
            src_ref=src, dst_ref=dst, send_sem=send, recv_sem=recv,
            device_id=(to_pipe, to_seq), device_id_type=MESH,
        )

    def lat_copy(to_pipe, to_seq, index):
        return remote(lat_ref, latbuf.at[pipe, seq], lat_send.at[index],
                      lat_recv.at[pipe, seq], to_pipe, to_seq)

    def lat_local():
        return pltpu.make_async_copy(lat_ref, latbuf.at[pipe, seq], lat_recv.at[pipe, seq])

    def lat_arrived(from_pipe, from_seq):
        pltpu.make_async_copy(lat_ref, latbuf.at[from_pipe, from_seq],
                              lat_recv.at[from_pipe, from_seq]).wait()

    keeper = (pipe // per_block) * sharers + seq // per_part
    for ahead in range(n_seq):
        target = lax.rem(seq + ahead, n_seq)
        if ahead == 0:
            @pl.when(pipe == 0)
            def _():
                lat_local().start()

            @pl.when(pipe != 0)
            def _():
                lat_copy(0, target, ahead).start()
        else:
            lat_copy(0, target, ahead).start()
    keeps_own = (pipe == last) & (keeper == seq)

    @pl.when(keeps_own)
    def _():
        lat_local().start()

    @pl.when(jnp.logical_not(keeps_own))
    def _():
        lat_copy(last, keeper, n_seq).start()

    wkv = (wk, wv)

    def columns(kv, group):
        start = pl.multiple_of(kv * inner + group * block, 128)
        return wrows.at[:, pl.ds(start, block)]

    def slab(kv, owner):
        return wkv[kv].at[pl.ds(pl.multiple_of(owner * depth, 16), depth), :]

    def kv_copy(kv, ahead):
        group = lax.rem(mine + ahead, groups)
        return remote(columns(kv, group), slab(kv, seq), kv_send.at[kv, ahead],
                      kv_recv.at[kv, seq], pipe, group * sharers + sharer)

    def kv_pass(kv, ahead, step):
        group = lax.rem(mine + ahead, groups)
        owner = group * sharers + sharer
        source = columns(kv, mine) if ahead == 0 else slab(kv, owner)
        return remote(source, slab(kv, owner), kv_fwd.at[kv, ahead, step],
                      kv_recv.at[kv, owner], pipe, mine * sharers + lax.rem(sharer + step, sharers))

    def kv_arrived(kv, owner):
        pltpu.make_async_copy(columns(kv, mine), slab(kv, owner), kv_recv.at[kv, owner]).wait()

    rows_in = pltpu.make_async_copy(wkv_hbm.at[0], wrows, local_sem.at[6])
    rows_in.start()
    own_columns = pl.ds(pl.multiple_of(mine * block, 128), block)
    copy_q = pltpu.make_async_copy(wq_hbm.at[0, :, own_columns], wq, local_sem.at[0])
    copy_o = pltpu.make_async_copy(wo_hbm.at[0, :, own_columns], wo, local_sem.at[1])
    def weights_start():
        for kv in range(2):
            for ahead in range(groups - 1, 0, -1):
                kv_copy(kv, ahead).start()
        for kv in range(2):
            pltpu.make_async_copy(columns(kv, mine), slab(kv, seq), kv_recv.at[kv, seq]).start()
            for step in range(1, sharers):
                kv_pass(kv, 0, step).start()

    def weights_finish():
        for kv in range(2):
            for ahead in range(1, groups):
                kv_arrived(kv, lax.rem(mine + ahead, groups) * sharers + sharer)
                for step in range(1, sharers):
                    kv_pass(kv, ahead, step).start()
        for kv in range(2):
            kv_arrived(kv, seq)
            for step in range(1, sharers):
                for group in range(groups):
                    kv_arrived(kv, group * sharers + lax.rem(sharer + step, sharers))

    rows_in.wait()
    pl.when(pipe != 0)(weights_start)
    locals_in = [
        copy_q, copy_o,
        pltpu.make_async_copy(ts_hbm, ts_ref, local_sem.at[2]),
        pltpu.make_async_copy(ss_hbm, ss_ref, local_sem.at[3]),
        pltpu.make_async_copy(mod_hbm, mod_ref, local_sem.at[4]),
        pltpu.make_async_copy(gain_hbm, gain_ref, local_sem.at[5]),
    ]
    for copy in locals_in:
        copy.start()
    for copy in locals_in:
        copy.wait()

    def modulate(as_float, tau):
        center = jnp.mean(as_float, axis=-1, keepdims=True)
        away = as_float - center
        spread = jnp.mean(away * away, axis=-1, keepdims=True)
        shift_row = mod_ref[0, pl.ds(tau, 1), 0:width]
        scale_row = mod_ref[0, pl.ds(tau, 1), width:2 * width]
        return (
            away * lax.rsqrt(spread + norm_eps) * (1.0 + scale_row) + shift_row
        ).astype(jnp.bfloat16)

    def pin_copy(slot, ahead):
        other = lax.rem(sharer + ahead, sharers)
        return remote(pbuf.at[slot, other], pin.at[slot, sharer], pin_send.at[slot, ahead],
                      pin_recv.at[slot, sharer], pipe, mine * sharers + other)

    def cin_copy(slot, ahead):
        group = lax.rem(mine + ahead, groups)
        return remote(csum.at[slot, group], cin.at[slot, mine], cin_send.at[slot, ahead],
                      cin_recv.at[slot, mine], pipe, group * sharers + sharer)

    @pl.when(pipe == 0)
    def _():
        for from_pipe in range(n_pipe):
            for from_seq in range(n_seq):
                lat_arrived(from_pipe, from_seq)
        for slot in range(micro):
            pieces = []
            for from_pipe in range(n_pipe):
                pieces.append(jnp.concatenate([
                    latbuf[from_pipe, index, slot].astype(jnp.float32) for index in range(n_seq)
                ], axis=0))
            whole = jnp.concatenate(pieces, axis=1)
            first_x[...] = whole.astype(jnp.bfloat16)
            mine_rows = pl.ds(pl.multiple_of(sharer * part, 16), part)
            for group in range(groups):
                hid[0, slot, group] = first_x[mine_rows, group * block:(group + 1) * block]
            whole_mod = modulate(whole, ts_ref[0, slot])
            first_mod[slot] = whole_mod
            for index in range(n_seq):
                slabs[index] = whole_mod[:, index * depth:(index + 1) * depth]
            feature_rows = slabs[seq]
            for kv in range(2):
                for group in range(groups):
                    start = kv * inner + group * block
                    partial = jnp.dot(feature_rows, wrows[:, start:start + block],
                                      preferred_element_type=jnp.float32).astype(jnp.bfloat16)
                    for at in range(sharers):
                        pbuf[slot, at, group, kv] = partial[at * part:(at + 1) * part]
            for ahead in range(1, sharers):
                pin_copy(slot, ahead).start()
        for slot in range(micro):
            for ahead in range(1, sharers):
                other = lax.rem(sharer + ahead, sharers)
                pltpu.make_async_copy(pbuf.at[slot, other], pin.at[slot, other],
                                      pin_recv.at[slot, other]).wait()
            total = pbuf[slot, sharer].astype(jnp.float32)
            for ahead in range(1, sharers):
                total += pin[slot, lax.rem(sharer + ahead, sharers)].astype(jnp.float32)
            csum[slot] = total.astype(jnp.bfloat16)
            for ahead in range(1, groups):
                cin_copy(slot, ahead).start()

    pl.when(pipe != 0)(weights_finish)

    @pl.when(pipe == last)
    def _():
        for slot in range(micro):
            pieces = []
            for wide in range(per_block):
                pieces.append(jnp.concatenate([
                    latbuf_wait_load(latbuf, lat_arrived, slot == 0, mine * per_block + wide,
                                     sharer * per_part + index, slot)
                    for index in range(per_part)
                ], axis=0))
            prev[slot] = jnp.concatenate(pieces, axis=1) if per_block > 1 else pieces[0]

    def hid_send_copy(step, slot, group):
        at_last = pipe == last
        to_step = step + jnp.where(at_last, 1, 0)
        return remote(outb.at[step, slot], hid.at[to_step, slot, mine],
                      hid_send.at[step, slot, group], hid_recv.at[to_step, slot, mine],
                      lax.rem(pipe + 1, n_pipe), group * sharers + sharer)

    def hid_arrived(step, slot, group):
        pltpu.make_async_copy(outb.at[step, slot], hid.at[step, slot, group],
                              hid_recv.at[step, slot, group]).wait()

    def kvx_copy(step, slot, ahead):
        other = lax.rem(sharer + ahead, sharers)
        return remote(kvx.at[step, slot, sharer], kvx.at[step, slot, sharer], kvx_send.at[step, slot, ahead],
                      kvx_recv.at[step, slot, sharer], pipe, mine * sharers + other)

    def att_copy(step, slot, ahead):
        group = lax.rem(mine + ahead, groups)
        return remote(att.at[step, slot, mine], att.at[step, slot, mine],
                      att_send.at[step, slot, ahead], att_recv.at[step, slot, mine],
                      pipe, group * sharers + sharer)

    def att_arrived(step, slot, ahead):
        group = lax.rem(mine + ahead, groups)
        pltpu.make_async_copy(att.at[step, slot, mine], att.at[step, slot, group],
                              att_recv.at[step, slot, group]).wait()

    def fin_targets(slot):
        for wide in range(per_block):
            for index in range(per_part):
                to_pipe, to_seq = mine * per_block + wide, sharer * per_part + index
                source = fin_src.at[slot, wide, pl.ds(index * rows, rows), :]
                yield to_pipe, to_seq, source, fin_send.at[slot, wide, index]

    def first_half(step, slot):
        tau = ts_ref[step, slot]
        from_latents = (pipe == 0) & (step == 0)

        @pl.when(from_latents)
        def _():
            modded[...] = first_mod[slot, pl.ds(pl.multiple_of(sharer * part, 16), part), :]
            total = csum[slot, mine].astype(jnp.float32)
            for ahead in range(1, groups):
                group = lax.rem(mine + ahead, groups)
                pltpu.make_async_copy(csum.at[slot, group], cin.at[slot, group],
                                      cin_recv.at[slot, group]).wait()
                total += cin[slot, group].astype(jnp.float32)
            pre[...] = total

        @pl.when(jnp.logical_not(from_latents))
        def _():
            for group in range(groups):
                hid_arrived(step, slot, group)
            modded[...] = modulate(
                jnp.concatenate([hid[step, slot, group].astype(jnp.float32) for group in range(groups)], axis=1),
                tau,
            )
            for kv in range(2):
                pre[kv] = jnp.dot(modded[...], wkv[kv][...], preferred_element_type=jnp.float32)

        gain_query, gain_key = gain_ref[0, 0:1, :], gain_ref[0, 1:2, :]
        slices = [slice(head * head_dim, (head + 1) * head_dim) for head in range(heads)]
        for here in slices:
            kvx[step, slot, sharer, 0, :, here] = rms_rows(pre[0, :, here], gain_key)
        kvx[step, slot, sharer, 1] = pre[1].astype(jnp.bfloat16)
        for ahead in range(1, sharers):
            kvx_copy(step, slot, ahead).start()
        projected = jnp.dot(modded[...], wq[...], preferred_element_type=jnp.float32)
        queries = [rms_rows(projected[:, here], gain_query) for here in slices]
        totals, weighted = [0.0] * heads, [0.0] * heads
        for ahead in range(sharers):
            owner = lax.rem(sharer + ahead, sharers)
            if ahead > 0:
                pltpu.make_async_copy(kvx.at[step, slot, sharer], kvx.at[step, slot, owner],
                                      kvx_recv.at[step, slot, owner]).wait()
            for head, here in enumerate(slices):
                logits = lax.dot_general(
                    queries[head], kvx[step, slot, owner, 0, :, here],
                    (((1,), (1,)), ((), ())), preferred_element_type=jnp.float32,
                ) * score_scale
                weights = jnp.exp(logits)
                totals[head] += jnp.sum(weights, axis=-1, keepdims=True)
                weighted[head] += jnp.dot(weights.astype(jnp.bfloat16), kvx[step, slot, owner, 1, :, here],
                                          preferred_element_type=jnp.float32)
        for head, here in enumerate(slices):
            att[step, slot, mine, :, here] = (weighted[head] / totals[head]).astype(jnp.bfloat16)
        for ahead in range(1, groups):
            att_copy(step, slot, ahead).start()

    def second_half(step, slot):
        tau = ts_ref[step, slot]
        gate_row = mod_ref[0, pl.ds(tau, 1), pl.ds(pl.multiple_of(2 * width + mine * block, 128), block)]
        residual = hid[step, slot, mine].astype(jnp.float32)
        projected = 0.0
        for ahead in range(groups):
            group = lax.rem(mine + ahead, groups)
            if ahead > 0:
                att_arrived(step, slot, ahead)
            attended = att[step, slot, group]
            rows_here = pl.ds(pl.multiple_of(group * block, 128), block)
            projected += jnp.dot(attended, wo[rows_here, :], preferred_element_type=jnp.float32)
        layer_out = (residual + gate_row * projected).astype(jnp.bfloat16)
        ends = (pipe == last) & (step == steps - 1)

        @pl.when(pipe != last)
        def _():
            outb[step, slot] = layer_out

        @pl.when(pipe == last)
        def _():
            update = (prev[slot] - ss_ref[tau] * layer_out.astype(jnp.float32)).astype(jnp.bfloat16)
            outb[step, slot] = update
            prev[slot] = update.astype(jnp.float32)

        @pl.when(jnp.logical_not(ends))
        def _():
            for ahead in range(groups):
                hid_send_copy(step, slot, lax.rem(mine + ahead, groups)).start()

        @pl.when(ends)
        def _():
            update = prev[slot]
            for wide in range(per_block):
                fin_src[slot, wide] = update[:, wide * share:(wide + 1) * share]
            for to_pipe, to_seq, source, send in fin_targets(slot):
                own = (to_pipe == pipe) & (to_seq == seq)

                @pl.when(own)
                def _():
                    pltpu.make_async_copy(source, fin.at[slot], fin_recv.at[slot]).start()

                @pl.when(jnp.logical_not(own))
                def _():
                    remote(source, fin.at[slot], send, fin_recv.at[slot], to_pipe, to_seq).start()

    def visit(step, carry):
        @pl.when((pipe == 0) & (step == 1))
        def _():
            weights_start()
            weights_finish()

        for slot in range(micro):
            first_half(step, slot)
        for slot in range(micro):
            second_half(step, slot)
        return carry

    lax.fori_loop(0, steps, visit, 0)

    for slot in range(micro):
        pltpu.make_async_copy(fin_src.at[slot, 0, pl.ds(0, rows), :], fin.at[slot],
                              fin_recv.at[slot]).wait()
        out_ref[slot] = fin[slot].astype(jnp.bfloat16)

    for ahead in range(n_seq):
        target = lax.rem(seq + ahead, n_seq)
        if ahead == 0:
            @pl.when(pipe != 0)
            def _():
                lat_copy(0, target, ahead).wait_send()
        else:
            lat_copy(0, target, ahead).wait_send()

    @pl.when(jnp.logical_not(keeps_own))
    def _():
        lat_copy(last, keeper, n_seq).wait_send()

    @pl.when(pipe == 0)
    def _():
        for slot in range(micro):
            for ahead in range(1, sharers):
                pin_copy(slot, ahead).wait_send()
            for ahead in range(1, groups):
                cin_copy(slot, ahead).wait_send()

    for kv in range(2):
        for ahead in range(1, groups):
            kv_copy(kv, ahead).wait_send()
        for ahead in range(groups):
            for step in range(1, sharers):
                kv_pass(kv, ahead, step).wait_send()

    def drain(item, carry):
        step, slot = item // micro, item % micro
        ends = (pipe == last) & (step == steps - 1)
        for ahead in range(1, groups):
            att_copy(step, slot, ahead).wait_send()
        for ahead in range(1, sharers):
            kvx_copy(step, slot, ahead).wait_send()

        @pl.when(jnp.logical_not(ends))
        def _():
            for group in range(groups):
                hid_send_copy(step, slot, group).wait_send()

        @pl.when(ends)
        def _():
            for to_pipe, to_seq, source, send in fin_targets(slot):
                @pl.when(jnp.logical_not((to_pipe == pipe) & (to_seq == seq)))
                def _():
                    remote(source, fin.at[slot], send, fin_recv.at[slot], to_pipe, to_seq).wait_send()
        return carry

    lax.fori_loop(0, micro * steps, drain, 0)


def latbuf_wait_load(latbuf, lat_arrived, first, from_pipe, from_seq, slot):
    if first:
        lat_arrived(from_pipe, from_seq)
    return latbuf[from_pipe, from_seq, slot].astype(jnp.float32)


def shards(latents, timesteps, step_sizes, mod_table, qk_gain, w_query, w_kv, w_out):
    n_pipe, n_seq = lax.axis_size("pipe"), lax.axis_size("seq")
    micro, rows, share = latents.shape
    steps = timesteps.shape[0]
    head_dim = qk_gain.shape[2]
    width, inner = w_query.shape[1], w_query.shape[2]
    heads = inner // head_dim
    groups = math.gcd(math.gcd(heads, n_seq), n_pipe)
    while n_seq // groups < 2:
        groups //= 2
    sharers = n_seq // groups
    block = inner // groups
    part = rows * n_seq // sharers
    per_block, per_part = n_pipe // groups, n_seq // sharers
    bf16, f32 = jnp.bfloat16, jnp.float32
    vmem = pl.BlockSpec(memory_space=pltpu.VMEM)
    hbm = pl.BlockSpec(memory_space=pl.ANY)
    dma = pltpu.SemaphoreType.DMA
    return pl.pallas_call(
        functools.partial(kernel, n_pipe, n_seq, groups, micro, steps, head_dim),
        out_shape=jax.ShapeDtypeStruct(latents.shape, bf16),
        in_specs=[hbm] * 8,
        out_specs=vmem,
        scratch_shapes=[
            pltpu.SMEM(timesteps.shape, timesteps.dtype),
            pltpu.SMEM(step_sizes.shape, f32),
            pltpu.VMEM(mod_table.shape, f32),
            pltpu.VMEM(qk_gain.shape, f32),
            pltpu.VMEM((width, block), bf16),
            pltpu.VMEM((width, block), bf16),
            pltpu.VMEM((width, block), bf16),
            pltpu.VMEM((inner, block), bf16),
            pltpu.VMEM(w_kv.shape[1:], bf16),
            pltpu.VMEM((n_pipe, n_seq, micro, rows, share), bf16),
            pltpu.VMEM((steps, micro, groups, part, block), bf16),
            pltpu.VMEM((steps, micro, groups, part, block), bf16),
            pltpu.VMEM((steps, micro, part, block), bf16),
            pltpu.VMEM((micro, part, block), f32),
            pltpu.VMEM((part, width), bf16),
            pltpu.VMEM((rows * n_seq, width), bf16),
            pltpu.VMEM((micro, rows * n_seq, width), bf16),
            pltpu.VMEM((n_seq, rows * n_seq, w_kv.shape[1]), bf16),
            pltpu.VMEM((micro, sharers, groups, 2, part, block), bf16),
            pltpu.VMEM((micro, sharers, groups, 2, part, block), bf16),
            pltpu.VMEM((micro, groups, 2, part, block), bf16),
            pltpu.VMEM((micro, groups, 2, part, block), bf16),
            pltpu.VMEM((2, part, block), f32),
            pltpu.VMEM((steps, micro, sharers, 2, part, block), bf16),
            pltpu.VMEM((micro, per_block, part, share), f32),
            pltpu.VMEM((micro, rows, share), f32),
            dma((7,)),
            dma((2, n_seq)),
            dma((2, groups)),
            dma((2, groups, sharers)),
            dma((n_seq + 1,)),
            dma((n_pipe, n_seq)),
            dma((micro, sharers)),
            dma((micro, sharers)),
            dma((micro, groups)),
            dma((micro, groups)),
            dma((steps, micro, groups)),
            dma((steps, micro, groups)),
            dma((steps, micro, sharers)),
            dma((steps, micro, sharers)),
            dma((steps, micro, groups)),
            dma((steps, micro, groups)),
            dma((micro, per_block, per_part)),
            dma((micro,)),
        ],
        compiler_params=pltpu.CompilerParams(
            has_side_effects=True, vmem_limit_bytes=64 * 1024 * 1024
        ),
        cost_estimate=pl.CostEstimate(
            flops=2 * 4 * rows * n_seq * width * block * micro * steps,
            bytes_accessed=2 * 4 * width * block, transcendentals=0,
        ),
        name="denoise",
    )(latents, timesteps, step_sizes, mod_table, qk_gain, w_query, w_kv, w_out)


def solution(mesh):
    in_specs = (
        P(None, "seq", "pipe"),
        P(),
        P(),
        P("pipe", None, None),
        P("pipe", None, None),
        P("pipe", None, None),
        P("pipe", "seq", None),
        P("pipe", None, None),
    )
    out_specs = P(None, "seq", "pipe")
    return jax.shard_map(shards, mesh=mesh, in_specs=in_specs, out_specs=out_specs, check_vma=False)
```

```python
import functools
import math

import jax
import jax.numpy as jnp
from jax import lax
from jax.experimental import pallas as pl
from jax.experimental.pallas import tpu as pltpu
from jax.sharding import PartitionSpec as P

norm_eps = 1e-06
MESH = pl.DeviceIdType.MESH


def rms_rows(values, gain_row):
    mean_square = jnp.mean(values * values, axis=-1, keepdims=True)
    return (values * lax.rsqrt(mean_square + norm_eps) * gain_row).astype(jnp.bfloat16)


def kernel(
    n_pipe, n_seq, groups, micro, steps, head_dim,
    lat_ref, ts_hbm, ss_hbm, mod_hbm, gain_hbm, wq_hbm, wkv_hbm, wo_hbm,
    out_ref,
    ts_ref, ss_ref, mod_ref, gain_ref, wq, wkv, wo, wrows, latbuf, hid, att, outb, prev, modded,
    first_x, first_mod, slabs, pbuf, pin, csum, cin, pre, kvx, fin_src, fin,
    local_sem, kv_recv, kv_send, kv_fwd, lat_send, lat_recv, pin_send, pin_recv, cin_send, cin_recv,
    hid_recv, hid_send, kvx_send, kvx_recv, att_recv, att_send, fin_send, fin_recv,
):
    sharers = n_seq // groups
    rows, share = lat_ref.shape[1], lat_ref.shape[2]
    tokens = rows * n_seq
    width = share * n_pipe
    block = wq.shape[1]
    inner = block * groups
    depth = wkv_hbm.shape[1]
    part = tokens // sharers
    per_block = n_pipe // groups
    per_part = n_seq // sharers
    heads = block // head_dim
    score_scale = 1.0 / math.sqrt(head_dim)
    last = n_pipe - 1

    pipe, seq = lax.axis_index("pipe"), lax.axis_index("seq")
    mine, sharer = seq // sharers, seq % sharers

    def remote(src, dst, send, recv, to_pipe, to_seq):
        return pltpu.make_async_remote_copy(
            src_ref=src, dst_ref=dst, send_sem=send, recv_sem=recv,
            device_id=(to_pipe, to_seq), device_id_type=MESH,
        )

    def lat_copy(to_pipe, to_seq, index):
        return remote(lat_ref, latbuf.at[pipe, seq], lat_send.at[index],
                      lat_recv.at[pipe, seq], to_pipe, to_seq)

    def lat_local():
        return pltpu.make_async_copy(lat_ref, latbuf.at[pipe, seq], lat_recv.at[pipe, seq])

    def lat_arrived(from_pipe, from_seq):
        pltpu.make_async_copy(lat_ref, latbuf.at[from_pipe, from_seq],
                              lat_recv.at[from_pipe, from_seq]).wait()

    keeper = (pipe // per_block) * sharers + seq // per_part
    for ahead in range(n_seq):
        target = lax.rem(seq + ahead, n_seq)
        if ahead == 0:
            @pl.when(pipe == 0)
            def _():
                lat_local().start()

            @pl.when(pipe != 0)
            def _():
                lat_copy(0, target, ahead).start()
        else:
            lat_copy(0, target, ahead).start()
    keeps_own = (pipe == last) & (keeper == seq)

    @pl.when(keeps_own)
    def _():
        lat_local().start()

    @pl.when(jnp.logical_not(keeps_own))
    def _():
        lat_copy(last, keeper, n_seq).start()


    def columns(kv, group):
        start = pl.multiple_of(kv * inner + group * block, 128)
        return wrows.at[:, pl.ds(start, block)]

    def slab(kv, owner):
        return wkv.at[pl.ds(pl.multiple_of(owner * depth, 16), depth), kv * block:(kv + 1) * block]

    def kv_copy(kv, ahead):
        group = lax.rem(mine + ahead, groups)
        return remote(columns(kv, group), slab(kv, seq), kv_send.at[kv, ahead],
                      kv_recv.at[kv, seq], pipe, group * sharers + sharer)

    def kv_pass(kv, ahead, step):
        group = lax.rem(mine + ahead, groups)
        owner = group * sharers + sharer
        source = columns(kv, mine) if ahead == 0 else slab(kv, owner)
        return remote(source, slab(kv, owner), kv_fwd.at[kv, ahead, step],
                      kv_recv.at[kv, owner], pipe, mine * sharers + lax.rem(sharer + step, sharers))

    def kv_arrived(kv, owner):
        pltpu.make_async_copy(columns(kv, mine), slab(kv, owner), kv_recv.at[kv, owner]).wait()

    rows_in = pltpu.make_async_copy(wkv_hbm.at[0], wrows, local_sem.at[6])
    rows_in.start()
    own_columns = pl.ds(pl.multiple_of(mine * block, 128), block)
    copy_q = pltpu.make_async_copy(wq_hbm.at[0, :, own_columns], wq, local_sem.at[0])
    copy_o = pltpu.make_async_copy(wo_hbm.at[0, :, own_columns], wo, local_sem.at[1])
    def weights_start():
        for kv in range(2):
            for ahead in range(groups - 1, 0, -1):
                kv_copy(kv, ahead).start()
        for kv in range(2):
            pltpu.make_async_copy(columns(kv, mine), slab(kv, seq), kv_recv.at[kv, seq]).start()
            for step in range(1, sharers):
                kv_pass(kv, 0, step).start()

    def weights_finish():
        for kv in range(2):
            for ahead in range(1, groups):
                kv_arrived(kv, lax.rem(mine + ahead, groups) * sharers + sharer)
                for step in range(1, sharers):
                    kv_pass(kv, ahead, step).start()
        for kv in range(2):
            kv_arrived(kv, seq)
            for step in range(1, sharers):
                for group in range(groups):
                    kv_arrived(kv, group * sharers + lax.rem(sharer + step, sharers))

    rows_in.wait()
    pl.when(pipe != 0)(weights_start)
    locals_in = [
        copy_q, copy_o,
        pltpu.make_async_copy(ts_hbm, ts_ref, local_sem.at[2]),
        pltpu.make_async_copy(ss_hbm, ss_ref, local_sem.at[3]),
        pltpu.make_async_copy(mod_hbm, mod_ref, local_sem.at[4]),
        pltpu.make_async_copy(gain_hbm, gain_ref, local_sem.at[5]),
    ]
    for copy in locals_in:
        copy.start()
    for copy in locals_in:
        copy.wait()

    def modulate(as_float, tau):
        center = jnp.mean(as_float, axis=-1, keepdims=True)
        away = as_float - center
        spread = jnp.mean(away * away, axis=-1, keepdims=True)
        shift_row = mod_ref[0, pl.ds(tau, 1), 0:width]
        scale_row = mod_ref[0, pl.ds(tau, 1), width:2 * width]
        return (
            away * lax.rsqrt(spread + norm_eps) * (1.0 + scale_row) + shift_row
        ).astype(jnp.bfloat16)

    def pin_copy(slot, ahead):
        other = lax.rem(sharer + ahead, sharers)
        return remote(pbuf.at[slot, other], pin.at[slot, sharer], pin_send.at[slot, ahead],
                      pin_recv.at[slot, sharer], pipe, mine * sharers + other)

    def cin_copy(slot, ahead):
        group = lax.rem(mine + ahead, groups)
        return remote(csum.at[slot, group], cin.at[slot, mine], cin_send.at[slot, ahead],
                      cin_recv.at[slot, mine], pipe, group * sharers + sharer)

    @pl.when(pipe == 0)
    def _():
        for from_pipe in range(n_pipe):
            for from_seq in range(n_seq):
                lat_arrived(from_pipe, from_seq)
        for slot in range(micro):
            pieces = []
            for from_pipe in range(n_pipe):
                pieces.append(jnp.concatenate([
                    latbuf[from_pipe, index, slot].astype(jnp.float32) for index in range(n_seq)
                ], axis=0))
            whole = jnp.concatenate(pieces, axis=1)
            first_x[...] = whole.astype(jnp.bfloat16)
            mine_rows = pl.ds(pl.multiple_of(sharer * part, 16), part)
            for group in range(groups):
                hid[0, slot, group] = first_x[mine_rows, group * block:(group + 1) * block]
            whole_mod = modulate(whole, ts_ref[0, slot])
            first_mod[slot] = whole_mod
            for index in range(n_seq):
                slabs[index] = whole_mod[:, index * depth:(index + 1) * depth]
            feature_rows = slabs[seq]
            for kv in range(2):
                for group in range(groups):
                    start = kv * inner + group * block
                    partial = jnp.dot(feature_rows, wrows[:, start:start + block],
                                      preferred_element_type=jnp.float32).astype(jnp.bfloat16)
                    for at in range(sharers):
                        pbuf[slot, at, group, kv] = partial[at * part:(at + 1) * part]
            for ahead in range(1, sharers):
                pin_copy(slot, ahead).start()
        for slot in range(micro):
            for ahead in range(1, sharers):
                other = lax.rem(sharer + ahead, sharers)
                pltpu.make_async_copy(pbuf.at[slot, other], pin.at[slot, other],
                                      pin_recv.at[slot, other]).wait()
            total = pbuf[slot, sharer].astype(jnp.float32)
            for ahead in range(1, sharers):
                total += pin[slot, lax.rem(sharer + ahead, sharers)].astype(jnp.float32)
            csum[slot] = total.astype(jnp.bfloat16)
            for ahead in range(1, groups):
                cin_copy(slot, ahead).start()

    pl.when(pipe != 0)(weights_finish)

    @pl.when(pipe == last)
    def _():
        for slot in range(micro):
            pieces = []
            for wide in range(per_block):
                pieces.append(jnp.concatenate([
                    latbuf_wait_load(latbuf, lat_arrived, slot == 0, mine * per_block + wide,
                                     sharer * per_part + index, slot)
                    for index in range(per_part)
                ], axis=0))
            prev[slot] = jnp.concatenate(pieces, axis=1) if per_block > 1 else pieces[0]

    def hid_send_copy(step, slot, group):
        at_last = pipe == last
        to_step = step + jnp.where(at_last, 1, 0)
        return remote(outb.at[step, slot], hid.at[to_step, slot, mine],
                      hid_send.at[step, slot, group], hid_recv.at[to_step, slot, mine],
                      lax.rem(pipe + 1, n_pipe), group * sharers + sharer)

    def hid_arrived(step, slot, group):
        pltpu.make_async_copy(outb.at[step, slot], hid.at[step, slot, group],
                              hid_recv.at[step, slot, group]).wait()

    def kvx_copy(step, slot, ahead):
        other = lax.rem(sharer + ahead, sharers)
        return remote(kvx.at[step, slot, sharer], kvx.at[step, slot, sharer], kvx_send.at[step, slot, ahead],
                      kvx_recv.at[step, slot, sharer], pipe, mine * sharers + other)

    def att_copy(step, slot, ahead):
        group = lax.rem(mine + ahead, groups)
        return remote(att.at[step, slot, mine], att.at[step, slot, mine],
                      att_send.at[step, slot, ahead], att_recv.at[step, slot, mine],
                      pipe, group * sharers + sharer)

    def att_arrived(step, slot, ahead):
        group = lax.rem(mine + ahead, groups)
        pltpu.make_async_copy(att.at[step, slot, mine], att.at[step, slot, group],
                              att_recv.at[step, slot, group]).wait()

    def fin_targets(slot):
        for wide in range(per_block):
            for index in range(per_part):
                to_pipe, to_seq = mine * per_block + wide, sharer * per_part + index
                source = fin_src.at[slot, wide, pl.ds(index * rows, rows), :]
                yield to_pipe, to_seq, source, fin_send.at[slot, wide, index]

    def first_half(step, slot):
        tau = ts_ref[step, slot]
        from_latents = (pipe == 0) & (step == 0)

        @pl.when(from_latents)
        def _():
            modded[...] = first_mod[slot, pl.ds(pl.multiple_of(sharer * part, 16), part), :]
            total = csum[slot, mine].astype(jnp.float32)
            for ahead in range(1, groups):
                group = lax.rem(mine + ahead, groups)
                pltpu.make_async_copy(csum.at[slot, group], cin.at[slot, group],
                                      cin_recv.at[slot, group]).wait()
                total += cin[slot, group].astype(jnp.float32)
            pre[:, :block] = total[0]
            pre[:, block:] = total[1]

        @pl.when(jnp.logical_not(from_latents))
        def _():
            for group in range(groups):
                hid_arrived(step, slot, group)
            modded[...] = modulate(
                jnp.concatenate([hid[step, slot, group].astype(jnp.float32) for group in range(groups)], axis=1),
                tau,
            )
            pre[...] = jnp.dot(modded[...], wkv[...], preferred_element_type=jnp.float32)

        gain_query, gain_key = gain_ref[0, 0:1, :], gain_ref[0, 1:2, :]
        slices = [slice(head * head_dim, (head + 1) * head_dim) for head in range(heads)]
        for here in slices:
            kvx[step, slot, sharer, 0, :, here] = rms_rows(pre[:, here], gain_key)
        kvx[step, slot, sharer, 1] = pre[:, block:].astype(jnp.bfloat16)
        for ahead in range(1, sharers):
            kvx_copy(step, slot, ahead).start()
        projected = jnp.dot(modded[...], wq[...], preferred_element_type=jnp.float32)
        queries = [rms_rows(projected[:, here], gain_query) for here in slices]
        totals, weighted = [0.0] * heads, [0.0] * heads
        for ahead in range(sharers):
            owner = lax.rem(sharer + ahead, sharers)
            if ahead > 0:
                pltpu.make_async_copy(kvx.at[step, slot, sharer], kvx.at[step, slot, owner],
                                      kvx_recv.at[step, slot, owner]).wait()
            for head, here in enumerate(slices):
                logits = lax.dot_general(
                    queries[head], kvx[step, slot, owner, 0, :, here],
                    (((1,), (1,)), ((), ())), preferred_element_type=jnp.float32,
                ) * score_scale
                weights = jnp.exp(logits)
                totals[head] += jnp.sum(weights, axis=-1, keepdims=True)
                weighted[head] += jnp.dot(weights.astype(jnp.bfloat16), kvx[step, slot, owner, 1, :, here],
                                          preferred_element_type=jnp.float32)
        for head, here in enumerate(slices):
            att[step, slot, mine, :, here] = (weighted[head] / totals[head]).astype(jnp.bfloat16)
        for ahead in range(1, groups):
            att_copy(step, slot, ahead).start()

    def second_half(step, slot):
        tau = ts_ref[step, slot]
        gate_row = mod_ref[0, pl.ds(tau, 1), pl.ds(pl.multiple_of(2 * width + mine * block, 128), block)]
        residual = hid[step, slot, mine].astype(jnp.float32)
        projected = 0.0
        for ahead in range(groups):
            group = lax.rem(mine + ahead, groups)
            if ahead > 0:
                att_arrived(step, slot, ahead)
            attended = att[step, slot, group]
            rows_here = pl.ds(pl.multiple_of(group * block, 128), block)
            projected += jnp.dot(attended, wo[rows_here, :], preferred_element_type=jnp.float32)
        layer_out = (residual + gate_row * projected).astype(jnp.bfloat16)
        ends = (pipe == last) & (step == steps - 1)

        @pl.when(pipe != last)
        def _():
            outb[step, slot] = layer_out

        @pl.when(pipe == last)
        def _():
            update = (prev[slot] - ss_ref[tau] * layer_out.astype(jnp.float32)).astype(jnp.bfloat16)
            outb[step, slot] = update
            prev[slot] = update.astype(jnp.float32)

        @pl.when(jnp.logical_not(ends))
        def _():
            for ahead in range(groups):
                hid_send_copy(step, slot, lax.rem(mine + ahead, groups)).start()

        @pl.when(ends)
        def _():
            update = prev[slot]
            for wide in range(per_block):
                fin_src[slot, wide] = update[:, wide * share:(wide + 1) * share]
            for to_pipe, to_seq, source, send in fin_targets(slot):
                own = (to_pipe == pipe) & (to_seq == seq)

                @pl.when(own)
                def _():
                    pltpu.make_async_copy(source, fin.at[slot], fin_recv.at[slot]).start()

                @pl.when(jnp.logical_not(own))
                def _():
                    remote(source, fin.at[slot], send, fin_recv.at[slot], to_pipe, to_seq).start()

    def visit(step, carry):
        @pl.when((pipe == 0) & (step == 1))
        def _():
            weights_start()
            weights_finish()

        for slot in range(micro):
            first_half(step, slot)
            second_half(step, slot)
        return carry

    lax.fori_loop(0, steps, visit, 0)

    for slot in range(micro):
        pltpu.make_async_copy(fin_src.at[slot, 0, pl.ds(0, rows), :], fin.at[slot],
                              fin_recv.at[slot]).wait()
        out_ref[slot] = fin[slot].astype(jnp.bfloat16)

    for ahead in range(n_seq):
        target = lax.rem(seq + ahead, n_seq)
        if ahead == 0:
            @pl.when(pipe != 0)
            def _():
                lat_copy(0, target, ahead).wait_send()
        else:
            lat_copy(0, target, ahead).wait_send()

    @pl.when(jnp.logical_not(keeps_own))
    def _():
        lat_copy(last, keeper, n_seq).wait_send()

    @pl.when(pipe == 0)
    def _():
        for slot in range(micro):
            for ahead in range(1, sharers):
                pin_copy(slot, ahead).wait_send()
            for ahead in range(1, groups):
                cin_copy(slot, ahead).wait_send()

    for kv in range(2):
        for ahead in range(1, groups):
            kv_copy(kv, ahead).wait_send()
        for ahead in range(groups):
            for step in range(1, sharers):
                kv_pass(kv, ahead, step).wait_send()

    def drain(item, carry):
        step, slot = item // micro, item % micro
        ends = (pipe == last) & (step == steps - 1)
        for ahead in range(1, groups):
            att_copy(step, slot, ahead).wait_send()
        for ahead in range(1, sharers):
            kvx_copy(step, slot, ahead).wait_send()

        @pl.when(jnp.logical_not(ends))
        def _():
            for group in range(groups):
                hid_send_copy(step, slot, group).wait_send()

        @pl.when(ends)
        def _():
            for to_pipe, to_seq, source, send in fin_targets(slot):
                @pl.when(jnp.logical_not((to_pipe == pipe) & (to_seq == seq)))
                def _():
                    remote(source, fin.at[slot], send, fin_recv.at[slot], to_pipe, to_seq).wait_send()
        return carry

    lax.fori_loop(0, micro * steps, drain, 0)


def latbuf_wait_load(latbuf, lat_arrived, first, from_pipe, from_seq, slot):
    if first:
        lat_arrived(from_pipe, from_seq)
    return latbuf[from_pipe, from_seq, slot].astype(jnp.float32)


def shards(latents, timesteps, step_sizes, mod_table, qk_gain, w_query, w_kv, w_out):
    n_pipe, n_seq = lax.axis_size("pipe"), lax.axis_size("seq")
    micro, rows, share = latents.shape
    steps = timesteps.shape[0]
    head_dim = qk_gain.shape[2]
    width, inner = w_query.shape[1], w_query.shape[2]
    heads = inner // head_dim
    groups = math.gcd(math.gcd(heads, n_seq), n_pipe)
    while n_seq // groups < 2:
        groups //= 2
    sharers = n_seq // groups
    block = inner // groups
    part = rows * n_seq // sharers
    per_block, per_part = n_pipe // groups, n_seq // sharers
    bf16, f32 = jnp.bfloat16, jnp.float32
    vmem = pl.BlockSpec(memory_space=pltpu.VMEM)
    hbm = pl.BlockSpec(memory_space=pl.ANY)
    dma = pltpu.SemaphoreType.DMA
    return pl.pallas_call(
        functools.partial(kernel, n_pipe, n_seq, groups, micro, steps, head_dim),
        out_shape=jax.ShapeDtypeStruct(latents.shape, bf16),
        in_specs=[hbm] * 8,
        out_specs=vmem,
        scratch_shapes=[
            pltpu.SMEM(timesteps.shape, timesteps.dtype),
            pltpu.SMEM(step_sizes.shape, f32),
            pltpu.VMEM(mod_table.shape, f32),
            pltpu.VMEM(qk_gain.shape, f32),
            pltpu.VMEM((width, block), bf16),
            pltpu.VMEM((width, 2 * block), bf16),
            pltpu.VMEM((inner, block), bf16),
            pltpu.VMEM(w_kv.shape[1:], bf16),
            pltpu.VMEM((n_pipe, n_seq, micro, rows, share), bf16),
            pltpu.VMEM((steps, micro, groups, part, block), bf16),
            pltpu.VMEM((steps, micro, groups, part, block), bf16),
            pltpu.VMEM((steps, micro, part, block), bf16),
            pltpu.VMEM((micro, part, block), f32),
            pltpu.VMEM((part, width), bf16),
            pltpu.VMEM((rows * n_seq, width), bf16),
            pltpu.VMEM((micro, rows * n_seq, width), bf16),
            pltpu.VMEM((n_seq, rows * n_seq, w_kv.shape[1]), bf16),
            pltpu.VMEM((micro, sharers, groups, 2, part, block), bf16),
            pltpu.VMEM((micro, sharers, groups, 2, part, block), bf16),
            pltpu.VMEM((micro, groups, 2, part, block), bf16),
            pltpu.VMEM((micro, groups, 2, part, block), bf16),
            pltpu.VMEM((part, 2 * block), f32),
            pltpu.VMEM((steps, micro, sharers, 2, part, block), bf16),
            pltpu.VMEM((micro, per_block, part, share), f32),
            pltpu.VMEM((micro, rows, share), f32),
            dma((7,)),
            dma((2, n_seq)),
            dma((2, groups)),
            dma((2, groups, sharers)),
            dma((n_seq + 1,)),
            dma((n_pipe, n_seq)),
            dma((micro, sharers)),
            dma((micro, sharers)),
            dma((micro, groups)),
            dma((micro, groups)),
            dma((steps, micro, groups)),
            dma((steps, micro, groups)),
            dma((steps, micro, sharers)),
            dma((steps, micro, sharers)),
            dma((steps, micro, groups)),
            dma((steps, micro, groups)),
            dma((micro, per_block, per_part)),
            dma((micro,)),
        ],
        compiler_params=pltpu.CompilerParams(
            has_side_effects=True, vmem_limit_bytes=64 * 1024 * 1024
        ),
        cost_estimate=pl.CostEstimate(
            flops=2 * 4 * rows * n_seq * width * block * micro * steps,
            bytes_accessed=2 * 4 * width * block, transcendentals=0,
        ),
        name="denoise",
    )(latents, timesteps, step_sizes, mod_table, qk_gain, w_query, w_kv, w_out)


def solution(mesh):
    in_specs = (
        P(None, "seq", "pipe"),
        P(),
        P(),
        P("pipe", None, None),
        P("pipe", None, None),
        P("pipe", None, None),
        P("pipe", "seq", None),
        P("pipe", None, None),
    )
    out_specs = P(None, "seq", "pipe")
    return jax.shard_map(shards, mesh=mesh, in_specs=in_specs, out_specs=out_specs, check_vma=False)
```

```python
import functools
import math

import jax
import jax.numpy as jnp
from jax import lax
from jax.experimental import pallas as pl
from jax.experimental.pallas import tpu as pltpu
from jax.sharding import PartitionSpec as P

norm_eps = 1e-06
MESH = pl.DeviceIdType.MESH


def rms_rows(values, gain_row):
    mean_square = jnp.mean(values * values, axis=-1, keepdims=True)
    return (values * lax.rsqrt(mean_square + norm_eps) * gain_row).astype(jnp.bfloat16)


def kernel(
    n_pipe, n_seq, groups, micro, steps, head_dim,
    lat_ref, ts_hbm, ss_hbm, mod_hbm, gain_hbm, wq_hbm, wkv_hbm, wo_hbm,
    out_ref,
    ts_ref, ss_ref, mod_ref, gain_ref, wq, wkv, wo, stage, latbuf, hid, att, outb, prev, modded,
    first_x, first_mod, slabs, pbuf, pin, csum, cin, pre, kvx, fin_src, fin,
    local_sem, stage_sem, kv_recv, kv_send, kv_fwd, lat_send, lat_recv, pin_send, pin_recv, cin_send, cin_recv,
    hid_recv, hid_send, kvx_send, kvx_recv, att_recv, att_send, fin_send, fin_recv,
):
    sharers = n_seq // groups
    rows, share = lat_ref.shape[1], lat_ref.shape[2]
    tokens = rows * n_seq
    width = share * n_pipe
    block = wq.shape[1]
    inner = block * groups
    depth = wkv_hbm.shape[1]
    part = tokens // sharers
    per_block = n_pipe // groups
    per_part = n_seq // sharers
    heads = block // head_dim
    score_scale = 1.0 / math.sqrt(head_dim)
    last = n_pipe - 1

    pipe, seq = lax.axis_index("pipe"), lax.axis_index("seq")
    mine, sharer = seq // sharers, seq % sharers

    def remote(src, dst, send, recv, to_pipe, to_seq):
        return pltpu.make_async_remote_copy(
            src_ref=src, dst_ref=dst, send_sem=send, recv_sem=recv,
            device_id=(to_pipe, to_seq), device_id_type=MESH,
        )

    def lat_copy(to_pipe, to_seq, index):
        return remote(lat_ref, latbuf.at[pipe, seq], lat_send.at[index],
                      lat_recv.at[pipe, seq], to_pipe, to_seq)

    def lat_local():
        return pltpu.make_async_copy(lat_ref, latbuf.at[pipe, seq], lat_recv.at[pipe, seq])

    def lat_arrived(from_pipe, from_seq):
        pltpu.make_async_copy(lat_ref, latbuf.at[from_pipe, from_seq],
                              lat_recv.at[from_pipe, from_seq]).wait()

    keeper = (pipe // per_block) * sharers + seq // per_part
    for ahead in range(n_seq):
        target = lax.rem(seq + ahead, n_seq)
        if ahead == 0:
            @pl.when(pipe == 0)
            def _():
                lat_local().start()

            @pl.when(pipe != 0)
            def _():
                lat_copy(0, target, ahead).start()
        else:
            lat_copy(0, target, ahead).start()
    keeps_own = (pipe == last) & (keeper == seq)

    @pl.when(keeps_own)
    def _():
        lat_local().start()

    @pl.when(jnp.logical_not(keeps_own))
    def _():
        lat_copy(last, keeper, n_seq).start()


    def slab(owner):
        return wkv.at[pl.ds(pl.multiple_of(owner * depth, 16), depth), :]

    def kv_copy(ahead):
        group = lax.rem(mine + ahead, groups)
        return remote(stage.at[group], slab(seq), kv_send.at[ahead],
                      kv_recv.at[seq], pipe, group * sharers + sharer)

    def kv_pass(ahead, step):
        owner = lax.rem(mine + ahead, groups) * sharers + sharer
        source = stage.at[mine] if ahead == 0 else slab(owner)
        return remote(source, slab(owner), kv_fwd.at[ahead, step],
                      kv_recv.at[owner], pipe, mine * sharers + lax.rem(sharer + step, sharers))

    def kv_arrived(owner):
        pltpu.make_async_copy(stage.at[mine], slab(owner), kv_recv.at[owner]).wait()

    def weights_start():
        for ahead in range(groups - 1, 0, -1):
            kv_copy(ahead).start()
        pltpu.make_async_copy(stage.at[mine], slab(seq), kv_recv.at[seq]).start()
        for step in range(1, sharers):
            kv_pass(0, step).start()

    def weights_finish():
        for ahead in range(1, groups):
            kv_arrived(lax.rem(mine + ahead, groups) * sharers + sharer)
            for step in range(1, sharers):
                kv_pass(ahead, step).start()
        kv_arrived(seq)
        for step in range(1, sharers):
            for group in range(groups):
                kv_arrived(group * sharers + lax.rem(sharer + step, sharers))

    staging = [
        pltpu.make_async_copy(
            wkv_hbm.at[0, :, kv * inner + group * block:kv * inner + (group + 1) * block],
            stage.at[group, :, kv * block:(kv + 1) * block], stage_sem.at[kv, group],
        )
        for group in range(groups) for kv in range(2)
    ]
    for copy in staging:
        copy.start()
    own_columns = pl.ds(pl.multiple_of(mine * block, 128), block)
    copy_q = pltpu.make_async_copy(wq_hbm.at[0, :, own_columns], wq, local_sem.at[0])
    copy_o = pltpu.make_async_copy(wo_hbm.at[0, :, own_columns], wo, local_sem.at[1])
    for copy in staging:
        copy.wait()
    pl.when(pipe != 0)(weights_start)
    locals_in = [
        copy_q, copy_o,
        pltpu.make_async_copy(ts_hbm, ts_ref, local_sem.at[2]),
        pltpu.make_async_copy(ss_hbm, ss_ref, local_sem.at[3]),
        pltpu.make_async_copy(mod_hbm, mod_ref, local_sem.at[4]),
        pltpu.make_async_copy(gain_hbm, gain_ref, local_sem.at[5]),
    ]
    for copy in locals_in:
        copy.start()
    for copy in locals_in:
        copy.wait()

    def modulate(as_float, tau):
        center = jnp.mean(as_float, axis=-1, keepdims=True)
        away = as_float - center
        spread = jnp.mean(away * away, axis=-1, keepdims=True)
        shift_row = mod_ref[0, pl.ds(tau, 1), 0:width]
        scale_row = mod_ref[0, pl.ds(tau, 1), width:2 * width]
        return (
            away * lax.rsqrt(spread + norm_eps) * (1.0 + scale_row) + shift_row
        ).astype(jnp.bfloat16)

    def pin_copy(slot, ahead):
        other = lax.rem(sharer + ahead, sharers)
        return remote(pbuf.at[slot, other], pin.at[slot, sharer], pin_send.at[slot, ahead],
                      pin_recv.at[slot, sharer], pipe, mine * sharers + other)

    def cin_copy(slot, ahead):
        group = lax.rem(mine + ahead, groups)
        return remote(csum.at[slot, group], cin.at[slot, mine], cin_send.at[slot, ahead],
                      cin_recv.at[slot, mine], pipe, group * sharers + sharer)

    @pl.when(pipe == 0)
    def _():
        for from_pipe in range(n_pipe):
            for from_seq in range(n_seq):
                lat_arrived(from_pipe, from_seq)
        for slot in range(micro):
            pieces = []
            for from_pipe in range(n_pipe):
                pieces.append(jnp.concatenate([
                    latbuf[from_pipe, index, slot].astype(jnp.float32) for index in range(n_seq)
                ], axis=0))
            whole = jnp.concatenate(pieces, axis=1)
            first_x[...] = whole.astype(jnp.bfloat16)
            mine_rows = pl.ds(pl.multiple_of(sharer * part, 16), part)
            for group in range(groups):
                hid[0, slot, group] = first_x[mine_rows, group * block:(group + 1) * block]
            whole_mod = modulate(whole, ts_ref[0, slot])
            first_mod[slot] = whole_mod
            for index in range(n_seq):
                slabs[index] = whole_mod[:, index * depth:(index + 1) * depth]
            feature_rows = slabs[seq]
            for group in range(groups):
                partial = jnp.dot(feature_rows, stage[group],
                                  preferred_element_type=jnp.float32).astype(jnp.bfloat16)
                for at in range(sharers):
                    for kv in range(2):
                        pbuf[slot, at, group, kv] = partial[at * part:(at + 1) * part,
                                                            kv * block:(kv + 1) * block]
            for ahead in range(1, sharers):
                pin_copy(slot, ahead).start()
        for slot in range(micro):
            for ahead in range(1, sharers):
                other = lax.rem(sharer + ahead, sharers)
                pltpu.make_async_copy(pbuf.at[slot, other], pin.at[slot, other],
                                      pin_recv.at[slot, other]).wait()
            total = pbuf[slot, sharer].astype(jnp.float32)
            for ahead in range(1, sharers):
                total += pin[slot, lax.rem(sharer + ahead, sharers)].astype(jnp.float32)
            csum[slot] = total.astype(jnp.bfloat16)
            for ahead in range(1, groups):
                cin_copy(slot, ahead).start()
        weights_start()

    pl.when(pipe != 0)(weights_finish)

    @pl.when(pipe == last)
    def _():
        for slot in range(micro):
            pieces = []
            for wide in range(per_block):
                pieces.append(jnp.concatenate([
                    latbuf_wait_load(latbuf, lat_arrived, slot == 0, mine * per_block + wide,
                                     sharer * per_part + index, slot)
                    for index in range(per_part)
                ], axis=0))
            prev[slot] = jnp.concatenate(pieces, axis=1) if per_block > 1 else pieces[0]

    def hid_send_copy(step, slot, group):
        at_last = pipe == last
        to_step = step + jnp.where(at_last, 1, 0)
        return remote(outb.at[step, slot], hid.at[to_step, slot, mine],
                      hid_send.at[step, slot, group], hid_recv.at[to_step, slot, mine],
                      lax.rem(pipe + 1, n_pipe), group * sharers + sharer)

    def hid_arrived(step, slot, group):
        pltpu.make_async_copy(outb.at[step, slot], hid.at[step, slot, group],
                              hid_recv.at[step, slot, group]).wait()

    def kvx_copy(step, slot, ahead):
        other = lax.rem(sharer + ahead, sharers)
        return remote(kvx.at[step, slot, sharer], kvx.at[step, slot, sharer], kvx_send.at[step, slot, ahead],
                      kvx_recv.at[step, slot, sharer], pipe, mine * sharers + other)

    def att_copy(step, slot, ahead):
        group = lax.rem(mine + ahead, groups)
        return remote(att.at[step, slot, mine], att.at[step, slot, mine],
                      att_send.at[step, slot, ahead], att_recv.at[step, slot, mine],
                      pipe, group * sharers + sharer)

    def att_arrived(step, slot, ahead):
        group = lax.rem(mine + ahead, groups)
        pltpu.make_async_copy(att.at[step, slot, mine], att.at[step, slot, group],
                              att_recv.at[step, slot, group]).wait()

    def fin_targets(slot):
        for wide in range(per_block):
            for index in range(per_part):
                to_pipe, to_seq = mine * per_block + wide, sharer * per_part + index
                source = fin_src.at[slot, wide, pl.ds(index * rows, rows), :]
                yield to_pipe, to_seq, source, fin_send.at[slot, wide, index]

    def first_half(step, slot):
        tau = ts_ref[step, slot]
        from_latents = (pipe == 0) & (step == 0)

        @pl.when(from_latents)
        def _():
            modded[...] = first_mod[slot, pl.ds(pl.multiple_of(sharer * part, 16), part), :]
            total = csum[slot, mine].astype(jnp.float32)
            for ahead in range(1, groups):
                group = lax.rem(mine + ahead, groups)
                pltpu.make_async_copy(csum.at[slot, group], cin.at[slot, group],
                                      cin_recv.at[slot, group]).wait()
                total += cin[slot, group].astype(jnp.float32)
            pre[:, :block] = total[0]
            pre[:, block:] = total[1]

        @pl.when(jnp.logical_not(from_latents))
        def _():
            for group in range(groups):
                hid_arrived(step, slot, group)
            modded[...] = modulate(
                jnp.concatenate([hid[step, slot, group].astype(jnp.float32) for group in range(groups)], axis=1),
                tau,
            )
            pre[...] = jnp.dot(modded[...], wkv[...], preferred_element_type=jnp.float32)

        gain_query, gain_key = gain_ref[0, 0:1, :], gain_ref[0, 1:2, :]
        slices = [slice(head * head_dim, (head + 1) * head_dim) for head in range(heads)]
        for here in slices:
            kvx[step, slot, sharer, 0, :, here] = rms_rows(pre[:, here], gain_key)
        kvx[step, slot, sharer, 1] = pre[:, block:].astype(jnp.bfloat16)
        for ahead in range(1, sharers):
            kvx_copy(step, slot, ahead).start()
        projected = jnp.dot(modded[...], wq[...], preferred_element_type=jnp.float32)
        queries = [rms_rows(projected[:, here], gain_query) for here in slices]
        totals, weighted = [0.0] * heads, [0.0] * heads
        for ahead in range(sharers):
            owner = lax.rem(sharer + ahead, sharers)
            if ahead > 0:
                pltpu.make_async_copy(kvx.at[step, slot, sharer], kvx.at[step, slot, owner],
                                      kvx_recv.at[step, slot, owner]).wait()
            for head, here in enumerate(slices):
                logits = lax.dot_general(
                    queries[head], kvx[step, slot, owner, 0, :, here],
                    (((1,), (1,)), ((), ())), preferred_element_type=jnp.float32,
                ) * score_scale
                weights = jnp.exp(logits)
                totals[head] += jnp.sum(weights, axis=-1, keepdims=True)
                weighted[head] += jnp.dot(weights.astype(jnp.bfloat16), kvx[step, slot, owner, 1, :, here],
                                          preferred_element_type=jnp.float32)
        for head, here in enumerate(slices):
            att[step, slot, mine, :, here] = (weighted[head] / totals[head]).astype(jnp.bfloat16)
        for ahead in range(1, groups):
            att_copy(step, slot, ahead).start()

    def second_half(step, slot):
        tau = ts_ref[step, slot]
        gate_row = mod_ref[0, pl.ds(tau, 1), pl.ds(pl.multiple_of(2 * width + mine * block, 128), block)]
        residual = hid[step, slot, mine].astype(jnp.float32)
        projected = 0.0
        for ahead in range(groups):
            group = lax.rem(mine + ahead, groups)
            if ahead > 0:
                att_arrived(step, slot, ahead)
            attended = att[step, slot, group]
            rows_here = pl.ds(pl.multiple_of(group * block, 128), block)
            projected += jnp.dot(attended, wo[rows_here, :], preferred_element_type=jnp.float32)
        layer_out = (residual + gate_row * projected).astype(jnp.bfloat16)
        ends = (pipe == last) & (step == steps - 1)

        @pl.when(pipe != last)
        def _():
            outb[step, slot] = layer_out

        @pl.when(pipe == last)
        def _():
            update = (prev[slot] - ss_ref[tau] * layer_out.astype(jnp.float32)).astype(jnp.bfloat16)
            outb[step, slot] = update
            prev[slot] = update.astype(jnp.float32)

        @pl.when(jnp.logical_not(ends))
        def _():
            for ahead in range(groups):
                hid_send_copy(step, slot, lax.rem(mine + ahead, groups)).start()

        @pl.when(ends)
        def _():
            update = prev[slot]
            for wide in range(per_block):
                fin_src[slot, wide] = update[:, wide * share:(wide + 1) * share]
            for to_pipe, to_seq, source, send in fin_targets(slot):
                own = (to_pipe == pipe) & (to_seq == seq)

                @pl.when(own)
                def _():
                    pltpu.make_async_copy(source, fin.at[slot], fin_recv.at[slot]).start()

                @pl.when(jnp.logical_not(own))
                def _():
                    remote(source, fin.at[slot], send, fin_recv.at[slot], to_pipe, to_seq).start()

    def visit(step, carry):
        @pl.when((pipe == 0) & (step == 1))
        def _():
            weights_finish()

        for slot in range(micro):
            first_half(step, slot)
            second_half(step, slot)
        return carry

    lax.fori_loop(0, steps, visit, 0)

    for slot in range(micro):
        pltpu.make_async_copy(fin_src.at[slot, 0, pl.ds(0, rows), :], fin.at[slot],
                              fin_recv.at[slot]).wait()
        out_ref[slot] = fin[slot].astype(jnp.bfloat16)

    for ahead in range(n_seq):
        target = lax.rem(seq + ahead, n_seq)
        if ahead == 0:
            @pl.when(pipe != 0)
            def _():
                lat_copy(0, target, ahead).wait_send()
        else:
            lat_copy(0, target, ahead).wait_send()

    @pl.when(jnp.logical_not(keeps_own))
    def _():
        lat_copy(last, keeper, n_seq).wait_send()

    @pl.when(pipe == 0)
    def _():
        for slot in range(micro):
            for ahead in range(1, sharers):
                pin_copy(slot, ahead).wait_send()
            for ahead in range(1, groups):
                cin_copy(slot, ahead).wait_send()

    for ahead in range(1, groups):
        kv_copy(ahead).wait_send()
    for ahead in range(groups):
        for step in range(1, sharers):
            kv_pass(ahead, step).wait_send()

    def drain(item, carry):
        step, slot = item // micro, item % micro
        ends = (pipe == last) & (step == steps - 1)
        for ahead in range(1, groups):
            att_copy(step, slot, ahead).wait_send()
        for ahead in range(1, sharers):
            kvx_copy(step, slot, ahead).wait_send()

        @pl.when(jnp.logical_not(ends))
        def _():
            for group in range(groups):
                hid_send_copy(step, slot, group).wait_send()

        @pl.when(ends)
        def _():
            for to_pipe, to_seq, source, send in fin_targets(slot):
                @pl.when(jnp.logical_not((to_pipe == pipe) & (to_seq == seq)))
                def _():
                    remote(source, fin.at[slot], send, fin_recv.at[slot], to_pipe, to_seq).wait_send()
        return carry

    lax.fori_loop(0, micro * steps, drain, 0)


def latbuf_wait_load(latbuf, lat_arrived, first, from_pipe, from_seq, slot):
    if first:
        lat_arrived(from_pipe, from_seq)
    return latbuf[from_pipe, from_seq, slot].astype(jnp.float32)


def shards(latents, timesteps, step_sizes, mod_table, qk_gain, w_query, w_kv, w_out):
    n_pipe, n_seq = lax.axis_size("pipe"), lax.axis_size("seq")
    micro, rows, share = latents.shape
    steps = timesteps.shape[0]
    head_dim = qk_gain.shape[2]
    width, inner = w_query.shape[1], w_query.shape[2]
    heads = inner // head_dim
    groups = math.gcd(math.gcd(heads, n_seq), n_pipe)
    while n_seq // groups < 2:
        groups //= 2
    sharers = n_seq // groups
    block = inner // groups
    part = rows * n_seq // sharers
    per_block, per_part = n_pipe // groups, n_seq // sharers
    bf16, f32 = jnp.bfloat16, jnp.float32
    vmem = pl.BlockSpec(memory_space=pltpu.VMEM)
    hbm = pl.BlockSpec(memory_space=pl.ANY)
    dma = pltpu.SemaphoreType.DMA
    return pl.pallas_call(
        functools.partial(kernel, n_pipe, n_seq, groups, micro, steps, head_dim),
        out_shape=jax.ShapeDtypeStruct(latents.shape, bf16),
        in_specs=[hbm] * 8,
        out_specs=vmem,
        scratch_shapes=[
            pltpu.SMEM(timesteps.shape, timesteps.dtype),
            pltpu.SMEM(step_sizes.shape, f32),
            pltpu.VMEM(mod_table.shape, f32),
            pltpu.VMEM(qk_gain.shape, f32),
            pltpu.VMEM((width, block), bf16),
            pltpu.VMEM((width, 2 * block), bf16),
            pltpu.VMEM((inner, block), bf16),
            pltpu.VMEM((groups, w_kv.shape[1], 2 * block), bf16),
            pltpu.VMEM((n_pipe, n_seq, micro, rows, share), bf16),
            pltpu.VMEM((steps, micro, groups, part, block), bf16),
            pltpu.VMEM((steps, micro, groups, part, block), bf16),
            pltpu.VMEM((steps, micro, part, block), bf16),
            pltpu.VMEM((micro, part, block), f32),
            pltpu.VMEM((part, width), bf16),
            pltpu.VMEM((rows * n_seq, width), bf16),
            pltpu.VMEM((micro, rows * n_seq, width), bf16),
            pltpu.VMEM((n_seq, rows * n_seq, w_kv.shape[1]), bf16),
            pltpu.VMEM((micro, sharers, groups, 2, part, block), bf16),
            pltpu.VMEM((micro, sharers, groups, 2, part, block), bf16),
            pltpu.VMEM((micro, groups, 2, part, block), bf16),
            pltpu.VMEM((micro, groups, 2, part, block), bf16),
            pltpu.VMEM((part, 2 * block), f32),
            pltpu.VMEM((steps, micro, sharers, 2, part, block), bf16),
            pltpu.VMEM((micro, per_block, part, share), f32),
            pltpu.VMEM((micro, rows, share), f32),
            dma((6,)),
            dma((2, groups)),
            dma((n_seq,)),
            dma((groups,)),
            dma((groups, sharers)),
            dma((n_seq + 1,)),
            dma((n_pipe, n_seq)),
            dma((micro, sharers)),
            dma((micro, sharers)),
            dma((micro, groups)),
            dma((micro, groups)),
            dma((steps, micro, groups)),
            dma((steps, micro, groups)),
            dma((steps, micro, sharers)),
            dma((steps, micro, sharers)),
            dma((steps, micro, groups)),
            dma((steps, micro, groups)),
            dma((micro, per_block, per_part)),
            dma((micro,)),
        ],
        compiler_params=pltpu.CompilerParams(
            has_side_effects=True, vmem_limit_bytes=64 * 1024 * 1024
        ),
        cost_estimate=pl.CostEstimate(
            flops=2 * 4 * rows * n_seq * width * block * micro * steps,
            bytes_accessed=2 * 4 * width * block, transcendentals=0,
        ),
        name="denoise",
    )(latents, timesteps, step_sizes, mod_table, qk_gain, w_query, w_kv, w_out)


def solution(mesh):
    in_specs = (
        P(None, "seq", "pipe"),
        P(),
        P(),
        P("pipe", None, None),
        P("pipe", None, None),
        P("pipe", None, None),
        P("pipe", "seq", None),
        P("pipe", None, None),
    )
    out_specs = P(None, "seq", "pipe")
    return jax.shard_map(shards, mesh=mesh, in_specs=in_specs, out_specs=out_specs, check_vma=False)
```

```python
import functools
import math

import jax
import jax.numpy as jnp
from jax import lax
from jax.experimental import pallas as pl
from jax.experimental.pallas import tpu as pltpu
from jax.sharding import PartitionSpec as P

norm_eps = 1e-06
MESH = pl.DeviceIdType.MESH


def rms_rows(values, gain_row):
    mean_square = jnp.mean(values * values, axis=-1, keepdims=True)
    return (values * lax.rsqrt(mean_square + norm_eps) * gain_row).astype(jnp.bfloat16)


def kernel(
    n_pipe, n_seq, groups, micro, steps, head_dim,
    lat_ref, ts_hbm, ss_hbm, mod_hbm, gain_hbm, wq_hbm, wkv_hbm, wo_hbm,
    out_ref,
    ts_ref, ss_ref, mod_ref, gain_ref, wq, wkv, wo, stage, relay, latbuf, hid, att, outb, prev, modded,
    first_x, first_mod, slabs, pbuf, pin, csum, cin, pre, kvx, fin_src, fin,
    local_sem, stage_sem, kv_recv, kv_send, kv_fwd, relay_send, relay_recv, lat_send, lat_recv, pin_send, pin_recv, cin_send, cin_recv,
    hid_recv, hid_send, kvx_send, kvx_recv, att_recv, att_send, fin_send, fin_recv,
):
    sharers = n_seq // groups
    rows, share = lat_ref.shape[1], lat_ref.shape[2]
    tokens = rows * n_seq
    width = share * n_pipe
    block = wq.shape[1]
    inner = block * groups
    depth = wkv_hbm.shape[1]
    part = tokens // sharers
    per_block = n_pipe // groups
    per_part = n_seq // sharers
    heads = block // head_dim
    score_scale = 1.0 / math.sqrt(head_dim)
    last = n_pipe - 1

    pipe, seq = lax.axis_index("pipe"), lax.axis_index("seq")
    mine, sharer = seq // sharers, seq % sharers

    def remote(src, dst, send, recv, to_pipe, to_seq):
        return pltpu.make_async_remote_copy(
            src_ref=src, dst_ref=dst, send_sem=send, recv_sem=recv,
            device_id=(to_pipe, to_seq), device_id_type=MESH,
        )

    def lat_copy(to_pipe, to_seq, index):
        return remote(lat_ref, latbuf.at[pipe, seq], lat_send.at[index],
                      lat_recv.at[pipe, seq], to_pipe, to_seq)

    def lat_local():
        return pltpu.make_async_copy(lat_ref, latbuf.at[pipe, seq], lat_recv.at[pipe, seq])

    def lat_arrived(from_pipe, from_seq):
        pltpu.make_async_copy(lat_ref, latbuf.at[from_pipe, from_seq],
                              lat_recv.at[from_pipe, from_seq]).wait()

    keeper = (pipe // per_block) * sharers + seq // per_part
    for ahead in range(n_seq):
        target = lax.rem(seq + ahead, n_seq)
        if ahead == 0:
            @pl.when(pipe == 0)
            def _():
                lat_local().start()

            @pl.when(pipe != 0)
            def _():
                lat_copy(0, target, ahead).start()
        else:
            lat_copy(0, target, ahead).start()
    keeps_own = (pipe == last) & (keeper == seq)

    @pl.when(keeps_own)
    def _():
        lat_local().start()

    @pl.when(jnp.logical_not(keeps_own))
    def _():
        lat_copy(last, keeper, n_seq).start()


    def slab(owner):
        return wkv.at[pl.ds(pl.multiple_of(owner * depth, 16), depth), :]

    pairs = [(i, j) for i in range(groups) for j in range(groups) if i != j]
    relayed = {pair: at for at, pair in enumerate(pair for pair in pairs if abs(pair[0] - pair[1]) > 1)}

    def hop(i, j, k):
        beyond = k + (1 if j > k else -1)
        owner = i * sharers + sharer
        source, send = (stage.at[j], kv_send.at[j]) if k == i else (
            relay.at[relayed[i, j]], relay_send.at[relayed[i, j]])
        target, recv = (slab(owner), kv_recv.at[owner]) if beyond == j else (
            relay.at[relayed[i, j]], relay_recv.at[relayed[i, j]])
        return remote(source, target, send, recv, pipe, beyond * sharers + sharer)

    def passing(k):
        return sorted((pair for pair in relayed if min(pair) < k < max(pair)), key=lambda pair: abs(pair[0] - k))

    def kv_pass(group, step, source):
        owner = group * sharers + sharer
        return remote(source, slab(owner), kv_fwd.at[group, step],
                      kv_recv.at[owner], pipe, mine * sharers + lax.rem(sharer + step, sharers))

    def kv_arrived(owner):
        pltpu.make_async_copy(stage.at[mine], slab(owner), kv_recv.at[owner]).wait()

    def weights_start():
        for k in range(groups):
            @pl.when(mine == k)
            def _():
                for j in sorted(range(groups), key=lambda j: -abs(j - k)):
                    if j != k:
                        hop(k, j, k).start()
        pltpu.make_async_copy(stage.at[mine], slab(seq), kv_recv.at[seq]).start()
        for step in range(1, sharers):
            kv_pass(mine, step, stage.at[mine]).start()

    def weights_finish():
        for k in range(groups):
            @pl.when(mine == k)
            def _():
                events = [(abs(i - k), 0, i, j) for i, j in passing(k)]
                events += [(abs(i - k), 1, i, k) for i in range(groups) if i != k]
                for _, kind, i, j in sorted(events):
                    if kind == 0:
                        at = relayed[i, j]
                        pltpu.make_async_copy(stage.at[0], relay.at[at], relay_recv.at[at]).wait()
                        hop(i, j, k).start()
                    else:
                        kv_arrived(i * sharers + sharer)
                        for step in range(1, sharers):
                            kv_pass(i, step, slab(i * sharers + sharer)).start()
        kv_arrived(seq)
        for step in range(1, sharers):
            for group in range(groups):
                kv_arrived(group * sharers + lax.rem(sharer + step, sharers))

    staging = [
        pltpu.make_async_copy(
            wkv_hbm.at[0, :, kv * inner + group * block:kv * inner + (group + 1) * block],
            stage.at[group, :, kv * block:(kv + 1) * block], stage_sem.at[kv, group],
        )
        for group in range(groups) for kv in range(2)
    ]
    for copy in staging:
        copy.start()
    own_columns = pl.ds(pl.multiple_of(mine * block, 128), block)
    copy_q = pltpu.make_async_copy(wq_hbm.at[0, :, own_columns], wq, local_sem.at[0])
    copy_o = pltpu.make_async_copy(wo_hbm.at[0, :, own_columns], wo, local_sem.at[1])
    for copy in staging:
        copy.wait()
    pl.when(pipe != 0)(weights_start)
    locals_in = [
        copy_q, copy_o,
        pltpu.make_async_copy(ts_hbm, ts_ref, local_sem.at[2]),
        pltpu.make_async_copy(ss_hbm, ss_ref, local_sem.at[3]),
        pltpu.make_async_copy(mod_hbm, mod_ref, local_sem.at[4]),
        pltpu.make_async_copy(gain_hbm, gain_ref, local_sem.at[5]),
    ]
    for copy in locals_in:
        copy.start()
    for copy in locals_in:
        copy.wait()

    def modulate(as_float, tau):
        center = jnp.mean(as_float, axis=-1, keepdims=True)
        away = as_float - center
        spread = jnp.mean(away * away, axis=-1, keepdims=True)
        shift_row = mod_ref[0, pl.ds(tau, 1), 0:width]
        scale_row = mod_ref[0, pl.ds(tau, 1), width:2 * width]
        return (
            away * lax.rsqrt(spread + norm_eps) * (1.0 + scale_row) + shift_row
        ).astype(jnp.bfloat16)

    def pin_copy(slot, ahead):
        other = lax.rem(sharer + ahead, sharers)
        return remote(pbuf.at[slot, other], pin.at[slot, sharer], pin_send.at[slot, ahead],
                      pin_recv.at[slot, sharer], pipe, mine * sharers + other)

    def cin_copy(slot, ahead):
        group = lax.rem(mine + ahead, groups)
        return remote(csum.at[slot, group], cin.at[slot, mine], cin_send.at[slot, ahead],
                      cin_recv.at[slot, mine], pipe, group * sharers + sharer)

    @pl.when(pipe == 0)
    def _():
        for from_pipe in range(n_pipe):
            for from_seq in range(n_seq):
                lat_arrived(from_pipe, from_seq)
        for slot in range(micro):
            pieces = []
            for from_pipe in range(n_pipe):
                pieces.append(jnp.concatenate([
                    latbuf[from_pipe, index, slot].astype(jnp.float32) for index in range(n_seq)
                ], axis=0))
            whole = jnp.concatenate(pieces, axis=1)
            first_x[...] = whole.astype(jnp.bfloat16)
            mine_rows = pl.ds(pl.multiple_of(sharer * part, 16), part)
            for group in range(groups):
                hid[0, slot, group] = first_x[mine_rows, group * block:(group + 1) * block]
            whole_mod = modulate(whole, ts_ref[0, slot])
            first_mod[slot] = whole_mod
            for index in range(n_seq):
                slabs[index] = whole_mod[:, index * depth:(index + 1) * depth]
            feature_rows = slabs[seq]
            for group in range(groups):
                partial = jnp.dot(feature_rows, stage[group],
                                  preferred_element_type=jnp.float32).astype(jnp.bfloat16)
                for at in range(sharers):
                    for kv in range(2):
                        pbuf[slot, at, group, kv] = partial[at * part:(at + 1) * part,
                                                            kv * block:(kv + 1) * block]
            for ahead in range(1, sharers):
                pin_copy(slot, ahead).start()
        for slot in range(micro):
            for ahead in range(1, sharers):
                other = lax.rem(sharer + ahead, sharers)
                pltpu.make_async_copy(pbuf.at[slot, other], pin.at[slot, other],
                                      pin_recv.at[slot, other]).wait()
            total = pbuf[slot, sharer].astype(jnp.float32)
            for ahead in range(1, sharers):
                total += pin[slot, lax.rem(sharer + ahead, sharers)].astype(jnp.float32)
            csum[slot] = total.astype(jnp.bfloat16)
            for ahead in range(1, groups):
                cin_copy(slot, ahead).start()

    pl.when(pipe != 0)(weights_finish)

    @pl.when(pipe == last)
    def _():
        for slot in range(micro):
            pieces = []
            for wide in range(per_block):
                pieces.append(jnp.concatenate([
                    latbuf_wait_load(latbuf, lat_arrived, slot == 0, mine * per_block + wide,
                                     sharer * per_part + index, slot)
                    for index in range(per_part)
                ], axis=0))
            prev[slot] = jnp.concatenate(pieces, axis=1) if per_block > 1 else pieces[0]

    def hid_send_copy(step, slot, group):
        at_last = pipe == last
        to_step = step + jnp.where(at_last, 1, 0)
        return remote(outb.at[step, slot], hid.at[to_step, slot, mine],
                      hid_send.at[step, slot, group], hid_recv.at[to_step, slot, mine],
                      lax.rem(pipe + 1, n_pipe), group * sharers + sharer)

    def hid_arrived(step, slot, group):
        pltpu.make_async_copy(outb.at[step, slot], hid.at[step, slot, group],
                              hid_recv.at[step, slot, group]).wait()

    def kvx_copy(step, slot, ahead):
        other = lax.rem(sharer + ahead, sharers)
        return remote(kvx.at[step, slot, sharer], kvx.at[step, slot, sharer], kvx_send.at[step, slot, ahead],
                      kvx_recv.at[step, slot, sharer], pipe, mine * sharers + other)

    def att_copy(step, slot, ahead):
        group = lax.rem(mine + ahead, groups)
        return remote(att.at[step, slot, mine], att.at[step, slot, mine],
                      att_send.at[step, slot, ahead], att_recv.at[step, slot, mine],
                      pipe, group * sharers + sharer)

    def att_arrived(step, slot, ahead):
        group = lax.rem(mine + ahead, groups)
        pltpu.make_async_copy(att.at[step, slot, mine], att.at[step, slot, group],
                              att_recv.at[step, slot, group]).wait()

    def fin_targets(slot):
        for wide in range(per_block):
            for index in range(per_part):
                to_pipe, to_seq = mine * per_block + wide, sharer * per_part + index
                source = fin_src.at[slot, wide, pl.ds(index * rows, rows), :]
                yield to_pipe, to_seq, source, fin_send.at[slot, wide, index]

    def first_half(step, slot):
        tau = ts_ref[step, slot]
        from_latents = (pipe == 0) & (step == 0)

        @pl.when(from_latents)
        def _():
            modded[...] = first_mod[slot, pl.ds(pl.multiple_of(sharer * part, 16), part), :]
            total = csum[slot, mine].astype(jnp.float32)
            for ahead in range(1, groups):
                group = lax.rem(mine + ahead, groups)
                pltpu.make_async_copy(csum.at[slot, group], cin.at[slot, group],
                                      cin_recv.at[slot, group]).wait()
                total += cin[slot, group].astype(jnp.float32)
            pre[:, :block] = total[0]
            pre[:, block:] = total[1]

        @pl.when(jnp.logical_not(from_latents))
        def _():
            for group in range(groups):
                hid_arrived(step, slot, group)
            modded[...] = modulate(
                jnp.concatenate([hid[step, slot, group].astype(jnp.float32) for group in range(groups)], axis=1),
                tau,
            )
            pre[...] = jnp.dot(modded[...], wkv[...], preferred_element_type=jnp.float32)

        gain_query, gain_key = gain_ref[0, 0:1, :], gain_ref[0, 1:2, :]
        slices = [slice(head * head_dim, (head + 1) * head_dim) for head in range(heads)]
        for here in slices:
            kvx[step, slot, sharer, 0, :, here] = rms_rows(pre[:, here], gain_key)
        kvx[step, slot, sharer, 1] = pre[:, block:].astype(jnp.bfloat16)
        for ahead in range(1, sharers):
            kvx_copy(step, slot, ahead).start()
        projected = jnp.dot(modded[...], wq[...], preferred_element_type=jnp.float32)
        queries = [rms_rows(projected[:, here], gain_query) for here in slices]
        totals, weighted = [0.0] * heads, [0.0] * heads
        for ahead in range(sharers):
            owner = lax.rem(sharer + ahead, sharers)
            if ahead > 0:
                pltpu.make_async_copy(kvx.at[step, slot, sharer], kvx.at[step, slot, owner],
                                      kvx_recv.at[step, slot, owner]).wait()
            for head, here in enumerate(slices):
                logits = lax.dot_general(
                    queries[head], kvx[step, slot, owner, 0, :, here],
                    (((1,), (1,)), ((), ())), preferred_element_type=jnp.float32,
                ) * score_scale
                weights = jnp.exp(logits)
                totals[head] += jnp.sum(weights, axis=-1, keepdims=True)
                weighted[head] += jnp.dot(weights.astype(jnp.bfloat16), kvx[step, slot, owner, 1, :, here],
                                          preferred_element_type=jnp.float32)
        for head, here in enumerate(slices):
            att[step, slot, mine, :, here] = (weighted[head] / totals[head]).astype(jnp.bfloat16)
        for ahead in range(1, groups):
            att_copy(step, slot, ahead).start()

    def second_half(step, slot):
        tau = ts_ref[step, slot]
        gate_row = mod_ref[0, pl.ds(tau, 1), pl.ds(pl.multiple_of(2 * width + mine * block, 128), block)]
        residual = hid[step, slot, mine].astype(jnp.float32)
        projected = 0.0
        for ahead in range(groups):
            group = lax.rem(mine + ahead, groups)
            if ahead > 0:
                att_arrived(step, slot, ahead)
            attended = att[step, slot, group]
            rows_here = pl.ds(pl.multiple_of(group * block, 128), block)
            projected += jnp.dot(attended, wo[rows_here, :], preferred_element_type=jnp.float32)
        layer_out = (residual + gate_row * projected).astype(jnp.bfloat16)
        ends = (pipe == last) & (step == steps - 1)

        @pl.when(pipe != last)
        def _():
            outb[step, slot] = layer_out

        @pl.when(pipe == last)
        def _():
            update = (prev[slot] - ss_ref[tau] * layer_out.astype(jnp.float32)).astype(jnp.bfloat16)
            outb[step, slot] = update
            prev[slot] = update.astype(jnp.float32)

        @pl.when(jnp.logical_not(ends))
        def _():
            for ahead in range(groups):
                hid_send_copy(step, slot, lax.rem(mine + ahead, groups)).start()

        @pl.when(ends)
        def _():
            update = prev[slot]
            for wide in range(per_block):
                fin_src[slot, wide] = update[:, wide * share:(wide + 1) * share]
            for to_pipe, to_seq, source, send in fin_targets(slot):
                own = (to_pipe == pipe) & (to_seq == seq)

                @pl.when(own)
                def _():
                    pltpu.make_async_copy(source, fin.at[slot], fin_recv.at[slot]).start()

                @pl.when(jnp.logical_not(own))
                def _():
                    remote(source, fin.at[slot], send, fin_recv.at[slot], to_pipe, to_seq).start()

    def visit(step, carry):
        @pl.when((pipe == 0) & (step == 1))
        def _():
            weights_start()
            weights_finish()

        for slot in range(micro):
            first_half(step, slot)
            second_half(step, slot)
        return carry

    lax.fori_loop(0, steps, visit, 0)

    for slot in range(micro):
        pltpu.make_async_copy(fin_src.at[slot, 0, pl.ds(0, rows), :], fin.at[slot],
                              fin_recv.at[slot]).wait()
        out_ref[slot] = fin[slot].astype(jnp.bfloat16)

    for ahead in range(n_seq):
        target = lax.rem(seq + ahead, n_seq)
        if ahead == 0:
            @pl.when(pipe != 0)
            def _():
                lat_copy(0, target, ahead).wait_send()
        else:
            lat_copy(0, target, ahead).wait_send()

    @pl.when(jnp.logical_not(keeps_own))
    def _():
        lat_copy(last, keeper, n_seq).wait_send()

    @pl.when(pipe == 0)
    def _():
        for slot in range(micro):
            for ahead in range(1, sharers):
                pin_copy(slot, ahead).wait_send()
            for ahead in range(1, groups):
                cin_copy(slot, ahead).wait_send()

    for k in range(groups):
        @pl.when(mine == k)
        def _():
            for j in range(groups):
                if j != k:
                    hop(k, j, k).wait_send()
            for i, j in passing(k):
                hop(i, j, k).wait_send()
    for group in range(groups):
        for step in range(1, sharers):
            kv_pass(group, step, stage.at[group]).wait_send()

    def drain(item, carry):
        step, slot = item // micro, item % micro
        ends = (pipe == last) & (step == steps - 1)
        for ahead in range(1, groups):
            att_copy(step, slot, ahead).wait_send()
        for ahead in range(1, sharers):
            kvx_copy(step, slot, ahead).wait_send()

        @pl.when(jnp.logical_not(ends))
        def _():
            for group in range(groups):
                hid_send_copy(step, slot, group).wait_send()

        @pl.when(ends)
        def _():
            for to_pipe, to_seq, source, send in fin_targets(slot):
                @pl.when(jnp.logical_not((to_pipe == pipe) & (to_seq == seq)))
                def _():
                    remote(source, fin.at[slot], send, fin_recv.at[slot], to_pipe, to_seq).wait_send()
        return carry

    lax.fori_loop(0, micro * steps, drain, 0)


def latbuf_wait_load(latbuf, lat_arrived, first, from_pipe, from_seq, slot):
    if first:
        lat_arrived(from_pipe, from_seq)
    return latbuf[from_pipe, from_seq, slot].astype(jnp.float32)


def shards(latents, timesteps, step_sizes, mod_table, qk_gain, w_query, w_kv, w_out):
    n_pipe, n_seq = lax.axis_size("pipe"), lax.axis_size("seq")
    micro, rows, share = latents.shape
    steps = timesteps.shape[0]
    head_dim = qk_gain.shape[2]
    width, inner = w_query.shape[1], w_query.shape[2]
    heads = inner // head_dim
    groups = math.gcd(math.gcd(heads, n_seq), n_pipe)
    while n_seq // groups < 2:
        groups //= 2
    sharers = n_seq // groups
    block = inner // groups
    part = rows * n_seq // sharers
    per_block, per_part = n_pipe // groups, n_seq // sharers
    bf16, f32 = jnp.bfloat16, jnp.float32
    vmem = pl.BlockSpec(memory_space=pltpu.VMEM)
    hbm = pl.BlockSpec(memory_space=pl.ANY)
    dma = pltpu.SemaphoreType.DMA
    return pl.pallas_call(
        functools.partial(kernel, n_pipe, n_seq, groups, micro, steps, head_dim),
        out_shape=jax.ShapeDtypeStruct(latents.shape, bf16),
        in_specs=[hbm] * 8,
        out_specs=vmem,
        scratch_shapes=[
            pltpu.SMEM(timesteps.shape, timesteps.dtype),
            pltpu.SMEM(step_sizes.shape, f32),
            pltpu.VMEM(mod_table.shape, f32),
            pltpu.VMEM(qk_gain.shape, f32),
            pltpu.VMEM((width, block), bf16),
            pltpu.VMEM((width, 2 * block), bf16),
            pltpu.VMEM((inner, block), bf16),
            pltpu.VMEM((groups, w_kv.shape[1], 2 * block), bf16),
            pltpu.VMEM((max(1, (groups - 1) * (groups - 2)), w_kv.shape[1], 2 * block), bf16),
            pltpu.VMEM((n_pipe, n_seq, micro, rows, share), bf16),
            pltpu.VMEM((steps, micro, groups, part, block), bf16),
            pltpu.VMEM((steps, micro, groups, part, block), bf16),
            pltpu.VMEM((steps, micro, part, block), bf16),
            pltpu.VMEM((micro, part, block), f32),
            pltpu.VMEM((part, width), bf16),
            pltpu.VMEM((rows * n_seq, width), bf16),
            pltpu.VMEM((micro, rows * n_seq, width), bf16),
            pltpu.VMEM((n_seq, rows * n_seq, w_kv.shape[1]), bf16),
            pltpu.VMEM((micro, sharers, groups, 2, part, block), bf16),
            pltpu.VMEM((micro, sharers, groups, 2, part, block), bf16),
            pltpu.VMEM((micro, groups, 2, part, block), bf16),
            pltpu.VMEM((micro, groups, 2, part, block), bf16),
            pltpu.VMEM((part, 2 * block), f32),
            pltpu.VMEM((steps, micro, sharers, 2, part, block), bf16),
            pltpu.VMEM((micro, per_block, part, share), f32),
            pltpu.VMEM((micro, rows, share), f32),
            dma((6,)),
            dma((2, groups)),
            dma((n_seq,)),
            dma((groups,)),
            dma((groups, sharers)),
            dma((max(1, (groups - 1) * (groups - 2)),)),
            dma((max(1, (groups - 1) * (groups - 2)),)),
            dma((n_seq + 1,)),
            dma((n_pipe, n_seq)),
            dma((micro, sharers)),
            dma((micro, sharers)),
            dma((micro, groups)),
            dma((micro, groups)),
            dma((steps, micro, groups)),
            dma((steps, micro, groups)),
            dma((steps, micro, sharers)),
            dma((steps, micro, sharers)),
            dma((steps, micro, groups)),
            dma((steps, micro, groups)),
            dma((micro, per_block, per_part)),
            dma((micro,)),
        ],
        compiler_params=pltpu.CompilerParams(
            has_side_effects=True, vmem_limit_bytes=64 * 1024 * 1024
        ),
        cost_estimate=pl.CostEstimate(
            flops=2 * 4 * rows * n_seq * width * block * micro * steps,
            bytes_accessed=2 * 4 * width * block, transcendentals=0,
        ),
        name="denoise",
    )(latents, timesteps, step_sizes, mod_table, qk_gain, w_query, w_kv, w_out)


def solution(mesh):
    in_specs = (
        P(None, "seq", "pipe"),
        P(),
        P(),
        P("pipe", None, None),
        P("pipe", None, None),
        P("pipe", None, None),
        P("pipe", "seq", None),
        P("pipe", None, None),
    )
    out_specs = P(None, "seq", "pipe")
    return jax.shard_map(shards, mesh=mesh, in_specs=in_specs, out_specs=out_specs, check_vma=False)
```

```python
import functools
import math

import jax
import jax.numpy as jnp
from jax import lax
from jax.experimental import pallas as pl
from jax.experimental.pallas import tpu as pltpu
from jax.sharding import PartitionSpec as P

norm_eps = 1e-06
MESH = pl.DeviceIdType.MESH


def rms_rows(values, gain_row):
    mean_square = jnp.mean(values * values, axis=-1, keepdims=True)
    return (values * lax.rsqrt(mean_square + norm_eps) * gain_row).astype(jnp.bfloat16)


def kernel(
    n_pipe, n_seq, groups, micro, steps, head_dim,
    lat_ref, ts_hbm, ss_hbm, mod_hbm, gain_hbm, wq_hbm, wkv_hbm, wo_hbm,
    out_ref,
    ts_ref, ss_ref, mod_ref, gain_ref, wq, wkv, wo, wrows, latbuf, hid, att, outb, prev, modded,
    first_x, first_mod, slabs, pbuf, pin, csum, cin, pre, qbuf, kvx, fin_src, fin,
    local_sem, kv_recv, kv_send, kv_fwd, lat_send, lat_recv, pin_send, pin_recv, cin_send, cin_recv,
    hid_recv, hid_send, kvx_send, kvx_recv, att_recv, att_send, fin_send, fin_recv,
):
    sharers = n_seq // groups
    rows, share = lat_ref.shape[1], lat_ref.shape[2]
    tokens = rows * n_seq
    width = share * n_pipe
    block = wq.shape[1]
    inner = block * groups
    depth = wkv_hbm.shape[1]
    part = tokens // sharers
    per_block = n_pipe // groups
    per_part = n_seq // sharers
    heads = block // head_dim
    score_scale = 1.0 / math.sqrt(head_dim)
    last = n_pipe - 1

    pipe, seq = lax.axis_index("pipe"), lax.axis_index("seq")
    mine, sharer = seq // sharers, seq % sharers

    def remote(src, dst, send, recv, to_pipe, to_seq):
        return pltpu.make_async_remote_copy(
            src_ref=src, dst_ref=dst, send_sem=send, recv_sem=recv,
            device_id=(to_pipe, to_seq), device_id_type=MESH,
        )

    def lat_copy(to_pipe, to_seq, index):
        return remote(lat_ref, latbuf.at[pipe, seq], lat_send.at[index],
                      lat_recv.at[pipe, seq], to_pipe, to_seq)

    def lat_local():
        return pltpu.make_async_copy(lat_ref, latbuf.at[pipe, seq], lat_recv.at[pipe, seq])

    def lat_arrived(from_pipe, from_seq):
        pltpu.make_async_copy(lat_ref, latbuf.at[from_pipe, from_seq],
                              lat_recv.at[from_pipe, from_seq]).wait()

    keeper = (pipe // per_block) * sharers + seq // per_part
    for ahead in range(n_seq):
        target = lax.rem(seq + ahead, n_seq)
        if ahead == 0:
            @pl.when(pipe == 0)
            def _():
                lat_local().start()

            @pl.when(pipe != 0)
            def _():
                lat_copy(0, target, ahead).start()
        else:
            lat_copy(0, target, ahead).start()
    keeps_own = (pipe == last) & (keeper == seq)

    @pl.when(keeps_own)
    def _():
        lat_local().start()

    @pl.when(jnp.logical_not(keeps_own))
    def _():
        lat_copy(last, keeper, n_seq).start()


    def columns(kv, group):
        start = pl.multiple_of(kv * inner + group * block, 128)
        return wrows.at[:, pl.ds(start, block)]

    def slab(kv, owner):
        return wkv.at[pl.ds(pl.multiple_of(owner * depth, 16), depth), kv * block:(kv + 1) * block]

    def kv_copy(kv, ahead):
        group = lax.rem(mine + ahead, groups)
        return remote(columns(kv, group), slab(kv, seq), kv_send.at[kv, ahead],
                      kv_recv.at[kv, seq], pipe, group * sharers + sharer)

    def kv_pass(kv, ahead, step):
        group = lax.rem(mine + ahead, groups)
        owner = group * sharers + sharer
        source = columns(kv, mine) if ahead == 0 else slab(kv, owner)
        return remote(source, slab(kv, owner), kv_fwd.at[kv, ahead, step],
                      kv_recv.at[kv, owner], pipe, mine * sharers + lax.rem(sharer + step, sharers))

    def kv_arrived(kv, owner):
        pltpu.make_async_copy(columns(kv, mine), slab(kv, owner), kv_recv.at[kv, owner]).wait()

    rows_in = pltpu.make_async_copy(wkv_hbm.at[0], wrows, local_sem.at[6])
    rows_in.start()
    own_columns = pl.ds(pl.multiple_of(mine * block, 128), block)
    copy_q = pltpu.make_async_copy(wq_hbm.at[0, :, own_columns], wq, local_sem.at[0])
    copy_o = pltpu.make_async_copy(wo_hbm.at[0, :, own_columns], wo, local_sem.at[1])
    def weights_start():
        for kv in range(2):
            for ahead in range(groups - 1, 0, -1):
                kv_copy(kv, ahead).start()
        for kv in range(2):
            pltpu.make_async_copy(columns(kv, mine), slab(kv, seq), kv_recv.at[kv, seq]).start()
            for step in range(1, sharers):
                kv_pass(kv, 0, step).start()

    def weights_finish():
        for kv in range(2):
            for ahead in range(1, groups):
                kv_arrived(kv, lax.rem(mine + ahead, groups) * sharers + sharer)
                for step in range(1, sharers):
                    kv_pass(kv, ahead, step).start()
        for kv in range(2):
            kv_arrived(kv, seq)
            for step in range(1, sharers):
                for group in range(groups):
                    kv_arrived(kv, group * sharers + lax.rem(sharer + step, sharers))

    rows_in.wait()
    pl.when(pipe != 0)(weights_start)
    locals_in = [
        copy_q, copy_o,
        pltpu.make_async_copy(ts_hbm, ts_ref, local_sem.at[2]),
        pltpu.make_async_copy(ss_hbm, ss_ref, local_sem.at[3]),
        pltpu.make_async_copy(mod_hbm, mod_ref, local_sem.at[4]),
        pltpu.make_async_copy(gain_hbm, gain_ref, local_sem.at[5]),
    ]
    for copy in locals_in:
        copy.start()
    for copy in locals_in:
        copy.wait()

    def modulate(as_float, tau):
        center = jnp.mean(as_float, axis=-1, keepdims=True)
        away = as_float - center
        spread = jnp.mean(away * away, axis=-1, keepdims=True)
        shift_row = mod_ref[0, pl.ds(tau, 1), 0:width]
        scale_row = mod_ref[0, pl.ds(tau, 1), width:2 * width]
        return (
            away * lax.rsqrt(spread + norm_eps) * (1.0 + scale_row) + shift_row
        ).astype(jnp.bfloat16)

    def pin_copy(slot, ahead):
        other = lax.rem(sharer + ahead, sharers)
        return remote(pbuf.at[slot, other], pin.at[slot, sharer], pin_send.at[slot, ahead],
                      pin_recv.at[slot, sharer], pipe, mine * sharers + other)

    def cin_copy(slot, ahead):
        group = lax.rem(mine + ahead, groups)
        return remote(csum.at[slot, group], cin.at[slot, mine], cin_send.at[slot, ahead],
                      cin_recv.at[slot, mine], pipe, group * sharers + sharer)

    @pl.when(pipe == 0)
    def _():
        for from_pipe in range(n_pipe):
            for from_seq in range(n_seq):
                lat_arrived(from_pipe, from_seq)
        for slot in range(micro):
            pieces = []
            for from_pipe in range(n_pipe):
                pieces.append(jnp.concatenate([
                    latbuf[from_pipe, index, slot].astype(jnp.float32) for index in range(n_seq)
                ], axis=0))
            whole = jnp.concatenate(pieces, axis=1)
            first_x[...] = whole.astype(jnp.bfloat16)
            mine_rows = pl.ds(pl.multiple_of(sharer * part, 16), part)
            for group in range(groups):
                hid[0, slot, group] = first_x[mine_rows, group * block:(group + 1) * block]
            whole_mod = modulate(whole, ts_ref[0, slot])
            first_mod[slot] = whole_mod
            for index in range(n_seq):
                slabs[index] = whole_mod[:, index * depth:(index + 1) * depth]
            feature_rows = slabs[seq]
            for kv in range(2):
                for group in range(groups):
                    start = kv * inner + group * block
                    partial = jnp.dot(feature_rows, wrows[:, start:start + block],
                                      preferred_element_type=jnp.float32).astype(jnp.bfloat16)
                    for at in range(sharers):
                        pbuf[slot, at, group, kv] = partial[at * part:(at + 1) * part]
            for ahead in range(1, sharers):
                pin_copy(slot, ahead).start()
            for ahead in range(1, sharers):
                other = lax.rem(sharer + ahead, sharers)
                pltpu.make_async_copy(pbuf.at[slot, other], pin.at[slot, other],
                                      pin_recv.at[slot, other]).wait()
            total = pbuf[slot, sharer].astype(jnp.float32)
            for ahead in range(1, sharers):
                total += pin[slot, lax.rem(sharer + ahead, sharers)].astype(jnp.float32)
            csum[slot] = total.astype(jnp.bfloat16)
            for ahead in range(1, groups):
                cin_copy(slot, ahead).start()

    pl.when(pipe != 0)(weights_finish)

    @pl.when(pipe == last)
    def _():
        for slot in range(micro):
            pieces = []
            for wide in range(per_block):
                pieces.append(jnp.concatenate([
                    latbuf_wait_load(latbuf, lat_arrived, slot == 0, mine * per_block + wide,
                                     sharer * per_part + index, slot)
                    for index in range(per_part)
                ], axis=0))
            prev[slot] = jnp.concatenate(pieces, axis=1) if per_block > 1 else pieces[0]

    def hid_send_copy(step, slot, group):
        at_last = pipe == last
        to_step = step + jnp.where(at_last, 1, 0)
        return remote(outb.at[step, slot], hid.at[to_step, slot, mine],
                      hid_send.at[step, slot, group], hid_recv.at[to_step, slot, mine],
                      lax.rem(pipe + 1, n_pipe), group * sharers + sharer)

    def hid_arrived(step, slot, group):
        pltpu.make_async_copy(outb.at[step, slot], hid.at[step, slot, group],
                              hid_recv.at[step, slot, group]).wait()

    def kvx_copy(step, slot, ahead):
        other = lax.rem(sharer + ahead, sharers)
        return remote(kvx.at[step, slot, sharer], kvx.at[step, slot, sharer], kvx_send.at[step, slot, ahead],
                      kvx_recv.at[step, slot, sharer], pipe, mine * sharers + other)

    def att_copy(step, slot, ahead):
        group = lax.rem(mine + ahead, groups)
        return remote(att.at[step, slot, mine], att.at[step, slot, mine],
                      att_send.at[step, slot, ahead], att_recv.at[step, slot, mine],
                      pipe, group * sharers + sharer)

    def att_arrived(step, slot, ahead):
        group = lax.rem(mine + ahead, groups)
        pltpu.make_async_copy(att.at[step, slot, mine], att.at[step, slot, group],
                              att_recv.at[step, slot, group]).wait()

    def fin_targets(slot):
        for wide in range(per_block):
            for index in range(per_part):
                to_pipe, to_seq = mine * per_block + wide, sharer * per_part + index
                source = fin_src.at[slot, wide, pl.ds(index * rows, rows), :]
                yield to_pipe, to_seq, source, fin_send.at[slot, wide, index]

    def project(step, slot):
        tau = ts_ref[step, slot]
        from_latents = (pipe == 0) & (step == 0)

        @pl.when(from_latents)
        def _():
            modded[...] = first_mod[slot, pl.ds(pl.multiple_of(sharer * part, 16), part), :]
            total = csum[slot, mine].astype(jnp.float32)
            for ahead in range(1, groups):
                group = lax.rem(mine + ahead, groups)
                pltpu.make_async_copy(csum.at[slot, group], cin.at[slot, group],
                                      cin_recv.at[slot, group]).wait()
                total += cin[slot, group].astype(jnp.float32)
            pre[:, :block] = total[0]
            pre[:, block:] = total[1]

        @pl.when(jnp.logical_not(from_latents))
        def _():
            for group in range(groups):
                hid_arrived(step, slot, group)
            modded[...] = modulate(
                jnp.concatenate([hid[step, slot, group].astype(jnp.float32) for group in range(groups)], axis=1),
                tau,
            )
            pre[...] = jnp.dot(modded[...], wkv[...], preferred_element_type=jnp.float32)

        gain_query, gain_key = gain_ref[0, 0:1, :], gain_ref[0, 1:2, :]
        slices = [slice(head * head_dim, (head + 1) * head_dim) for head in range(heads)]
        for here in slices:
            kvx[step, slot, sharer, 0, :, here] = rms_rows(pre[:, here], gain_key)
        kvx[step, slot, sharer, 1] = pre[:, block:].astype(jnp.bfloat16)
        for ahead in range(1, sharers):
            kvx_copy(step, slot, ahead).start()
        projected = jnp.dot(modded[...], wq[...], preferred_element_type=jnp.float32)
        for here in slices:
            qbuf[slot, :, here] = rms_rows(projected[:, here], gain_query)

    def attend(step, slot):
        slices = [slice(head * head_dim, (head + 1) * head_dim) for head in range(heads)]
        queries = [qbuf[slot, :, here] for here in slices]
        totals, weighted = [0.0] * heads, [0.0] * heads
        for ahead in range(sharers):
            owner = lax.rem(sharer + ahead, sharers)
            if ahead > 0:
                pltpu.make_async_copy(kvx.at[step, slot, sharer], kvx.at[step, slot, owner],
                                      kvx_recv.at[step, slot, owner]).wait()
            for head, here in enumerate(slices):
                logits = lax.dot_general(
                    queries[head], kvx[step, slot, owner, 0, :, here],
                    (((1,), (1,)), ((), ())), preferred_element_type=jnp.float32,
                ) * score_scale
                weights = jnp.exp(logits)
                totals[head] += jnp.sum(weights, axis=-1, keepdims=True)
                weighted[head] += jnp.dot(weights.astype(jnp.bfloat16), kvx[step, slot, owner, 1, :, here],
                                          preferred_element_type=jnp.float32)
        for head, here in enumerate(slices):
            att[step, slot, mine, :, here] = (weighted[head] / totals[head]).astype(jnp.bfloat16)
        for ahead in range(1, groups):
            att_copy(step, slot, ahead).start()

    def second_half(step, slot):
        tau = ts_ref[step, slot]
        gate_row = mod_ref[0, pl.ds(tau, 1), pl.ds(pl.multiple_of(2 * width + mine * block, 128), block)]
        residual = hid[step, slot, mine].astype(jnp.float32)
        projected = 0.0
        for ahead in range(groups):
            group = lax.rem(mine + ahead, groups)
            if ahead > 0:
                att_arrived(step, slot, ahead)
            attended = att[step, slot, group]
            rows_here = pl.ds(pl.multiple_of(group * block, 128), block)
            projected += jnp.dot(attended, wo[rows_here, :], preferred_element_type=jnp.float32)
        layer_out = (residual + gate_row * projected).astype(jnp.bfloat16)
        ends = (pipe == last) & (step == steps - 1)

        @pl.when(pipe != last)
        def _():
            outb[step, slot] = layer_out

        @pl.when(pipe == last)
        def _():
            update = (prev[slot] - ss_ref[tau] * layer_out.astype(jnp.float32)).astype(jnp.bfloat16)
            outb[step, slot] = update
            prev[slot] = update.astype(jnp.float32)

        @pl.when(jnp.logical_not(ends))
        def _():
            for ahead in range(groups):
                hid_send_copy(step, slot, lax.rem(mine + ahead, groups)).start()

        @pl.when(ends)
        def _():
            update = prev[slot]
            for wide in range(per_block):
                fin_src[slot, wide] = update[:, wide * share:(wide + 1) * share]
            for to_pipe, to_seq, source, send in fin_targets(slot):
                own = (to_pipe == pipe) & (to_seq == seq)

                @pl.when(own)
                def _():
                    pltpu.make_async_copy(source, fin.at[slot], fin_recv.at[slot]).start()

                @pl.when(jnp.logical_not(own))
                def _():
                    remote(source, fin.at[slot], send, fin_recv.at[slot], to_pipe, to_seq).start()

    def visit(step, carry):
        @pl.when((pipe == 0) & (step == 1))
        def _():
            weights_start()
            weights_finish()

        project(step, 0)
        attend(step, 0)
        for slot in range(micro):
            if slot + 1 < micro:
                project(step, slot + 1)
            second_half(step, slot)
            if slot + 1 < micro:
                attend(step, slot + 1)
        return carry

    lax.fori_loop(0, steps, visit, 0)

    for slot in range(micro):
        pltpu.make_async_copy(fin_src.at[slot, 0, pl.ds(0, rows), :], fin.at[slot],
                              fin_recv.at[slot]).wait()
        out_ref[slot] = fin[slot].astype(jnp.bfloat16)

    for ahead in range(n_seq):
        target = lax.rem(seq + ahead, n_seq)
        if ahead == 0:
            @pl.when(pipe != 0)
            def _():
                lat_copy(0, target, ahead).wait_send()
        else:
            lat_copy(0, target, ahead).wait_send()

    @pl.when(jnp.logical_not(keeps_own))
    def _():
        lat_copy(last, keeper, n_seq).wait_send()

    @pl.when(pipe == 0)
    def _():
        for slot in range(micro):
            for ahead in range(1, sharers):
                pin_copy(slot, ahead).wait_send()
            for ahead in range(1, groups):
                cin_copy(slot, ahead).wait_send()

    for kv in range(2):
        for ahead in range(1, groups):
            kv_copy(kv, ahead).wait_send()
        for ahead in range(groups):
            for step in range(1, sharers):
                kv_pass(kv, ahead, step).wait_send()

    def drain(item, carry):
        step, slot = item // micro, item % micro
        ends = (pipe == last) & (step == steps - 1)
        for ahead in range(1, groups):
            att_copy(step, slot, ahead).wait_send()
        for ahead in range(1, sharers):
            kvx_copy(step, slot, ahead).wait_send()

        @pl.when(jnp.logical_not(ends))
        def _():
            for group in range(groups):
                hid_send_copy(step, slot, group).wait_send()

        @pl.when(ends)
        def _():
            for to_pipe, to_seq, source, send in fin_targets(slot):
                @pl.when(jnp.logical_not((to_pipe == pipe) & (to_seq == seq)))
                def _():
                    remote(source, fin.at[slot], send, fin_recv.at[slot], to_pipe, to_seq).wait_send()
        return carry

    lax.fori_loop(0, micro * steps, drain, 0)


def latbuf_wait_load(latbuf, lat_arrived, first, from_pipe, from_seq, slot):
    if first:
        lat_arrived(from_pipe, from_seq)
    return latbuf[from_pipe, from_seq, slot].astype(jnp.float32)


def shards(latents, timesteps, step_sizes, mod_table, qk_gain, w_query, w_kv, w_out):
    n_pipe, n_seq = lax.axis_size("pipe"), lax.axis_size("seq")
    micro, rows, share = latents.shape
    steps = timesteps.shape[0]
    head_dim = qk_gain.shape[2]
    width, inner = w_query.shape[1], w_query.shape[2]
    heads = inner // head_dim
    groups = math.gcd(math.gcd(heads, n_seq), n_pipe)
    while n_seq // groups < 2:
        groups //= 2
    sharers = n_seq // groups
    block = inner // groups
    part = rows * n_seq // sharers
    per_block, per_part = n_pipe // groups, n_seq // sharers
    bf16, f32 = jnp.bfloat16, jnp.float32
    vmem = pl.BlockSpec(memory_space=pltpu.VMEM)
    hbm = pl.BlockSpec(memory_space=pl.ANY)
    dma = pltpu.SemaphoreType.DMA
    return pl.pallas_call(
        functools.partial(kernel, n_pipe, n_seq, groups, micro, steps, head_dim),
        out_shape=jax.ShapeDtypeStruct(latents.shape, bf16),
        in_specs=[hbm] * 8,
        out_specs=vmem,
        scratch_shapes=[
            pltpu.SMEM(timesteps.shape, timesteps.dtype),
            pltpu.SMEM(step_sizes.shape, f32),
            pltpu.VMEM(mod_table.shape, f32),
            pltpu.VMEM(qk_gain.shape, f32),
            pltpu.VMEM((width, block), bf16),
            pltpu.VMEM((width, 2 * block), bf16),
            pltpu.VMEM((inner, block), bf16),
            pltpu.VMEM(w_kv.shape[1:], bf16),
            pltpu.VMEM((n_pipe, n_seq, micro, rows, share), bf16),
            pltpu.VMEM((steps, micro, groups, part, block), bf16),
            pltpu.VMEM((steps, micro, groups, part, block), bf16),
            pltpu.VMEM((steps, micro, part, block), bf16),
            pltpu.VMEM((micro, part, block), f32),
            pltpu.VMEM((part, width), bf16),
            pltpu.VMEM((rows * n_seq, width), bf16),
            pltpu.VMEM((micro, rows * n_seq, width), bf16),
            pltpu.VMEM((n_seq, rows * n_seq, w_kv.shape[1]), bf16),
            pltpu.VMEM((micro, sharers, groups, 2, part, block), bf16),
            pltpu.VMEM((micro, sharers, groups, 2, part, block), bf16),
            pltpu.VMEM((micro, groups, 2, part, block), bf16),
            pltpu.VMEM((micro, groups, 2, part, block), bf16),
            pltpu.VMEM((part, 2 * block), f32),
            pltpu.VMEM((micro, part, block), bf16),
            pltpu.VMEM((steps, micro, sharers, 2, part, block), bf16),
            pltpu.VMEM((micro, per_block, part, share), f32),
            pltpu.VMEM((micro, rows, share), f32),
            dma((7,)),
            dma((2, n_seq)),
            dma((2, groups)),
            dma((2, groups, sharers)),
            dma((n_seq + 1,)),
            dma((n_pipe, n_seq)),
            dma((micro, sharers)),
            dma((micro, sharers)),
            dma((micro, groups)),
            dma((micro, groups)),
            dma((steps, micro, groups)),
            dma((steps, micro, groups)),
            dma((steps, micro, sharers)),
            dma((steps, micro, sharers)),
            dma((steps, micro, groups)),
            dma((steps, micro, groups)),
            dma((micro, per_block, per_part)),
            dma((micro,)),
        ],
        compiler_params=pltpu.CompilerParams(
            has_side_effects=True, vmem_limit_bytes=64 * 1024 * 1024
        ),
        cost_estimate=pl.CostEstimate(
            flops=2 * 4 * rows * n_seq * width * block * micro * steps,
            bytes_accessed=2 * 4 * width * block, transcendentals=0,
        ),
        name="denoise",
    )(latents, timesteps, step_sizes, mod_table, qk_gain, w_query, w_kv, w_out)


def solution(mesh):
    in_specs = (
        P(None, "seq", "pipe"),
        P(),
        P(),
        P("pipe", None, None),
        P("pipe", None, None),
        P("pipe", None, None),
        P("pipe", "seq", None),
        P("pipe", None, None),
    )
    out_specs = P(None, "seq", "pipe")
    return jax.shard_map(shards, mesh=mesh, in_specs=in_specs, out_specs=out_specs, check_vma=False)
```

```python
import functools
import math

import jax
import jax.numpy as jnp
from jax import lax
from jax.experimental import pallas as pl
from jax.experimental.pallas import tpu as pltpu
from jax.sharding import PartitionSpec as P

norm_eps = 1e-06
MESH = pl.DeviceIdType.MESH


def rms_rows(values, gain_row):
    mean_square = jnp.mean(values * values, axis=-1, keepdims=True)
    return (values * lax.rsqrt(mean_square + norm_eps) * gain_row).astype(jnp.bfloat16)


def kernel(
    n_pipe, n_seq, groups, micro, steps, head_dim,
    lat_ref, ts_hbm, ss_hbm, mod_hbm, gain_hbm, wq_hbm, wkv_hbm, wo_hbm,
    out_ref,
    ts_ref, ss_ref, mod_ref, gain_ref, wq, wkv, wo, wrows, latbuf, hid, att, outb, prev, modded,
    first_x, first_mod, slabs, pbuf, pin, csum, cin, pre, kvx, fin_src, fin,
    local_sem, kv_recv, kv_send, kv_fwd, lat_send, lat_recv, pin_send, pin_recv, cin_send, cin_recv,
    hid_recv, hid_send, kvx_send, kvx_recv, att_recv, att_send, fin_send, fin_recv,
):
    sharers = n_seq // groups
    rows, share = lat_ref.shape[1], lat_ref.shape[2]
    tokens = rows * n_seq
    width = share * n_pipe
    block = wq.shape[1]
    inner = block * groups
    depth = wkv_hbm.shape[1]
    part = tokens // sharers
    per_block = n_pipe // groups
    per_part = n_seq // sharers
    heads = block // head_dim
    score_scale = 1.0 / math.sqrt(head_dim)
    last = n_pipe - 1

    pipe, seq = lax.axis_index("pipe"), lax.axis_index("seq")
    mine, sharer = seq // sharers, seq % sharers

    def remote(src, dst, send, recv, to_pipe, to_seq):
        return pltpu.make_async_remote_copy(
            src_ref=src, dst_ref=dst, send_sem=send, recv_sem=recv,
            device_id=(to_pipe, to_seq), device_id_type=MESH,
        )

    def lat_copy(to_pipe, to_seq, index):
        return remote(lat_ref, latbuf.at[pipe, seq], lat_send.at[index],
                      lat_recv.at[pipe, seq], to_pipe, to_seq)

    def lat_local():
        return pltpu.make_async_copy(lat_ref, latbuf.at[pipe, seq], lat_recv.at[pipe, seq])

    def lat_arrived(from_pipe, from_seq):
        pltpu.make_async_copy(lat_ref, latbuf.at[from_pipe, from_seq],
                              lat_recv.at[from_pipe, from_seq]).wait()

    keeper = (pipe // per_block) * sharers + seq // per_part
    for ahead in range(n_seq):
        target = lax.rem(seq + ahead, n_seq)
        if ahead == 0:
            @pl.when(pipe == 0)
            def _():
                lat_local().start()

            @pl.when(pipe != 0)
            def _():
                lat_copy(0, target, ahead).start()
        else:
            lat_copy(0, target, ahead).start()
    keeps_own = (pipe == last) & (keeper == seq)

    @pl.when(keeps_own)
    def _():
        lat_local().start()

    @pl.when(jnp.logical_not(keeps_own))
    def _():
        lat_copy(last, keeper, n_seq).start()


    def columns(kv, group):
        start = pl.multiple_of(kv * inner + group * block, 128)
        return wrows.at[:, pl.ds(start, block)]

    def slab(kv, owner):
        return wkv.at[pl.ds(pl.multiple_of(owner * depth, 16), depth), kv * block:(kv + 1) * block]

    def kv_copy(kv, ahead):
        group = lax.rem(mine + ahead, groups)
        return remote(columns(kv, group), slab(kv, seq), kv_send.at[kv, ahead],
                      kv_recv.at[kv, seq], pipe, group * sharers + sharer)

    def kv_pass(kv, ahead, step):
        group = lax.rem(mine + ahead, groups)
        owner = group * sharers + sharer
        source = columns(kv, mine) if ahead == 0 else slab(kv, owner)
        return remote(source, slab(kv, owner), kv_fwd.at[kv, ahead, step],
                      kv_recv.at[kv, owner], pipe, mine * sharers + lax.rem(sharer + step, sharers))

    def kv_arrived(kv, owner):
        pltpu.make_async_copy(columns(kv, mine), slab(kv, owner), kv_recv.at[kv, owner]).wait()

    rows_in = pltpu.make_async_copy(wkv_hbm.at[0], wrows, local_sem.at[6])
    rows_in.start()
    own_columns = pl.ds(pl.multiple_of(mine * block, 128), block)
    copy_q = pltpu.make_async_copy(wq_hbm.at[0, :, own_columns], wq, local_sem.at[0])
    copy_o = pltpu.make_async_copy(wo_hbm.at[0, :, own_columns], wo, local_sem.at[1])
    def weights_rest():
        for kv in range(2):
            for ahead in range(groups - 1, 1, -1):
                kv_copy(kv, ahead).start()

    def weights_first():
        for kv in range(2):
            if groups > 1:
                kv_copy(kv, 1).start()
        for kv in range(2):
            pltpu.make_async_copy(columns(kv, mine), slab(kv, seq), kv_recv.at[kv, seq]).start()
            for step in range(1, sharers):
                kv_pass(kv, 0, step).start()

    def weights_finish():
        for kv in range(2):
            for ahead in range(1, groups):
                kv_arrived(kv, lax.rem(mine + ahead, groups) * sharers + sharer)
                for step in range(1, sharers):
                    kv_pass(kv, ahead, step).start()
        for kv in range(2):
            kv_arrived(kv, seq)
            for step in range(1, sharers):
                for group in range(groups):
                    kv_arrived(kv, group * sharers + lax.rem(sharer + step, sharers))

    rows_in.wait()
    pl.when(pipe != 0)(weights_rest)
    weights_first()
    locals_in = [
        copy_q, copy_o,
        pltpu.make_async_copy(ts_hbm, ts_ref, local_sem.at[2]),
        pltpu.make_async_copy(ss_hbm, ss_ref, local_sem.at[3]),
        pltpu.make_async_copy(mod_hbm, mod_ref, local_sem.at[4]),
        pltpu.make_async_copy(gain_hbm, gain_ref, local_sem.at[5]),
    ]
    for copy in locals_in:
        copy.start()
    for copy in locals_in:
        copy.wait()

    def modulate(as_float, tau):
        center = jnp.mean(as_float, axis=-1, keepdims=True)
        away = as_float - center
        spread = jnp.mean(away * away, axis=-1, keepdims=True)
        shift_row = mod_ref[0, pl.ds(tau, 1), 0:width]
        scale_row = mod_ref[0, pl.ds(tau, 1), width:2 * width]
        return (
            away * lax.rsqrt(spread + norm_eps) * (1.0 + scale_row) + shift_row
        ).astype(jnp.bfloat16)

    def pin_copy(slot, ahead):
        other = lax.rem(sharer + ahead, sharers)
        return remote(pbuf.at[slot, other], pin.at[slot, sharer], pin_send.at[slot, ahead],
                      pin_recv.at[slot, sharer], pipe, mine * sharers + other)

    def cin_copy(slot, ahead):
        group = lax.rem(mine + ahead, groups)
        return remote(csum.at[slot, group], cin.at[slot, mine], cin_send.at[slot, ahead],
                      cin_recv.at[slot, mine], pipe, group * sharers + sharer)

    @pl.when(pipe == 0)
    def _():
        for from_pipe in range(n_pipe):
            for from_seq in range(n_seq):
                lat_arrived(from_pipe, from_seq)
        for slot in range(micro):
            pieces = []
            for from_pipe in range(n_pipe):
                pieces.append(jnp.concatenate([
                    latbuf[from_pipe, index, slot].astype(jnp.float32) for index in range(n_seq)
                ], axis=0))
            whole = jnp.concatenate(pieces, axis=1)
            first_x[...] = whole.astype(jnp.bfloat16)
            mine_rows = pl.ds(pl.multiple_of(sharer * part, 16), part)
            for group in range(groups):
                hid[0, slot, group] = first_x[mine_rows, group * block:(group + 1) * block]
            whole_mod = modulate(whole, ts_ref[0, slot])
            first_mod[slot] = whole_mod
            for index in range(n_seq):
                slabs[index] = whole_mod[:, index * depth:(index + 1) * depth]
            feature_rows = slabs[seq]
            for kv in range(2):
                for group in range(groups):
                    start = kv * inner + group * block
                    partial = jnp.dot(feature_rows, wrows[:, start:start + block],
                                      preferred_element_type=jnp.float32).astype(jnp.bfloat16)
                    for at in range(sharers):
                        pbuf[slot, at, group, kv] = partial[at * part:(at + 1) * part]
            for ahead in range(1, sharers):
                pin_copy(slot, ahead).start()
        for slot in range(micro):
            for ahead in range(1, sharers):
                other = lax.rem(sharer + ahead, sharers)
                pltpu.make_async_copy(pbuf.at[slot, other], pin.at[slot, other],
                                      pin_recv.at[slot, other]).wait()
            total = pbuf[slot, sharer].astype(jnp.float32)
            for ahead in range(1, sharers):
                total += pin[slot, lax.rem(sharer + ahead, sharers)].astype(jnp.float32)
            csum[slot] = total.astype(jnp.bfloat16)
            for ahead in range(1, groups):
                cin_copy(slot, ahead).start()

    pl.when(pipe != 0)(weights_finish)

    @pl.when(pipe == last)
    def _():
        for slot in range(micro):
            pieces = []
            for wide in range(per_block):
                pieces.append(jnp.concatenate([
                    latbuf_wait_load(latbuf, lat_arrived, slot == 0, mine * per_block + wide,
                                     sharer * per_part + index, slot)
                    for index in range(per_part)
                ], axis=0))
            prev[slot] = jnp.concatenate(pieces, axis=1) if per_block > 1 else pieces[0]

    def hid_send_copy(step, slot, group):
        at_last = pipe == last
        to_step = step + jnp.where(at_last, 1, 0)
        return remote(outb.at[step, slot], hid.at[to_step, slot, mine],
                      hid_send.at[step, slot, group], hid_recv.at[to_step, slot, mine],
                      lax.rem(pipe + 1, n_pipe), group * sharers + sharer)

    def hid_arrived(step, slot, group):
        pltpu.make_async_copy(outb.at[step, slot], hid.at[step, slot, group],
                              hid_recv.at[step, slot, group]).wait()

    def kvx_copy(step, slot, ahead):
        other = lax.rem(sharer + ahead, sharers)
        return remote(kvx.at[step, slot, sharer], kvx.at[step, slot, sharer], kvx_send.at[step, slot, ahead],
                      kvx_recv.at[step, slot, sharer], pipe, mine * sharers + other)

    def att_copy(step, slot, ahead):
        group = lax.rem(mine + ahead, groups)
        return remote(att.at[step, slot, mine], att.at[step, slot, mine],
                      att_send.at[step, slot, ahead], att_recv.at[step, slot, mine],
                      pipe, group * sharers + sharer)

    def att_arrived(step, slot, ahead):
        group = lax.rem(mine + ahead, groups)
        pltpu.make_async_copy(att.at[step, slot, mine], att.at[step, slot, group],
                              att_recv.at[step, slot, group]).wait()

    def fin_targets(slot):
        for wide in range(per_block):
            for index in range(per_part):
                to_pipe, to_seq = mine * per_block + wide, sharer * per_part + index
                source = fin_src.at[slot, wide, pl.ds(index * rows, rows), :]
                yield to_pipe, to_seq, source, fin_send.at[slot, wide, index]

    def first_half(step, slot):
        tau = ts_ref[step, slot]
        from_latents = (pipe == 0) & (step == 0)

        @pl.when(from_latents)
        def _():
            modded[...] = first_mod[slot, pl.ds(pl.multiple_of(sharer * part, 16), part), :]
            total = csum[slot, mine].astype(jnp.float32)
            for ahead in range(1, groups):
                group = lax.rem(mine + ahead, groups)
                pltpu.make_async_copy(csum.at[slot, group], cin.at[slot, group],
                                      cin_recv.at[slot, group]).wait()
                total += cin[slot, group].astype(jnp.float32)
            pre[:, :block] = total[0]
            pre[:, block:] = total[1]

        @pl.when(jnp.logical_not(from_latents))
        def _():
            for group in range(groups):
                hid_arrived(step, slot, group)
            modded[...] = modulate(
                jnp.concatenate([hid[step, slot, group].astype(jnp.float32) for group in range(groups)], axis=1),
                tau,
            )
            pre[...] = jnp.dot(modded[...], wkv[...], preferred_element_type=jnp.float32)

        gain_query, gain_key = gain_ref[0, 0:1, :], gain_ref[0, 1:2, :]
        slices = [slice(head * head_dim, (head + 1) * head_dim) for head in range(heads)]
        for here in slices:
            kvx[step, slot, sharer, 0, :, here] = rms_rows(pre[:, here], gain_key)
        kvx[step, slot, sharer, 1] = pre[:, block:].astype(jnp.bfloat16)
        for ahead in range(1, sharers):
            kvx_copy(step, slot, ahead).start()
        projected = jnp.dot(modded[...], wq[...], preferred_element_type=jnp.float32)
        queries = [rms_rows(projected[:, here], gain_query) for here in slices]
        totals, weighted = [0.0] * heads, [0.0] * heads
        for ahead in range(sharers):
            owner = lax.rem(sharer + ahead, sharers)
            if ahead > 0:
                pltpu.make_async_copy(kvx.at[step, slot, sharer], kvx.at[step, slot, owner],
                                      kvx_recv.at[step, slot, owner]).wait()
            for head, here in enumerate(slices):
                logits = lax.dot_general(
                    queries[head], kvx[step, slot, owner, 0, :, here],
                    (((1,), (1,)), ((), ())), preferred_element_type=jnp.float32,
                ) * score_scale
                weights = jnp.exp(logits)
                totals[head] += jnp.sum(weights, axis=-1, keepdims=True)
                weighted[head] += jnp.dot(weights.astype(jnp.bfloat16), kvx[step, slot, owner, 1, :, here],
                                          preferred_element_type=jnp.float32)
        for head, here in enumerate(slices):
            att[step, slot, mine, :, here] = (weighted[head] / totals[head]).astype(jnp.bfloat16)
        for ahead in range(1, groups):
            att_copy(step, slot, ahead).start()

    def second_half(step, slot):
        tau = ts_ref[step, slot]
        gate_row = mod_ref[0, pl.ds(tau, 1), pl.ds(pl.multiple_of(2 * width + mine * block, 128), block)]
        residual = hid[step, slot, mine].astype(jnp.float32)
        projected = 0.0
        for ahead in range(groups):
            group = lax.rem(mine + ahead, groups)
            if ahead > 0:
                att_arrived(step, slot, ahead)
            attended = att[step, slot, group]
            rows_here = pl.ds(pl.multiple_of(group * block, 128), block)
            projected += jnp.dot(attended, wo[rows_here, :], preferred_element_type=jnp.float32)
        layer_out = (residual + gate_row * projected).astype(jnp.bfloat16)
        ends = (pipe == last) & (step == steps - 1)

        @pl.when(pipe != last)
        def _():
            outb[step, slot] = layer_out

        @pl.when(pipe == last)
        def _():
            update = (prev[slot] - ss_ref[tau] * layer_out.astype(jnp.float32)).astype(jnp.bfloat16)
            outb[step, slot] = update
            prev[slot] = update.astype(jnp.float32)

        @pl.when(jnp.logical_not(ends))
        def _():
            for ahead in range(groups):
                hid_send_copy(step, slot, lax.rem(mine + ahead, groups)).start()

        @pl.when(ends)
        def _():
            update = prev[slot]
            for wide in range(per_block):
                fin_src[slot, wide] = update[:, wide * share:(wide + 1) * share]
            for to_pipe, to_seq, source, send in fin_targets(slot):
                own = (to_pipe == pipe) & (to_seq == seq)

                @pl.when(own)
                def _():
                    pltpu.make_async_copy(source, fin.at[slot], fin_recv.at[slot]).start()

                @pl.when(jnp.logical_not(own))
                def _():
                    remote(source, fin.at[slot], send, fin_recv.at[slot], to_pipe, to_seq).start()

    def visit(step, carry):
        @pl.when((pipe == 0) & (step == 1))
        def _():
            weights_rest()
            weights_finish()

        for slot in range(micro):
            first_half(step, slot)
            second_half(step, slot)
        return carry

    lax.fori_loop(0, steps, visit, 0)

    for slot in range(micro):
        pltpu.make_async_copy(fin_src.at[slot, 0, pl.ds(0, rows), :], fin.at[slot],
                              fin_recv.at[slot]).wait()
        out_ref[slot] = fin[slot].astype(jnp.bfloat16)

    for ahead in range(n_seq):
        target = lax.rem(seq + ahead, n_seq)
        if ahead == 0:
            @pl.when(pipe != 0)
            def _():
                lat_copy(0, target, ahead).wait_send()
        else:
            lat_copy(0, target, ahead).wait_send()

    @pl.when(jnp.logical_not(keeps_own))
    def _():
        lat_copy(last, keeper, n_seq).wait_send()

    @pl.when(pipe == 0)
    def _():
        for slot in range(micro):
            for ahead in range(1, sharers):
                pin_copy(slot, ahead).wait_send()
            for ahead in range(1, groups):
                cin_copy(slot, ahead).wait_send()

    for kv in range(2):
        for ahead in range(1, groups):
            kv_copy(kv, ahead).wait_send()
        for ahead in range(groups):
            for step in range(1, sharers):
                kv_pass(kv, ahead, step).wait_send()

    def drain(item, carry):
        step, slot = item // micro, item % micro
        ends = (pipe == last) & (step == steps - 1)
        for ahead in range(1, groups):
            att_copy(step, slot, ahead).wait_send()
        for ahead in range(1, sharers):
            kvx_copy(step, slot, ahead).wait_send()

        @pl.when(jnp.logical_not(ends))
        def _():
            for group in range(groups):
                hid_send_copy(step, slot, group).wait_send()

        @pl.when(ends)
        def _():
            for to_pipe, to_seq, source, send in fin_targets(slot):
                @pl.when(jnp.logical_not((to_pipe == pipe) & (to_seq == seq)))
                def _():
                    remote(source, fin.at[slot], send, fin_recv.at[slot], to_pipe, to_seq).wait_send()
        return carry

    lax.fori_loop(0, micro * steps, drain, 0)


def latbuf_wait_load(latbuf, lat_arrived, first, from_pipe, from_seq, slot):
    if first:
        lat_arrived(from_pipe, from_seq)
    return latbuf[from_pipe, from_seq, slot].astype(jnp.float32)


def shards(latents, timesteps, step_sizes, mod_table, qk_gain, w_query, w_kv, w_out):
    n_pipe, n_seq = lax.axis_size("pipe"), lax.axis_size("seq")
    micro, rows, share = latents.shape
    steps = timesteps.shape[0]
    head_dim = qk_gain.shape[2]
    width, inner = w_query.shape[1], w_query.shape[2]
    heads = inner // head_dim
    groups = math.gcd(math.gcd(heads, n_seq), n_pipe)
    while n_seq // groups < 2:
        groups //= 2
    sharers = n_seq // groups
    block = inner // groups
    part = rows * n_seq // sharers
    per_block, per_part = n_pipe // groups, n_seq // sharers
    bf16, f32 = jnp.bfloat16, jnp.float32
    vmem = pl.BlockSpec(memory_space=pltpu.VMEM)
    hbm = pl.BlockSpec(memory_space=pl.ANY)
    dma = pltpu.SemaphoreType.DMA
    return pl.pallas_call(
        functools.partial(kernel, n_pipe, n_seq, groups, micro, steps, head_dim),
        out_shape=jax.ShapeDtypeStruct(latents.shape, bf16),
        in_specs=[hbm] * 8,
        out_specs=vmem,
        scratch_shapes=[
            pltpu.SMEM(timesteps.shape, timesteps.dtype),
            pltpu.SMEM(step_sizes.shape, f32),
            pltpu.VMEM(mod_table.shape, f32),
            pltpu.VMEM(qk_gain.shape, f32),
            pltpu.VMEM((width, block), bf16),
            pltpu.VMEM((width, 2 * block), bf16),
            pltpu.VMEM((inner, block), bf16),
            pltpu.VMEM(w_kv.shape[1:], bf16),
            pltpu.VMEM((n_pipe, n_seq, micro, rows, share), bf16),
            pltpu.VMEM((steps, micro, groups, part, block), bf16),
            pltpu.VMEM((steps, micro, groups, part, block), bf16),
            pltpu.VMEM((steps, micro, part, block), bf16),
            pltpu.VMEM((micro, part, block), f32),
            pltpu.VMEM((part, width), bf16),
            pltpu.VMEM((rows * n_seq, width), bf16),
            pltpu.VMEM((micro, rows * n_seq, width), bf16),
            pltpu.VMEM((n_seq, rows * n_seq, w_kv.shape[1]), bf16),
            pltpu.VMEM((micro, sharers, groups, 2, part, block), bf16),
            pltpu.VMEM((micro, sharers, groups, 2, part, block), bf16),
            pltpu.VMEM((micro, groups, 2, part, block), bf16),
            pltpu.VMEM((micro, groups, 2, part, block), bf16),
            pltpu.VMEM((part, 2 * block), f32),
            pltpu.VMEM((steps, micro, sharers, 2, part, block), bf16),
            pltpu.VMEM((micro, per_block, part, share), f32),
            pltpu.VMEM((micro, rows, share), f32),
            dma((7,)),
            dma((2, n_seq)),
            dma((2, groups)),
            dma((2, groups, sharers)),
            dma((n_seq + 1,)),
            dma((n_pipe, n_seq)),
            dma((micro, sharers)),
            dma((micro, sharers)),
            dma((micro, groups)),
            dma((micro, groups)),
            dma((steps, micro, groups)),
            dma((steps, micro, groups)),
            dma((steps, micro, sharers)),
            dma((steps, micro, sharers)),
            dma((steps, micro, groups)),
            dma((steps, micro, groups)),
            dma((micro, per_block, per_part)),
            dma((micro,)),
        ],
        compiler_params=pltpu.CompilerParams(
            has_side_effects=True, vmem_limit_bytes=64 * 1024 * 1024
        ),
        cost_estimate=pl.CostEstimate(
            flops=2 * 4 * rows * n_seq * width * block * micro * steps,
            bytes_accessed=2 * 4 * width * block, transcendentals=0,
        ),
        name="denoise",
    )(latents, timesteps, step_sizes, mod_table, qk_gain, w_query, w_kv, w_out)


def solution(mesh):
    in_specs = (
        P(None, "seq", "pipe"),
        P(),
        P(),
        P("pipe", None, None),
        P("pipe", None, None),
        P("pipe", None, None),
        P("pipe", "seq", None),
        P("pipe", None, None),
    )
    out_specs = P(None, "seq", "pipe")
    return jax.shard_map(shards, mesh=mesh, in_specs=in_specs, out_specs=out_specs, check_vma=False)
```

```python
import functools
import math

import jax
import jax.numpy as jnp
from jax import lax
from jax.experimental import pallas as pl
from jax.experimental.pallas import tpu as pltpu
from jax.sharding import PartitionSpec as P

norm_eps = 1e-06
MESH = pl.DeviceIdType.MESH


def rms_rows(values, gain_row):
    mean_square = jnp.mean(values * values, axis=-1, keepdims=True)
    return (values * lax.rsqrt(mean_square + norm_eps) * gain_row).astype(jnp.bfloat16)


def kernel(
    n_pipe, n_seq, groups, micro, steps, head_dim,
    lat_ref, ts_hbm, ss_hbm, mod_hbm, gain_hbm, wq_hbm, wkv_hbm, wo_hbm,
    out_ref,
    ts_ref, ss_ref, mod_ref, gain_ref, wq, wkv, wo, wrows, latbuf, hid, att, outb, prev, modded,
    first_x, first_mod, slabs, pbuf, pin, csum, cin, pre, kvx, fin_src, fin,
    local_sem, kv_recv, kv_send, kv_fwd, lat_send, lat_recv, lat_fwd, pin_send, pin_recv, cin_send, cin_recv,
    hid_recv, hid_send, kvx_send, kvx_recv, att_recv, att_send, fin_send, fin_recv,
):
    sharers = n_seq // groups
    rows, share = lat_ref.shape[1], lat_ref.shape[2]
    tokens = rows * n_seq
    width = share * n_pipe
    block = wq.shape[1]
    inner = block * groups
    depth = wkv_hbm.shape[1]
    part = tokens // sharers
    per_block = n_pipe // groups
    per_part = n_seq // sharers
    heads = block // head_dim
    score_scale = 1.0 / math.sqrt(head_dim)
    last = n_pipe - 1

    pipe, seq = lax.axis_index("pipe"), lax.axis_index("seq")
    mine, sharer = seq // sharers, seq % sharers

    def remote(src, dst, send, recv, to_pipe, to_seq):
        return pltpu.make_async_remote_copy(
            src_ref=src, dst_ref=dst, send_sem=send, recv_sem=recv,
            device_id=(to_pipe, to_seq), device_id_type=MESH,
        )

    def lat_copy(to_pipe, to_seq, index):
        return remote(lat_ref, latbuf.at[pipe, seq], lat_send.at[index],
                      lat_recv.at[pipe, seq], to_pipe, to_seq)

    def lat_local():
        return pltpu.make_async_copy(lat_ref, latbuf.at[pipe, seq], lat_recv.at[pipe, seq])

    def lat_arrived(from_pipe, from_seq):
        pltpu.make_async_copy(lat_ref, latbuf.at[from_pipe, from_seq],
                              lat_recv.at[from_pipe, from_seq]).wait()

    def lat_pass(from_pipe, group, step):
        from_seq = group * sharers + sharer
        return remote(latbuf.at[from_pipe, from_seq], latbuf.at[from_pipe, from_seq],
                      lat_fwd.at[from_pipe, group, step], lat_recv.at[from_pipe, from_seq],
                      pipe, mine * sharers + lax.rem(sharer + step, sharers))

    keeper = (pipe // per_block) * sharers + seq // per_part
    for ahead in range(groups):
        target = lax.rem(mine + ahead, groups) * sharers + sharer
        if ahead == 0:
            @pl.when(pipe == 0)
            def _():
                lat_local().start()

            @pl.when(pipe != 0)
            def _():
                lat_copy(0, target, ahead).start()
        else:
            lat_copy(0, target, ahead).start()
    keeps_own = (pipe == last) & (keeper == seq)

    @pl.when(keeps_own)
    def _():
        lat_local().start()

    @pl.when(jnp.logical_not(keeps_own))
    def _():
        lat_copy(last, keeper, n_seq).start()


    def columns(kv, group):
        start = pl.multiple_of(kv * inner + group * block, 128)
        return wrows.at[:, pl.ds(start, block)]

    def slab(kv, owner):
        return wkv.at[pl.ds(pl.multiple_of(owner * depth, 16), depth), kv * block:(kv + 1) * block]

    def kv_copy(kv, ahead):
        group = lax.rem(mine + ahead, groups)
        return remote(columns(kv, group), slab(kv, seq), kv_send.at[kv, ahead],
                      kv_recv.at[kv, seq], pipe, group * sharers + sharer)

    def kv_pass(kv, ahead, step):
        group = lax.rem(mine + ahead, groups)
        owner = group * sharers + sharer
        source = columns(kv, mine) if ahead == 0 else slab(kv, owner)
        return remote(source, slab(kv, owner), kv_fwd.at[kv, ahead, step],
                      kv_recv.at[kv, owner], pipe, mine * sharers + lax.rem(sharer + step, sharers))

    def kv_arrived(kv, owner):
        pltpu.make_async_copy(columns(kv, mine), slab(kv, owner), kv_recv.at[kv, owner]).wait()

    rows_in = pltpu.make_async_copy(wkv_hbm.at[0], wrows, local_sem.at[6])
    rows_in.start()
    own_columns = pl.ds(pl.multiple_of(mine * block, 128), block)
    copy_q = pltpu.make_async_copy(wq_hbm.at[0, :, own_columns], wq, local_sem.at[0])
    copy_o = pltpu.make_async_copy(wo_hbm.at[0, :, own_columns], wo, local_sem.at[1])
    def weights_start():
        for kv in range(2):
            for ahead in range(groups - 1, 0, -1):
                kv_copy(kv, ahead).start()
        for kv in range(2):
            pltpu.make_async_copy(columns(kv, mine), slab(kv, seq), kv_recv.at[kv, seq]).start()
            for step in range(1, sharers):
                kv_pass(kv, 0, step).start()

    def weights_finish():
        for kv in range(2):
            for ahead in range(1, groups):
                kv_arrived(kv, lax.rem(mine + ahead, groups) * sharers + sharer)
                for step in range(1, sharers):
                    kv_pass(kv, ahead, step).start()
        for kv in range(2):
            kv_arrived(kv, seq)
            for step in range(1, sharers):
                for group in range(groups):
                    kv_arrived(kv, group * sharers + lax.rem(sharer + step, sharers))

    rows_in.wait()
    pl.when(pipe != 0)(weights_start)
    locals_in = [
        copy_q, copy_o,
        pltpu.make_async_copy(ts_hbm, ts_ref, local_sem.at[2]),
        pltpu.make_async_copy(ss_hbm, ss_ref, local_sem.at[3]),
        pltpu.make_async_copy(mod_hbm, mod_ref, local_sem.at[4]),
        pltpu.make_async_copy(gain_hbm, gain_ref, local_sem.at[5]),
    ]
    for copy in locals_in:
        copy.start()
    for copy in locals_in:
        copy.wait()

    def modulate(as_float, tau):
        center = jnp.mean(as_float, axis=-1, keepdims=True)
        away = as_float - center
        spread = jnp.mean(away * away, axis=-1, keepdims=True)
        shift_row = mod_ref[0, pl.ds(tau, 1), 0:width]
        scale_row = mod_ref[0, pl.ds(tau, 1), width:2 * width]
        return (
            away * lax.rsqrt(spread + norm_eps) * (1.0 + scale_row) + shift_row
        ).astype(jnp.bfloat16)

    def pin_copy(slot, ahead):
        other = lax.rem(sharer + ahead, sharers)
        return remote(pbuf.at[slot, other], pin.at[slot, sharer], pin_send.at[slot, ahead],
                      pin_recv.at[slot, sharer], pipe, mine * sharers + other)

    def cin_copy(slot, ahead):
        group = lax.rem(mine + ahead, groups)
        return remote(csum.at[slot, group], cin.at[slot, mine], cin_send.at[slot, ahead],
                      cin_recv.at[slot, mine], pipe, group * sharers + sharer)

    @pl.when(pipe == 0)
    def _():
        for from_pipe in range(n_pipe):
            for group in range(groups):
                lat_arrived(from_pipe, group * sharers + sharer)
                for step in range(1, sharers):
                    lat_pass(from_pipe, group, step).start()
        for from_pipe in range(n_pipe):
            for group in range(groups):
                for step in range(1, sharers):
                    lat_arrived(from_pipe, group * sharers + lax.rem(sharer + step, sharers))
        for slot in range(micro):
            pieces = []
            for from_pipe in range(n_pipe):
                pieces.append(jnp.concatenate([
                    latbuf[from_pipe, index, slot].astype(jnp.float32) for index in range(n_seq)
                ], axis=0))
            whole = jnp.concatenate(pieces, axis=1)
            first_x[...] = whole.astype(jnp.bfloat16)
            mine_rows = pl.ds(pl.multiple_of(sharer * part, 16), part)
            for group in range(groups):
                hid[0, slot, group] = first_x[mine_rows, group * block:(group + 1) * block]
            whole_mod = modulate(whole, ts_ref[0, slot])
            first_mod[slot] = whole_mod
            for index in range(n_seq):
                slabs[index] = whole_mod[:, index * depth:(index + 1) * depth]
            feature_rows = slabs[seq]
            for kv in range(2):
                for group in range(groups):
                    start = kv * inner + group * block
                    partial = jnp.dot(feature_rows, wrows[:, start:start + block],
                                      preferred_element_type=jnp.float32).astype(jnp.bfloat16)
                    for at in range(sharers):
                        pbuf[slot, at, group, kv] = partial[at * part:(at + 1) * part]
            for ahead in range(1, sharers):
                pin_copy(slot, ahead).start()
        for slot in range(micro):
            for ahead in range(1, sharers):
                other = lax.rem(sharer + ahead, sharers)
                pltpu.make_async_copy(pbuf.at[slot, other], pin.at[slot, other],
                                      pin_recv.at[slot, other]).wait()
            total = pbuf[slot, sharer].astype(jnp.float32)
            for ahead in range(1, sharers):
                total += pin[slot, lax.rem(sharer + ahead, sharers)].astype(jnp.float32)
            csum[slot] = total.astype(jnp.bfloat16)
            for ahead in range(1, groups):
                cin_copy(slot, ahead).start()

    pl.when(pipe != 0)(weights_finish)

    @pl.when(pipe == last)
    def _():
        for slot in range(micro):
            pieces = []
            for wide in range(per_block):
                pieces.append(jnp.concatenate([
                    latbuf_wait_load(latbuf, lat_arrived, slot == 0, mine * per_block + wide,
                                     sharer * per_part + index, slot)
                    for index in range(per_part)
                ], axis=0))
            prev[slot] = jnp.concatenate(pieces, axis=1) if per_block > 1 else pieces[0]

    def hid_send_copy(step, slot, group):
        at_last = pipe == last
        to_step = step + jnp.where(at_last, 1, 0)
        return remote(outb.at[step, slot], hid.at[to_step, slot, mine],
                      hid_send.at[step, slot, group], hid_recv.at[to_step, slot, mine],
                      lax.rem(pipe + 1, n_pipe), group * sharers + sharer)

    def hid_arrived(step, slot, group):
        pltpu.make_async_copy(outb.at[step, slot], hid.at[step, slot, group],
                              hid_recv.at[step, slot, group]).wait()

    def kvx_copy(step, slot, ahead):
        other = lax.rem(sharer + ahead, sharers)
        return remote(kvx.at[step, slot, sharer], kvx.at[step, slot, sharer], kvx_send.at[step, slot, ahead],
                      kvx_recv.at[step, slot, sharer], pipe, mine * sharers + other)

    def att_copy(step, slot, ahead):
        group = lax.rem(mine + ahead, groups)
        return remote(att.at[step, slot, mine], att.at[step, slot, mine],
                      att_send.at[step, slot, ahead], att_recv.at[step, slot, mine],
                      pipe, group * sharers + sharer)

    def att_arrived(step, slot, ahead):
        group = lax.rem(mine + ahead, groups)
        pltpu.make_async_copy(att.at[step, slot, mine], att.at[step, slot, group],
                              att_recv.at[step, slot, group]).wait()

    def fin_targets(slot):
        for wide in range(per_block):
            for index in range(per_part):
                to_pipe, to_seq = mine * per_block + wide, sharer * per_part + index
                source = fin_src.at[slot, wide, pl.ds(index * rows, rows), :]
                yield to_pipe, to_seq, source, fin_send.at[slot, wide, index]

    def first_half(step, slot):
        tau = ts_ref[step, slot]
        from_latents = (pipe == 0) & (step == 0)

        @pl.when(from_latents)
        def _():
            modded[...] = first_mod[slot, pl.ds(pl.multiple_of(sharer * part, 16), part), :]
            total = csum[slot, mine].astype(jnp.float32)
            for ahead in range(1, groups):
                group = lax.rem(mine + ahead, groups)
                pltpu.make_async_copy(csum.at[slot, group], cin.at[slot, group],
                                      cin_recv.at[slot, group]).wait()
                total += cin[slot, group].astype(jnp.float32)
            pre[:, :block] = total[0]
            pre[:, block:] = total[1]

        @pl.when(jnp.logical_not(from_latents))
        def _():
            for group in range(groups):
                hid_arrived(step, slot, group)
            modded[...] = modulate(
                jnp.concatenate([hid[step, slot, group].astype(jnp.float32) for group in range(groups)], axis=1),
                tau,
            )
            pre[...] = jnp.dot(modded[...], wkv[...], preferred_element_type=jnp.float32)

        gain_query, gain_key = gain_ref[0, 0:1, :], gain_ref[0, 1:2, :]
        slices = [slice(head * head_dim, (head + 1) * head_dim) for head in range(heads)]
        for here in slices:
            kvx[step, slot, sharer, 0, :, here] = rms_rows(pre[:, here], gain_key)
        kvx[step, slot, sharer, 1] = pre[:, block:].astype(jnp.bfloat16)
        for ahead in range(1, sharers):
            kvx_copy(step, slot, ahead).start()
        projected = jnp.dot(modded[...], wq[...], preferred_element_type=jnp.float32)
        queries = [rms_rows(projected[:, here], gain_query) for here in slices]
        totals, weighted = [0.0] * heads, [0.0] * heads
        for ahead in range(sharers):
            owner = lax.rem(sharer + ahead, sharers)
            if ahead > 0:
                pltpu.make_async_copy(kvx.at[step, slot, sharer], kvx.at[step, slot, owner],
                                      kvx_recv.at[step, slot, owner]).wait()
            for head, here in enumerate(slices):
                logits = lax.dot_general(
                    queries[head], kvx[step, slot, owner, 0, :, here],
                    (((1,), (1,)), ((), ())), preferred_element_type=jnp.float32,
                ) * score_scale
                weights = jnp.exp(logits)
                totals[head] += jnp.sum(weights, axis=-1, keepdims=True)
                weighted[head] += jnp.dot(weights.astype(jnp.bfloat16), kvx[step, slot, owner, 1, :, here],
                                          preferred_element_type=jnp.float32)
        for head, here in enumerate(slices):
            att[step, slot, mine, :, here] = (weighted[head] / totals[head]).astype(jnp.bfloat16)
        for ahead in range(1, groups):
            att_copy(step, slot, ahead).start()

    def second_half(step, slot):
        tau = ts_ref[step, slot]
        gate_row = mod_ref[0, pl.ds(tau, 1), pl.ds(pl.multiple_of(2 * width + mine * block, 128), block)]
        residual = hid[step, slot, mine].astype(jnp.float32)
        projected = 0.0
        for ahead in range(groups):
            group = lax.rem(mine + ahead, groups)
            if ahead > 0:
                att_arrived(step, slot, ahead)
            attended = att[step, slot, group]
            rows_here = pl.ds(pl.multiple_of(group * block, 128), block)
            projected += jnp.dot(attended, wo[rows_here, :], preferred_element_type=jnp.float32)
        layer_out = (residual + gate_row * projected).astype(jnp.bfloat16)
        ends = (pipe == last) & (step == steps - 1)

        @pl.when(pipe != last)
        def _():
            outb[step, slot] = layer_out

        @pl.when(pipe == last)
        def _():
            update = (prev[slot] - ss_ref[tau] * layer_out.astype(jnp.float32)).astype(jnp.bfloat16)
            outb[step, slot] = update
            prev[slot] = update.astype(jnp.float32)

        @pl.when(jnp.logical_not(ends))
        def _():
            for ahead in range(groups):
                hid_send_copy(step, slot, lax.rem(mine + ahead, groups)).start()

        @pl.when(ends)
        def _():
            update = prev[slot]
            for wide in range(per_block):
                fin_src[slot, wide] = update[:, wide * share:(wide + 1) * share]
            for to_pipe, to_seq, source, send in fin_targets(slot):
                own = (to_pipe == pipe) & (to_seq == seq)

                @pl.when(own)
                def _():
                    pltpu.make_async_copy(source, fin.at[slot], fin_recv.at[slot]).start()

                @pl.when(jnp.logical_not(own))
                def _():
                    remote(source, fin.at[slot], send, fin_recv.at[slot], to_pipe, to_seq).start()

    def visit(step, carry):
        @pl.when((pipe == 0) & (step == 1))
        def _():
            weights_start()
            weights_finish()

        for slot in range(micro):
            first_half(step, slot)
            second_half(step, slot)
        return carry

    lax.fori_loop(0, steps, visit, 0)

    for slot in range(micro):
        pltpu.make_async_copy(fin_src.at[slot, 0, pl.ds(0, rows), :], fin.at[slot],
                              fin_recv.at[slot]).wait()
        out_ref[slot] = fin[slot].astype(jnp.bfloat16)

    for ahead in range(groups):
        target = lax.rem(mine + ahead, groups) * sharers + sharer
        if ahead == 0:
            @pl.when(pipe != 0)
            def _():
                lat_copy(0, target, ahead).wait_send()
        else:
            lat_copy(0, target, ahead).wait_send()

    @pl.when(jnp.logical_not(keeps_own))
    def _():
        lat_copy(last, keeper, n_seq).wait_send()

    @pl.when(pipe == 0)
    def _():
        for slot in range(micro):
            for ahead in range(1, sharers):
                pin_copy(slot, ahead).wait_send()
        for from_pipe in range(n_pipe):
            for group in range(groups):
                for step in range(1, sharers):
                    lat_pass(from_pipe, group, step).wait_send()
        for slot in range(micro):
            for ahead in range(1, groups):
                cin_copy(slot, ahead).wait_send()

    for kv in range(2):
        for ahead in range(1, groups):
            kv_copy(kv, ahead).wait_send()
        for ahead in range(groups):
            for step in range(1, sharers):
                kv_pass(kv, ahead, step).wait_send()

    def drain(item, carry):
        step, slot = item // micro, item % micro
        ends = (pipe == last) & (step == steps - 1)
        for ahead in range(1, groups):
            att_copy(step, slot, ahead).wait_send()
        for ahead in range(1, sharers):
            kvx_copy(step, slot, ahead).wait_send()

        @pl.when(jnp.logical_not(ends))
        def _():
            for group in range(groups):
                hid_send_copy(step, slot, group).wait_send()

        @pl.when(ends)
        def _():
            for to_pipe, to_seq, source, send in fin_targets(slot):
                @pl.when(jnp.logical_not((to_pipe == pipe) & (to_seq == seq)))
                def _():
                    remote(source, fin.at[slot], send, fin_recv.at[slot], to_pipe, to_seq).wait_send()
        return carry

    lax.fori_loop(0, micro * steps, drain, 0)


def latbuf_wait_load(latbuf, lat_arrived, first, from_pipe, from_seq, slot):
    if first:
        lat_arrived(from_pipe, from_seq)
    return latbuf[from_pipe, from_seq, slot].astype(jnp.float32)


def shards(latents, timesteps, step_sizes, mod_table, qk_gain, w_query, w_kv, w_out):
    n_pipe, n_seq = lax.axis_size("pipe"), lax.axis_size("seq")
    micro, rows, share = latents.shape
    steps = timesteps.shape[0]
    head_dim = qk_gain.shape[2]
    width, inner = w_query.shape[1], w_query.shape[2]
    heads = inner // head_dim
    groups = math.gcd(math.gcd(heads, n_seq), n_pipe)
    while n_seq // groups < 2:
        groups //= 2
    sharers = n_seq // groups
    block = inner // groups
    part = rows * n_seq // sharers
    per_block, per_part = n_pipe // groups, n_seq // sharers
    bf16, f32 = jnp.bfloat16, jnp.float32
    vmem = pl.BlockSpec(memory_space=pltpu.VMEM)
    hbm = pl.BlockSpec(memory_space=pl.ANY)
    dma = pltpu.SemaphoreType.DMA
    return pl.pallas_call(
        functools.partial(kernel, n_pipe, n_seq, groups, micro, steps, head_dim),
        out_shape=jax.ShapeDtypeStruct(latents.shape, bf16),
        in_specs=[hbm] * 8,
        out_specs=vmem,
        scratch_shapes=[
            pltpu.SMEM(timesteps.shape, timesteps.dtype),
            pltpu.SMEM(step_sizes.shape, f32),
            pltpu.VMEM(mod_table.shape, f32),
            pltpu.VMEM(qk_gain.shape, f32),
            pltpu.VMEM((width, block), bf16),
            pltpu.VMEM((width, 2 * block), bf16),
            pltpu.VMEM((inner, block), bf16),
            pltpu.VMEM(w_kv.shape[1:], bf16),
            pltpu.VMEM((n_pipe, n_seq, micro, rows, share), bf16),
            pltpu.VMEM((steps, micro, groups, part, block), bf16),
            pltpu.VMEM((steps, micro, groups, part, block), bf16),
            pltpu.VMEM((steps, micro, part, block), bf16),
            pltpu.VMEM((micro, part, block), f32),
            pltpu.VMEM((part, width), bf16),
            pltpu.VMEM((rows * n_seq, width), bf16),
            pltpu.VMEM((micro, rows * n_seq, width), bf16),
            pltpu.VMEM((n_seq, rows * n_seq, w_kv.shape[1]), bf16),
            pltpu.VMEM((micro, sharers, groups, 2, part, block), bf16),
            pltpu.VMEM((micro, sharers, groups, 2, part, block), bf16),
            pltpu.VMEM((micro, groups, 2, part, block), bf16),
            pltpu.VMEM((micro, groups, 2, part, block), bf16),
            pltpu.VMEM((part, 2 * block), f32),
            pltpu.VMEM((steps, micro, sharers, 2, part, block), bf16),
            pltpu.VMEM((micro, per_block, part, share), f32),
            pltpu.VMEM((micro, rows, share), f32),
            dma((7,)),
            dma((2, n_seq)),
            dma((2, groups)),
            dma((2, groups, sharers)),
            dma((n_seq + 1,)),
            dma((n_pipe, n_seq)),
            dma((n_pipe, groups, sharers)),
            dma((micro, sharers)),
            dma((micro, sharers)),
            dma((micro, groups)),
            dma((micro, groups)),
            dma((steps, micro, groups)),
            dma((steps, micro, groups)),
            dma((steps, micro, sharers)),
            dma((steps, micro, sharers)),
            dma((steps, micro, groups)),
            dma((steps, micro, groups)),
            dma((micro, per_block, per_part)),
            dma((micro,)),
        ],
        compiler_params=pltpu.CompilerParams(
            has_side_effects=True, vmem_limit_bytes=64 * 1024 * 1024
        ),
        cost_estimate=pl.CostEstimate(
            flops=2 * 4 * rows * n_seq * width * block * micro * steps,
            bytes_accessed=2 * 4 * width * block, transcendentals=0,
        ),
        name="denoise",
    )(latents, timesteps, step_sizes, mod_table, qk_gain, w_query, w_kv, w_out)


def solution(mesh):
    in_specs = (
        P(None, "seq", "pipe"),
        P(),
        P(),
        P("pipe", None, None),
        P("pipe", None, None),
        P("pipe", None, None),
        P("pipe", "seq", None),
        P("pipe", None, None),
    )
    out_specs = P(None, "seq", "pipe")
    return jax.shard_map(shards, mesh=mesh, in_specs=in_specs, out_specs=out_specs, check_vma=False)
```
